32 devices in a mesh: plots: 16 (over z, y, core), seq: 2 (over x).
Axes of the slice: x: 2, y: 2, z: 4, core: 2. Of those that a mesh axis runs over, the one named last changes fastest.
Arguments:
- decoder_states: bfloat16 [16, 1024, 768], P('plots', 'seq'), may hold values from -6 to 6
- encoder_patches: bfloat16 [16, 2048, 768], P('plots', 'seq'), may hold values from -6 to 6
- token_lengths: int32 [16], P('plots'), may hold values from 1 to 1024, as said below
- patch_counts: int32 [16], P('plots'), may hold values from 64 to 2048, as said below
- self_gain: bfloat16 [768], replicated, may hold values from 0.25 to 1.75
- cross_gain: bfloat16 [768], replicated, may hold values from 0.25 to 1.75
- mlp_gain: bfloat16 [768], replicated, may hold values from 0.25 to 1.75
- self_query: bfloat16 [768, 768], replicated, may hold values from -0.21875 to 0.21875
- self_key: bfloat16 [768, 768], replicated, may hold values from -0.21875 to 0.21875
- self_value: bfloat16 [768, 768], replicated, may hold values from -0.21875 to 0.21875
- self_output: bfloat16 [768, 768], replicated, may hold values from -1.75 to 1.75
- cross_query: bfloat16 [768, 768], replicated, may hold values from -0.21875 to 0.21875
- cross_key: bfloat16 [768, 768], replicated, may hold values from -0.21875 to 0.21875
- cross_value: bfloat16 [768, 768], replicated, may hold values from -0.21875 to 0.21875
- cross_output: bfloat16 [768, 768], replicated, may hold values from -1.75 to 1.75
- mlp_gate: bfloat16 [768, 2048], replicated, may hold values from -0.21875 to 0.21875
- mlp_up: bfloat16 [768, 2048], replicated, may hold values from -0.21875 to 0.21875
- mlp_down: bfloat16 [2048, 768], replicated, may hold values from -0.125 to 0.125
- output_grad: bfloat16 [16, 1024, 768], P('plots', 'seq'), may hold values from -6 to 6
Outputs:
- layer_output: bfloat16 [16, 1024, 768], P('plots', 'seq')
- input_grad: bfloat16 [16, 1024, 768], P('plots', 'seq')
- patch_grad: bfloat16 [16, 2048, 768], P('plots', 'seq')
- self_gain_grad: float32 [768], P('plots')
- cross_gain_grad: float32 [768], P('plots')
- mlp_gain_grad: float32 [768], P('plots')
- self_query_grad: float32 [768, 768], P('plots')
- self_key_grad: float32 [768, 768], P('plots')
- self_value_grad: float32 [768, 768], P('plots')
- self_output_grad: float32 [768, 768], P('plots')
- cross_query_grad: float32 [768, 768], P('plots')
- cross_key_grad: float32 [768, 768], P('plots')
- cross_value_grad: float32 [768, 768], P('plots')
- cross_output_grad: float32 [768, 768], P('plots')
- mlp_gate_grad: float32 [768, 2048], P('plots')
- mlp_up_grad: float32 [768, 2048], P('plots')
- mlp_down_grad: float32 [2048, 768], P('plots')
The draws below stay inside these ranges and needn't reach their ends.
Inputs may be any that keep to these rules, and one draw needn't show every extreme that they name: `token_lengths`: keys at or past a plot's length are padding; some plot has exactly 1024. `patch_counts`: patch slots at or past a plot's count are padding; some plot has exactly 2048.
All inputs are finite; a program needn't handle non-finite values.
Results may differ from the reference program's by a relative error of at most 0.024.
Values may be sent and summed in bfloat16 or wider, within the bound.
No kernel may reach another device: no remote copies, remote signals or barrier semaphores. Data moves between devices by JAX's collectives and lax.ppermute only.
A program may use at most 256 MiB of HBM per device.

```python
import jax
import jax.numpy as jnp
from jax import lax

D = 768
HEADS = 12
HEAD_DIM = 64
FF = 2048
PLOTS = 16
SEQ_LEN = 1024
PATCHES = 2048


def pick_full(key, count, lowest, highest_value):
    first_key, second_key = jax.random.split(key)
    values = jax.random.randint(first_key, (count,), lowest, highest_value + 1)
    chosen = jax.random.randint(second_key, (), 0, count)
    return jnp.where(jnp.arange(count) == chosen, highest_value, values).astype(jnp.int32)


def draw_token_lengths(key, part):
    key = jax.random.fold_in(key, 11)
    return pick_full(key, PLOTS, 1, SEQ_LEN)


def draw_patch_counts(key, part):
    key = jax.random.fold_in(key, 23)
    return pick_full(key, PLOTS, max(1, PATCHES // 32), PATCHES)


def levels(stream_key, dims, cuts, smallest, top_value):
    def one(dim, shards_of):
        steps = jax.random.uniform(jax.random.fold_in(jax.random.fold_in(stream_key, 6), dim), (shards_of,), jnp.float32, smallest / len(cuts), top_value / len(cuts))
        return jnp.repeat(jnp.exp(steps), dims[dim] // shards_of).reshape((-1,) + (1,) * (len(dims) - dim - 1))

    loudness = one(*cuts[0])
    for cut in cuts[1:]:
        loudness = loudness * one(*cut)
    return loudness


def bell_draw(own_key, shape, deviation, most, pieces=(), kind=jnp.bfloat16):
    result = deviation * jax.random.normal(own_key, shape, jnp.float32)
    if pieces:
        result = result * levels(own_key, shape, pieces, -0.22, 0.18)
    return jnp.clip(result, -most, most).astype(kind)


def setup_inputs(seed: int = 0) -> dict:
    arg_keys = jax.random.split(jax.random.key(seed), 20)
    return {
        "decoder_states": bell_draw(arg_keys[0], (PLOTS, SEQ_LEN, D), 1.0, 6.0, ((0, 16), (1, 2))),
        "encoder_patches": bell_draw(arg_keys[1], (PLOTS, PATCHES, D), 1.0, 6.0, ((0, 16), (1, 2))),
        "token_lengths": draw_token_lengths(jax.random.fold_in(arg_keys[19], 71), 0),
        "patch_counts": draw_patch_counts(jax.random.fold_in(arg_keys[19], 71), 0),
        "self_gain": jnp.clip(1.0 + 0.15 * jax.random.normal(arg_keys[4], (D,), jnp.float32), 0.25, 1.75).astype(jnp.bfloat16),
        "cross_gain": jnp.clip(1.0 + 0.15 * jax.random.normal(arg_keys[5], (D,), jnp.float32), 0.25, 1.75).astype(jnp.bfloat16),
        "mlp_gain": jnp.clip(1.0 + 0.15 * jax.random.normal(arg_keys[6], (D,), jnp.float32), 0.25, 1.75).astype(jnp.bfloat16),
        "self_query": bell_draw(arg_keys[7], (D, D), D ** -0.5, 0.21875),
        "self_key": bell_draw(arg_keys[8], (D, D), D ** -0.5, 0.21875),
        "self_value": bell_draw(arg_keys[9], (D, D), D ** -0.5, 0.21875),
        "self_output": bell_draw(arg_keys[10], (D, D), (max(D // 64, 1)) ** -0.5, 1.75),
        "cross_query": bell_draw(arg_keys[11], (D, D), D ** -0.5, 0.21875),
        "cross_key": bell_draw(arg_keys[12], (D, D), D ** -0.5, 0.21875),
        "cross_value": bell_draw(arg_keys[13], (D, D), D ** -0.5, 0.21875),
        "cross_output": bell_draw(arg_keys[14], (D, D), (max(D // 64, 1)) ** -0.5, 1.75),
        "mlp_gate": bell_draw(arg_keys[15], (D, FF), D ** -0.5, 0.21875),
        "mlp_up": bell_draw(arg_keys[16], (D, FF), D ** -0.5, 0.21875),
        "mlp_down": bell_draw(arg_keys[17], (FF, D), FF ** -0.5, 0.125),
        "output_grad": bell_draw(arg_keys[18], (PLOTS, SEQ_LEN, D), 1.0, 6.0, ((0, 16), (1, 2))),
    }


eps = 1e-06
highest = lax.Precision.HIGHEST

@jax.custom_vjp
def low(v):
    return lax.optimization_barrier(v.astype(jnp.bfloat16)).astype(jnp.float32)

@jax.custom_vjp
def low_back(v):
    return v

def low_keep(v):
    return (low(v), None)

def low_pass(kept, grad):
    return (grad,)

def back_keep(v):
    return (v, None)

def back_low(kept, grad):
    return (low(grad),)
low.defvjp(low_keep, low_pass)
low_back.defvjp(back_keep, back_low)

def norm(value, gain):
    return value * lax.rsqrt(lax.optimization_barrier(jnp.mean(value * value, axis=-1, keepdims=True)) + eps) * gain

def matmul(left, right):
    return jnp.dot(left, right, precision=highest)

def gelu(value):
    return 0.5 * value * (1.0 + jnp.tanh(0.7978845608028654 * (value + 0.044715 * value * value * value)))

def attend(query, keys, values, mask):
    rows = query.shape[0]
    cols = keys.shape[0]
    q_heads = query.reshape(rows, HEADS, HEAD_DIM)
    k_heads = keys.reshape(cols, HEADS, HEAD_DIM)
    v_heads = values.reshape(cols, HEADS, HEAD_DIM)
    scores = jnp.einsum('ihd,jhd->hij', q_heads, k_heads, precision=highest) * HEAD_DIM ** (-0.5)
    scores = low_back(scores)
    scores = jnp.where(mask[None], scores, -1e+30)
    top = lax.optimization_barrier(jnp.max(scores, axis=-1, keepdims=True))
    expo = jnp.exp(scores - top)
    probs = low(expo / lax.optimization_barrier(jnp.sum(expo, axis=-1, keepdims=True)))
    mixed = jnp.einsum('hij,jhd->ihd', probs, v_heads, precision=highest).reshape(rows, HEADS * HEAD_DIM)
    return low(low_back(mixed))

def plot_layer(weights, states, patches, length, count):
    self_gain, cross_gain, mlp_gain, self_query, self_key, self_value, self_output, cross_query, cross_key, cross_value, cross_output, mlp_gate, mlp_up, mlp_down = weights
    position = jnp.arange(SEQ_LEN, dtype=jnp.int32)
    self_mask = (position[None, :] <= position[:, None]) & (position[None, :] < length)
    cross_mask = (jnp.arange(PATCHES, dtype=jnp.int32) < count)[None, :]
    first = low(norm(states, self_gain))
    query = low(low_back(matmul(first, self_query)))
    keys = low(low_back(matmul(first, self_key)))
    values = low(low_back(matmul(first, self_value)))
    after_self = states + low_back(matmul(attend(query, keys, values, self_mask), self_output))
    second = low(norm(after_self, cross_gain))
    query = low(low_back(matmul(second, cross_query)))
    keys = low(matmul(patches, cross_key))
    values = low(matmul(patches, cross_value))
    after_cross = after_self + low_back(matmul(attend(query, keys, values, cross_mask), cross_output))
    third = low(norm(after_cross, mlp_gain))
    gate = low_back(matmul(third, mlp_gate))
    upward = low_back(matmul(third, mlp_up))
    hidden = low(gelu(gate) * upward)
    return after_cross + matmul(hidden, mlp_down)

def reference(decoder_states, encoder_patches, token_lengths, patch_counts, self_gain, cross_gain, mlp_gain, self_query, self_key, self_value, self_output, cross_query, cross_key, cross_value, cross_output, mlp_gate, mlp_up, mlp_down, output_grad):
    weights = tuple((w.astype(jnp.float32) for w in (self_gain, cross_gain, mlp_gain, self_query, self_key, self_value, self_output, cross_query, cross_key, cross_value, cross_output, mlp_gate, mlp_up, mlp_down)))

    def forward(params, states, patches):

        def single(item):
            return plot_layer(params, item[0], item[1], item[2], item[3])
        return lax.map(jax.checkpoint(single), (states, patches, token_lengths, patch_counts))
    outputs, backward = jax.vjp(forward, weights, decoder_states.astype(jnp.float32), encoder_patches.astype(jnp.float32))
    grads, states_grad, patches_grad = backward(output_grad.astype(jnp.float32))
    return (outputs.astype(jnp.bfloat16), states_grad.astype(jnp.bfloat16), patches_grad.astype(jnp.bfloat16), grads[0], grads[1], grads[2], grads[3], grads[4], grads[5], grads[6], grads[7], grads[8], grads[9], grads[10], grads[11], grads[12], grads[13])
```

```python
import functools
import math

import jax
import jax.numpy as jnp
from jax import lax
from jax.experimental import pallas as pl
from jax.experimental.pallas import tpu as pltpu
from jax.sharding import PartitionSpec as P

HEADS = 12
eps = 1e-06
bf = jnp.bfloat16
f32 = jnp.float32
LOG2E = 1.4426950408889634
LN2 = 0.6931471805599453
MASKED = -1e30
NT = (((1,), (1,)), ((), ()))
TN = (((0,), (0,)), ((), ()))
NN = (((1,), (0,)), ((), ()))
VMEM = 56 << 20


def dot(left, right, dims=NN):
    return lax.dot_general(left, right, dims, preferred_element_type=f32)


def lane_of(shape):
    return lax.broadcasted_iota(jnp.int32, shape, len(shape) - 1)


def head_lanes(lane, half):
    return (lane < 64) if half == 0 else (lane >= 64)


def attend_kernel(causal, merge, q_ref, k_ref, v_ref, bias_ref, *refs):
    if merge:
        before_ref, e_ref, o_ref, own_ref, new_ref = refs
    else:
        e_ref, o_ref = refs
    rows, keys = q_ref.shape[0], k_ref.shape[0]
    block = min(256, rows)
    q, k, v, bias = q_ref[...], k_ref[...], v_ref[...], bias_ref[...]
    lane_q, lane_k, lane_b = lane_of(q.shape), lane_of(k.shape), lane_of((block, 128))
    merged = []
    for half in range(2):
        spare = 64 - 64 * half
        qa = jnp.where(head_lanes(lane_q, half), q, jnp.where(lane_q == spare, 1.0, 0.0).astype(bf))
        ka = jnp.where(head_lanes(lane_k, half), k, bias)
        va = jnp.where(head_lanes(lane_k, half), v, jnp.where(lane_k == spare, 1.0, 0.0).astype(bf))
        for b in range(rows // block):
            at = slice(b * block, (b + 1) * block)
            reach = min(keys, (b + 1) * block) if causal else keys
            step = min(512, reach)
            pieces, top = [], None
            for c in range(0, reach, step):
                wide = min(step, reach - c)
                s = dot(qa[at], ka[c : c + wide], NT)
                if causal:
                    row = lax.broadcasted_iota(jnp.int32, s.shape, 0) + b * block
                    s = jnp.where(lane_of(s.shape) + c <= row, s, MASKED)
                most = jnp.max(s, axis=1, keepdims=True)
                top = most if top is None else jnp.maximum(top, most)
                pieces.append((c, wide, s))
            o = None
            for c, wide, s in pieces:
                e = jnp.exp2(s - top).astype(bf)
                e_ref[half, at, c : c + wide] = e
                part = dot(e, va[c : c + wide])
                o = part if o is None else o + part
            if not merge:
                o_ref[half, at, :] = jnp.where(lane_b == spare + 1, top, o)
                continue
            old = before_ref[half, at, :]
            l_old, m_old = old[:, spare : spare + 1], old[:, spare + 1 : spare + 2]
            l_new = o[:, spare : spare + 1]
            m = jnp.maximum(m_old, top)
            w_old, w_new = jnp.exp2(m_old - m), jnp.exp2(top - m)
            total = l_old * w_old + l_new * w_new
            f_old, f_new = w_old / total, w_new / total
            o = old * f_old + o * f_new
            if half == 0:
                merged.append((o, f_old, f_new))
            else:
                first = head_lanes(lane_b, 0)
                o0, old0, new0 = merged[b]
                o_ref[at, :] = jnp.where(first, o0, o).astype(bf)
                own_ref[at, :] = jnp.where(first, old0, f_old)
                new_ref[at, :] = jnp.where(first, new0, f_new)


def attend(q, k, v, bias, causal=False, before=None):
    rows, width = q.shape
    keys = k.shape[0]
    pairs = width // 128
    merge = before is not None
    wide = pl.BlockSpec((keys, 128), lambda p: (0, p))
    tall = pl.BlockSpec((rows, 128), lambda p: (0, p))
    e_spec = pl.BlockSpec((2, rows, keys), lambda p: (p, 0, 0))
    o_spec = pl.BlockSpec((2, rows, 128), lambda p: (p, 0, 0))
    e_shape = jax.ShapeDtypeStruct((2 * pairs, rows, keys), bf)
    flat = jax.ShapeDtypeStruct((rows, width), f32)
    in_specs = [tall, wide, wide, pl.BlockSpec((keys, 128), lambda p: (0, 0))]
    args = [q, k, v, bias]
    if merge:
        in_specs.append(o_spec)
        args.append(before)
        out_specs = [e_spec, tall, tall, tall]
        out_shape = [e_shape, jax.ShapeDtypeStruct((rows, width), bf), flat, flat]
    else:
        out_specs = [e_spec, o_spec]
        out_shape = [e_shape, jax.ShapeDtypeStruct((2 * pairs, rows, 128), f32)]
    return pl.pallas_call(
        functools.partial(attend_kernel, causal, merge),
        grid=(pairs,),
        in_specs=in_specs,
        out_specs=out_specs,
        out_shape=out_shape,
        compiler_params=pltpu.CompilerParams(vmem_limit_bytes=VMEM),
        cost_estimate=pl.CostEstimate(
            flops=16 * rows * keys * width, bytes_accessed=30 * rows * keys, transcendentals=12 * rows * keys
        ),
        name="attend",
    )(*args)


def attend_back_kernel(causal, last, e_ref, do_ref, o_ref, f_ref, q_ref, k_ref, v_ref, *refs):
    if last:
        before_ref, dq_ref, dk_ref, dv_ref = refs
    else:
        dq_ref, dk_ref, dv_ref = refs
    rows, keys = q_ref.shape[0], k_ref.shape[0]
    block = min(256, rows)
    q, k, v = q_ref[...], k_ref[...], v_ref[...]
    lane_k, lane_b = lane_of(k.shape), lane_of((block, 128))
    dq = [None] * (rows // block)
    dks, dvs = [], []
    for half in range(2):
        spare = 64 - 64 * half
        ink = head_lanes(lane_k, half)
        inb = head_lanes(lane_b, half)
        va = jnp.where(ink, v, jnp.where((lane_k == spare) | (lane_k == spare + 1), 1.0, 0.0).astype(bf))
        ka = jnp.where(ink, k, jnp.zeros_like(k))
        dk, dv = {}, {}
        for b in range(rows // block):
            at = slice(b * block, (b + 1) * block)
            reach = min(keys, (b + 1) * block) if causal else keys
            do = do_ref[at, :].astype(f32)
            f = f_ref[at, :]
            inner = jnp.sum(jnp.where(inb, do * o_ref[at, :].astype(f32), 0.0), axis=1, keepdims=True)
            off = -inner * f[:, 64 * half : 64 * half + 1]
            high = off.astype(bf).astype(f32)
            dos = jnp.where(
                inb, do * f, jnp.where(lane_b == spare, high, jnp.where(lane_b == spare + 1, off - high, 0.0))
            ).astype(bf)
            e = e_ref[half, at, :reach]
            dp = dot(dos, va[:reach], NT)
            ds = (e.astype(f32) * dp).astype(bf)
            part = dot(ds, ka[:reach])
            dq[b] = part if dq[b] is None else dq[b] + part
            step = min(reach, block if causal else keys)
            for c in range(0, reach, step):
                vt = dot(dos, e[:, c : c + step], TN)
                kt = dot(q[at], ds[:, c : c + step], TN)
                dv[c] = vt if c not in dv else dv[c] + vt
                dk[c] = kt if c not in dk else dk[c] + kt
        dks.append(dk)
        dvs.append(dv)
    for b in range(rows // block):
        at = slice(b * block, (b + 1) * block)
        if last:
            dq_ref[at, :] = ((dq[b] + before_ref[at, :]) * 0.125).astype(dq_ref.dtype)
        else:
            dq_ref[at, :] = dq[b]
    for c in dks[0]:
        wide = dks[0][c].shape[1]
        for half in range(2):
            at = slice(64 * half, 64 * half + 64)
            dk_ref[at, c : c + wide] = (dks[half][c][at] * LN2).astype(bf)
            dv_ref[at, c : c + wide] = dvs[half][c][at].astype(bf)


def attend_back(e, do, o, f, q, k, v, causal=False, before=None):
    rows, width = q.shape
    keys = k.shape[0]
    pairs = width // 128
    last = before is not None
    wide = pl.BlockSpec((keys, 128), lambda p: (0, p))
    tall = pl.BlockSpec((rows, 128), lambda p: (0, p))
    turned = pl.BlockSpec((128, keys), lambda p: (p, 0))
    in_specs = [pl.BlockSpec((2, rows, keys), lambda p: (p, 0, 0)), tall, tall, tall, tall, wide, wide]
    args = [e, do, o, f, q, k, v]
    if last:
        in_specs.append(tall)
        args.append(before)
    turned_shape = jax.ShapeDtypeStruct((width, keys), bf)
    return pl.pallas_call(
        functools.partial(attend_back_kernel, causal, last),
        grid=(pairs,),
        in_specs=in_specs,
        out_specs=[tall, turned, turned],
        out_shape=[jax.ShapeDtypeStruct((rows, width), bf if last else f32), turned_shape, turned_shape],
        compiler_params=pltpu.CompilerParams(vmem_limit_bytes=VMEM),
        cost_estimate=pl.CostEstimate(
            flops=16 * rows * keys * width, bytes_accessed=30 * rows * keys, transcendentals=0
        ),
        name="attend_back",
    )(*args)


def norm(value, gain):
    return value * lax.rsqrt(jnp.mean(value * value, axis=-1, keepdims=True) + eps) * gain


def norm_back(value, gain, grad):
    scale = lax.rsqrt(jnp.mean(value * value, axis=-1, keepdims=True) + eps)
    unit = value * scale
    inner = gain * grad
    back = scale * (inner - unit * jnp.mean(inner * unit, axis=-1, keepdims=True))
    return back, jnp.sum(grad * unit, axis=0)


def gelu_parts(u):
    inner = 0.7978845608028654 * (u + 0.044715 * u * u * u)
    t = jnp.tanh(inner)
    value = 0.5 * u * (1.0 + t)
    slope = 0.5 * (1.0 + t) + 0.5 * u * (1.0 - t * t) * (0.7978845608028654 * (1.0 + 3 * 0.044715 * u * u))
    return value, slope


def length_bias(valid):
    lane = jnp.arange(128, dtype=jnp.int32)[None, :]
    return jnp.where(jnp.logical_not(valid)[:, None] & ((lane == 0) | (lane == 64)), MASKED, 0.0).astype(bf)


def ring_factors(groups):
    inner = 1
    while inner * inner * 4 <= groups:
        inner *= 2
    return inner, groups // inner


def ring_reduce(value, size, stride, place, index):
    total = lax.axis_size("plots")

    def forward(i):
        spot = (i // stride) % size
        return i + ((spot + 1) % size - spot) * stride

    perm = [(i, forward(i)) for i in range(total)]
    running = None
    for step in range(size):
        mine = lax.dynamic_index_in_dim(value, (place - 1 - step) % size, 0, keepdims=False)
        if running is None:
            running = mine
        else:
            running = (running.astype(f32) + mine.astype(f32)).astype(bf)
        if step < size - 1:
            running = lax.ppermute(running, "plots", perm)
    return running


def reduce_pair(one, two):
    total = lax.axis_size("plots")
    index = lax.axis_index("plots")
    core = index % 2
    groups = total // 2
    inner, outer = ring_factors(groups)
    swap = [(i, i ^ 1) for i in range(total)]
    send = jnp.where(core == 0, two, one).astype(bf)
    keep = jnp.where(core == 0, one, two)
    keep = (keep.astype(f32) + lax.ppermute(send, "plots", swap).astype(f32)).astype(bf)
    rows = keep.shape[0] // groups
    keep = keep.reshape((outer, inner, rows) + keep.shape[1:])
    group = index // 2
    keep = ring_reduce(keep.swapaxes(0, 1), inner, 2, group % inner, index)
    keep = ring_reduce(keep, outer, 2 * inner, group // inner, index)
    keep = keep.astype(f32) + lax.ppermute(keep, "seq", [(0, 1), (1, 0)]).astype(f32)
    keep = keep.reshape((2, rows // 2) + keep.shape[1:])
    mine = lax.dynamic_index_in_dim(keep, core, 0, keepdims=False)
    other = lax.ppermute(lax.dynamic_index_in_dim(keep, 1 - core, 0, keepdims=False).astype(bf), "plots", swap)
    other = other.astype(f32)
    return jnp.where(core == 0, mine, other), jnp.where(core == 0, other, mine)


def per_device(
    decoder_states,
    encoder_patches,
    token_lengths,
    patch_counts,
    self_gain,
    cross_gain,
    mlp_gain,
    self_query,
    self_key,
    self_value,
    self_output,
    cross_query,
    cross_key,
    cross_value,
    cross_output,
    mlp_gate,
    mlp_up,
    mlp_down,
    output_grad,
):
    plots, rows, width = decoder_states.shape
    assert plots == 1 and width == 64 * HEADS
    patch_rows = encoder_patches.shape[1]
    place = lax.axis_index("seq")
    swap = [(0, 1), (1, 0)]
    token = jnp.arange(rows, dtype=jnp.int32)
    slot = jnp.arange(patch_rows, dtype=jnp.int32)
    self_own = length_bias(token + place * rows < token_lengths[0])
    self_far = length_bias((token < token_lengths[0]) & (place == 1))
    cross_own = length_bias(slot + place * patch_rows < patch_counts[0])
    cross_far = length_bias(slot + (1 - place) * patch_rows < patch_counts[0])
    gain_one = self_gain.astype(f32)
    gain_two = cross_gain.astype(f32)
    gain_three = mlp_gain.astype(f32)
    scale = 0.125 * LOG2E

    own_in = decoder_states[0]
    patches = encoder_patches[0]
    far_in = lax.ppermute(own_in, "seq", [(0, 1)])
    far_patches = lax.ppermute(patches, "seq", swap)

    states = own_in.astype(f32)
    first = norm(states, gain_one).astype(bf)
    q1 = (dot(first, self_query) * scale).astype(bf)
    k1 = dot(first, self_key).astype(bf)
    v1 = dot(first, self_value).astype(bf)
    k2 = dot(patches, cross_key).astype(bf)
    v2 = dot(patches, cross_value).astype(bf)
    e1, part1 = attend(q1, k1, v1, self_own, causal=True)
    far_first = norm(far_in.astype(f32), gain_one).astype(bf)
    far_k1 = dot(far_first, self_key).astype(bf)
    far_v1 = dot(far_first, self_value).astype(bf)
    far_e1, o1, f1, far_f1 = attend(q1, far_k1, far_v1, self_far, before=part1)
    y1 = states + dot(o1, self_output)
    second = norm(y1, gain_two).astype(bf)
    q2 = (dot(second, cross_query) * scale).astype(bf)
    e2, part2 = attend(q2, k2, v2, cross_own)
    far_k2 = dot(far_patches, cross_key).astype(bf)
    far_v2 = dot(far_patches, cross_value).astype(bf)
    far_e2, o2, f2, far_f2 = attend(q2, far_k2, far_v2, cross_far, before=part2)
    y2 = y1 + dot(o2, cross_output)
    third = norm(y2, gain_three).astype(bf)
    gate = dot(third, mlp_gate)
    up = dot(third, mlp_up)
    act, slope = gelu_parts(gate)
    hidden = (act * up).astype(bf)
    layer_output = (y2 + dot(hidden, mlp_down)).astype(bf)

    dy = output_grad[0]
    down_grad = dot(hidden, dy, TN).astype(bf)
    half = width // 2
    down_sums = reduce_pair(down_grad[:, :half], down_grad[:, half:])
    dhidden = dot(dy, mlp_down, NT)
    dgate = (dhidden * up * slope).astype(bf)
    dup = (dhidden * act).astype(bf)
    gate_sum, up_sum = reduce_pair(dot(third, dgate, TN).astype(bf), dot(third, dup, TN).astype(bf))
    dthird = dot(dgate, mlp_gate, NT) + dot(dup, mlp_up, NT)
    back, gain_three_grad = norm_back(y2, gain_three, dthird)
    dy2 = dy.astype(f32) + back
    b2 = dy2.astype(bf)
    cross_output_part = dot(o2, b2, TN).astype(bf)
    do2 = dot(b2, cross_output, NT).astype(bf)
    far_dq2, far_dk2, far_dv2 = attend_back(far_e2, do2, o2, far_f2, q2, far_k2, far_v2)
    far_patch_grad = (dot(far_dk2, cross_key, (((0,), (1,)), ((), ()))) + dot(far_dv2, cross_value, (((0,), (1,)), ((), ())))).astype(bf)
    near_patch_grad = lax.ppermute(far_patch_grad, "seq", swap)
    dq2, dk2, dv2 = attend_back(e2, do2, o2, f2, q2, k2, v2, before=far_dq2)
    patch_grad = dot(dk2, cross_key, (((0,), (1,)), ((), ()))) + dot(dv2, cross_value, (((0,), (1,)), ((), ())))
    patch_grad = (patch_grad + near_patch_grad.astype(f32)).astype(bf)
    turned = (((0,), (1,)), ((), ()))
    cross_key_part = (dot(patches, dk2, turned) + dot(far_patches, far_dk2, turned)).astype(bf)
    cross_value_part = (dot(patches, dv2, turned) + dot(far_patches, far_dv2, turned)).astype(bf)
    cross_query_part = dot(second, dq2, TN).astype(bf)
    key_value_sums = reduce_pair(
        jnp.concatenate([cross_key_part, cross_query_part], 1), jnp.concatenate([cross_value_part, cross_output_part], 1)
    )
    back, gain_two_grad = norm_back(y1, gain_two, dot(dq2, cross_query, NT))
    dy1 = dy2 + back
    b1 = dy1.astype(bf)
    self_output_part = dot(o1, b1, TN).astype(bf)
    do1 = dot(b1, self_output, NT).astype(bf)
    far_dq1, far_dk1, far_dv1 = attend_back(far_e1, do1, o1, far_f1, q1, far_k1, far_v1)
    far_first_grad = (dot(far_dk1, self_key, turned) + dot(far_dv1, self_value, turned)).astype(bf)
    near_first_grad = lax.ppermute(far_first_grad, "seq", [(1, 0)])
    dq1, dk1, dv1 = attend_back(e1, do1, o1, f1, q1, k1, v1, causal=True, before=far_dq1)
    self_query_part = dot(first, dq1, TN).astype(bf)
    self_key_part = (dot(first, dk1, turned) + dot(far_first, far_dk1, turned)).astype(bf)
    self_value_part = (dot(first, dv1, turned) + dot(far_first, far_dv1, turned)).astype(bf)
    self_sums = reduce_pair(
        jnp.concatenate([self_query_part, self_key_part], 1), jnp.concatenate([self_value_part, self_output_part], 1)
    )
    first_grad = dot(dq1, self_query, NT) + dot(dk1, self_key, turned) + dot(dv1, self_value, turned)
    first_grad = first_grad + near_first_grad.astype(f32)
    back, gain_one_grad = norm_back(states, gain_one, first_grad)
    input_grad = (dy1 + back).astype(bf)

    gains = lax.psum((gain_one_grad, gain_two_grad, gain_three_grad), ("plots", "seq"))
    share = width // lax.axis_size("plots")
    gains = [lax.dynamic_slice_in_dim(g, lax.axis_index("plots") * share, share, 0) for g in gains]
    return (
        layer_output[None],
        input_grad[None],
        patch_grad[None],
        *gains,
        self_sums[0][:, :width],
        self_sums[0][:, width:],
        self_sums[1][:, :width],
        self_sums[1][:, width:],
        key_value_sums[0][:, width:],
        key_value_sums[0][:, :width],
        key_value_sums[1][:, :width],
        key_value_sums[1][:, width:],
        gate_sum,
        up_sum,
        jnp.concatenate(down_sums, 1),
    )


def solution(mesh):
    rows = P("plots", "seq", None)
    placed = (rows, rows, P("plots"), P("plots")) + (P(),) * 14 + (rows,)
    return jax.shard_map(
        per_device,
        mesh=mesh,
        in_specs=placed,
        out_specs=(rows, rows, rows) + (P("plots"),) * 3 + (P("plots", None),) * 11,
        check_vma=False,
    )
```

```python
import functools

import jax
import jax.numpy as jnp
from jax import lax
from jax.experimental import pallas as pl
from jax.experimental.pallas import tpu as pltpu
from jax.sharding import PartitionSpec as P

HEADS = 12
eps = 1e-06
bf = jnp.bfloat16
f32 = jnp.float32
LOG2E = 1.4426950408889634
LN2 = 0.6931471805599453
MASKED = -1e30
NN = (((1,), (0,)), ((), ()))
NT = (((1,), (1,)), ((), ()))
TN = (((0,), (0,)), ((), ()))
TT = (((0,), (1,)), ((), ()))
SEQ_SWAP = [(0, 1), (1, 0)]


def dot(left, right, dims=NN):
    return lax.dot_general(left, right, dims, preferred_element_type=f32)


def lane_of(shape):
    return lax.broadcasted_iota(jnp.int32, shape, len(shape) - 1)


def head_lanes(lane, half):
    return (lane < 64) if half == 0 else (lane >= 64)


def lane_rows(half):
    lane = lane_of((1, 128))
    inside = jnp.where(head_lanes(lane, half), 1.0, 0.0)
    return inside.astype(bf), jnp.where(lane == 64 - 64 * half, 1.0, 0.0).astype(bf)


def shape_of(shape, dtype=bf):
    return jax.ShapeDtypeStruct(shape, dtype)


def call(kernel, args, outs, grid=(1,), in_specs=None, out_specs=None, scalars=None, scratch=(), flops=0, name=None):
    def whole(a):
        zeros = (0,) * len(a.shape)
        return pl.BlockSpec(a.shape, lambda *_: zeros)

    def specs(given, arrays):
        given = given or [None] * len(arrays)
        return [whole(a) if s is None else s for s, a in zip(given, arrays)]

    grid_spec = pltpu.PrefetchScalarGridSpec(
        num_scalar_prefetch=0 if scalars is None else 1,
        grid=grid,
        in_specs=specs(in_specs, args),
        out_specs=specs(out_specs, outs),
        scratch_shapes=scratch,
    )
    nbytes = sum(a.size * a.dtype.itemsize for a in args) + sum(a.size * a.dtype.itemsize for a in outs)
    if scalars is not None:
        args = [scalars] + list(args)
    return pl.pallas_call(
        kernel,
        grid_spec=grid_spec,
        out_shape=outs,
        compiler_params=pltpu.CompilerParams(vmem_limit_bytes=58 << 20),
        cost_estimate=pl.CostEstimate(flops=flops, bytes_accessed=nbytes, transcendentals=0),
        name=name,
    )(*args)


def attend_kernel(causal, merge, parts, block, q_ref, bias_ref, *refs):
    key_refs, value_refs = refs[:parts], refs[parts : 2 * parts]
    refs = refs[2 * parts :]
    if merge:
        before_ref, e_ref, o_ref, own_ref, new_ref = refs
    elif parts > 1:
        e_ref, o_ref, own_ref = refs
    else:
        e_ref, o_ref = refs
    rows = q_ref.shape[0]
    pairs = q_ref.shape[1] // 128
    lane_b = lane_of((block, 128))
    first = head_lanes(lane_b, 0)
    full = (block, 128)
    items = [(p, b, half) for p in range(pairs) for b in range(rows // block) for half in range(2)]
    kept = {}

    def reaches(b):
        offset, found = 0, []
        for i, k_ref in enumerate(key_refs):
            keys = k_ref.shape[0]
            seen = min(keys, (b + 1) * block) if causal and i == parts - 1 else keys
            found.append((offset, i, seen))
            offset += keys
        return found

    def scores(item):
        p, b, half = item
        lanes = slice(128 * p, 128 * p + 128)
        q = q_ref[b * block : (b + 1) * block, lanes] * lane_rows(half)[0]
        found = []
        for offset, i, seen in reaches(b):
            s = dot(q, key_refs[i][:seen, lanes], NT) + bias_ref[0:1, offset : offset + seen]
            if causal and i == parts - 1:
                row = lax.broadcasted_iota(jnp.int32, s.shape, 0) + b * block
                s = jnp.where(lane_of(s.shape) <= row, s, MASKED)
            found.append(s)
        return found

    def soften(item, found):
        p, b, half = item
        top = functools.reduce(jnp.maximum, [jnp.max(s, axis=1, keepdims=True) for s in found])
        es = []
        for (offset, i, seen), s in zip(reaches(b), found):
            e = jnp.exp2(s - top).astype(bf)
            e_ref[2 * p + half, b * block : (b + 1) * block, offset : offset + seen] = e
            es.append(e)
        return top, es

    def mix(item, top, es):
        p, b, half = item
        lanes = slice(128 * p, 128 * p + 128)
        at = slice(b * block, (b + 1) * block)
        inside, at0 = lane_rows(half)
        spare = 64 - 64 * half
        o = None
        for (offset, i, seen), e in zip(reaches(b), es):
            part = dot(e, value_refs[i][:seen, lanes] * inside + at0)
            o = part if o is None else o + part
        if not merge and parts == 1:
            o_ref[2 * p + half, at, :] = jnp.where(lane_b == spare + 1, top, o)
            return
        l_new = jnp.broadcast_to(o[:, spare : spare + 1], full)
        if merge:
            old = before_ref[2 * p + half, at, :]
            l_old = jnp.broadcast_to(old[:, spare : spare + 1], full)
            m_old = jnp.broadcast_to(old[:, spare + 1 : spare + 2], full)
            top = jnp.broadcast_to(top, full)
            m = jnp.maximum(m_old, top)
            w_old, w_new = jnp.exp2(m_old - m), jnp.exp2(top - m)
            turn = 1.0 / (l_old * w_old + l_new * w_new)
            f_old, f_new = w_old * turn, w_new * turn
            o = old * f_old + o * f_new
        else:
            f_old = f_new = 1.0 / l_new
            o = o * f_new
        if half == 0:
            kept[p, b] = (o, f_old, f_new)
        else:
            o0, old0, new0 = kept.pop((p, b))
            o_ref[at, lanes] = jnp.where(first, o0, o).astype(bf)
            own_ref[at, lanes] = jnp.where(first, old0, f_old)
            if merge:
                new_ref[at, lanes] = jnp.where(first, new0, f_new)

    s = scores(items[0])
    waiting = None
    for i, item in enumerate(items):
        following = scores(items[i + 1]) if i + 1 < len(items) else None
        if waiting is not None:
            mix(*waiting)
        top, es = soften(item, s)
        waiting = (item, top, es)
        s = following
    mix(*waiting)


def attend(q, keys, values, bias, causal=False, before=None, block=256, group=1):
    rows, width = q.shape
    pairs = width // 128
    merge = before is not None
    total = sum(k.shape[0] for k in keys)

    def column(a):
        return pl.BlockSpec((a.shape[0], 128 * group), lambda p: (0, p))

    tall = column(q)
    e_spec = pl.BlockSpec((2 * group, rows, total), lambda p: (p, 0, 0))
    o_spec = pl.BlockSpec((2 * group, rows, 128), lambda p: (p, 0, 0))
    outs, out_specs = [shape_of((2 * pairs, rows, total))], [e_spec]
    args = [q, bias, *keys, *values]
    in_specs = [tall, None] + [column(a) for a in args[2:]]
    if merge:
        args.append(before)
        in_specs.append(o_spec)
    if merge or len(keys) > 1:
        outs += [shape_of((rows, width))] + [shape_of((rows, width), f32)] * (2 if merge else 1)
        out_specs += [tall] * (3 if merge else 2)
    else:
        outs.append(shape_of((2 * pairs, rows, 128), f32))
        out_specs.append(o_spec)
    return call(
        functools.partial(attend_kernel, causal, merge, len(keys), block),
        args,
        outs,
        (pairs // group,),
        in_specs,
        out_specs,
        flops=16 * rows * total * width,
        name="attend",
    )


def attend_back_kernel(causal, last, parts, block, e_ref, do_ref, o_ref, f_ref, q_ref, *refs):
    key_refs, value_refs = refs[:parts], refs[parts : 2 * parts]
    refs = refs[2 * parts :]
    if last:
        before_ref, dq_ref, d_ref = refs
    elif len(refs) == 2:
        dq_ref, d_ref = refs
    else:
        dq_ref, d_ref = None, refs[0]
    base = d_ref.shape[0] - 2
    rows = q_ref.shape[0]
    pairs = q_ref.shape[1] // 128
    lane_b = lane_of((block, 128))
    items = [(p, half, b) for p in range(pairs) for half in range(2) for b in range(rows // block)]
    dq, dk, dv = {}, {}, {}

    def reaches(b):
        offset, found = 0, []
        for i, k_ref in enumerate(key_refs):
            keys = k_ref.shape[0]
            seen = min(keys, (b + 1) * block) if causal and i == parts - 1 else keys
            found.append((offset, i, seen))
            offset += keys
        return found

    def slopes(item):
        p, half, b = item
        lanes = slice(128 * p, 128 * p + 128)
        at = slice(b * block, (b + 1) * block)
        inb = head_lanes(lane_b, half)
        do = do_ref[at, lanes].astype(f32)
        f = f_ref[at, lanes]
        inner = jnp.sum(jnp.where(inb, do * o_ref[at, lanes].astype(f32), 0.0), axis=1, keepdims=True)
        off = inner * f[:, 64 * half : 64 * half + 1]
        dos = jnp.where(inb, do * f, 0.0).astype(bf)
        return dos, off, [dot(dos, value_refs[i][:seen, lanes], NT) for offset, i, seen in reaches(b)]

    def spread(item, dos, off, dps):
        p, half, b = item
        lanes = slice(128 * p, 128 * p + 128)
        at = slice(b * block, (b + 1) * block)
        q = q_ref[at, lanes]
        for (offset, i, seen), dp in zip(reaches(b), dps):
            e = e_ref[2 * p + half, at, offset : offset + seen]
            ds = (e.astype(f32) * (dp - off)).astype(bf)
            part = dot(ds, key_refs[i][:seen, lanes] * lane_rows(half)[0])
            dq[p, b] = part if (p, b) not in dq else dq[p, b] + part
            step = block if causal and i == parts - 1 else seen
            for c in range(0, seen, step):
                key = (p, half, offset + c)
                vt = dot(dos, e[:, c : c + step], TN)
                kt = dot(q, ds[:, c : c + step], TN)
                dv[key] = vt if key not in dv else dv[key] + vt
                dk[key] = kt if key not in dk else dk[key] + kt

    ready = slopes(items[0])
    for i, item in enumerate(items):
        following = slopes(items[i + 1]) if i + 1 < len(items) else None
        spread(item, *ready)
        ready = following
    for p, b in dq:
        lanes = slice(128 * p, 128 * p + 128)
        at = slice(b * block, (b + 1) * block)
        part = dq[p, b]
        if last:
            dq_ref[at, lanes] = ((part + before_ref[at, lanes]) * 0.125).astype(bf)
        elif base == 0:
            dq_ref[at, lanes] = part
        else:
            d_ref[0, lanes, d_ref.shape[2] - rows + b * block : d_ref.shape[2] - rows + (b + 1) * block] = (
                part.T * 0.125
            ).astype(bf)
    for p, half, c in dk:
        wide = dk[p, half, c].shape[1]
        inside = slice(64 * half, 64 * half + 64)
        at = slice(128 * p + 64 * half, 128 * p + 64 * half + 64)
        d_ref[base, at, c : c + wide] = (dk[p, half, c][inside] * LN2).astype(bf)
        d_ref[base + 1, at, c : c + wide] = dv[p, half, c][inside].astype(bf)


def attend_back(e, do, o, f, q, keys, values, causal=False, before=None, whole=False, block=256, group=1):
    rows, width = q.shape
    pairs = width // 128
    total = sum(k.shape[0] for k in keys)

    def column(a):
        return pl.BlockSpec((a.shape[0], 128 * group), lambda p: (0, p))

    tall = column(q)
    args = [e, do, o, f, q, *keys, *values]
    in_specs = [pl.BlockSpec((2 * group, rows, total), lambda p: (p, 0, 0))] + [column(a) for a in args[1:]]
    if before is not None:
        args.append(before)
        in_specs.append(tall)
    return call(
        functools.partial(attend_back_kernel, causal, before is not None, len(keys), block),
        args,
        ([] if whole else [shape_of((rows, width), f32 if before is None else bf)])
        + [shape_of((2 + whole, width, total))],
        (pairs // group,),
        in_specs,
        ([] if whole else [tall]) + [pl.BlockSpec((2 + whole, 128 * group, total), lambda p: (0, p, 0))],
        flops=16 * rows * total * width,
        name="attend_back",
    )


def late(refs, buffers, sems):
    copies = [pltpu.make_async_copy(ref, buffer, sems.at[i]) for i, (ref, buffer) in enumerate(zip(refs, buffers))]

    @pl.when(pl.program_id(0) == 0)
    def _():
        for copy in copies:
            copy.start()

    def fetch(i):
        copies[i].wait()
        return buffers[i]

    return fetch


def self_back(e, do, o, f, q, keys, values, far_first, first, wk, wv):
    rows, width = q.shape
    pairs = width // 128
    total = 2 * rows
    half = width // 2
    back = functools.partial(attend_back_kernel, True, False, 2, 256)

    def kernel(core_ref, *refs):
        blocks, (ff_ref, first_ref, wk_ref, wv_ref) = refs[:9], refs[9:13]
        d_ref, *send_refs, keep_ref, out_ref = refs[13:19]
        all_ref, part_ref, *buffers, sems = refs[19:]
        fetch = late([ff_ref, first_ref, wk_ref, wv_ref], buffers, sems)
        i = pl.program_id(0)
        core = core_ref[0]

        @pl.when(i < pairs)
        def _():
            back(*blocks, part_ref)
            d_ref[...] = part_ref[:, :, rows:]
            all_ref[:, pl.ds(pl.multiple_of(i * 128, 128), 128), :] = part_ref[...]

        @pl.when(i == pairs)
        def _():
            far, own = fetch(0)[...], fetch(1)[...]
            query = dot(own, all_ref[0, :, rows:], TT)
            key = dot(far, all_ref[1, :, :rows], TT) + dot(own, all_ref[1, :, rows:], TT)
            halves(send_refs, keep_ref, core, 0, query, key)

        @pl.when(i == pairs + 1)
        def _():
            far, own = buffers[0][...], buffers[1][...]
            value = dot(far, all_ref[2, :, :rows], TT) + dot(own, all_ref[2, :, rows:], TT)
            halves(send_refs, keep_ref, core, width, value[:, :half], value[:, half:])
            grad = dot(all_ref[1, :, :rows], fetch(2)[...], TT) + dot(all_ref[2, :, :rows], fetch(3)[...], TT)
            out_ref[...] = grad.astype(bf)

    def column(a):
        return pl.BlockSpec((a.shape[0], 128), lambda i, s: (0, jnp.minimum(i, pairs - 1)))

    args = [e, do, o, f, q, *keys, *values, far_first, first, wk, wv]
    in_specs = [pl.BlockSpec((2, rows, total), lambda i, s: (jnp.minimum(i, pairs - 1), 0, 0))]
    in_specs += [column(a) for a in args[1:9]] + [pl.BlockSpec(memory_space=pl.ANY)] * 4
    own = pl.BlockSpec((3, 128, rows), lambda i, s: (0, jnp.minimum(i, pairs - 1), 0))
    return call(
        kernel,
        args,
        [shape_of((3, width, rows))]
        + [shape_of((width, half))] * 3
        + [shape_of((width, width + half)), shape_of((rows, width))],
        (pairs + 2,),
        in_specs,
        [own] + [None] * 5,
        core_scalar(),
        scratch=[pltpu.VMEM((3, width, total), bf), pltpu.VMEM((3, 128, total), bf)]
        + [pltpu.VMEM(a.shape, bf) for a in args[9:]]
        + [pltpu.SemaphoreType.DMA((4,))],
        flops=16 * rows * total * width + 12 * rows * width * width,
        name="self_back",
    )


def norm_parts(value):
    scale = lax.rsqrt(jnp.mean(value * value, axis=-1, keepdims=True) + eps)
    return value * scale, scale


def norm_back(unit, scale, gain, grad):
    inner = gain * grad
    return scale * (inner - unit * jnp.mean(inner * unit, axis=-1, keepdims=True))


def gelu_parts(u):
    t = jnp.tanh(0.7978845608028654 * (u + 0.044715 * u * u * u))
    value = 0.5 * u * (1.0 + t)
    slope = 0.5 * (1.0 + t) + 0.5 * u * (1.0 - t * t) * (0.7978845608028654 * (1.0 + 3 * 0.044715 * u * u))
    return value, slope


def start(x, gain, patches, weights, scale):
    def kernel(x_ref, gain_ref, p_ref, w0, w1, w2, w3, w4, first_ref, q_ref, k1_ref, v1_ref, k2_ref, v2_ref):
        i = pl.program_id(0)

        @pl.when(i == 0)
        def _():
            first = (norm_parts(x_ref[...].astype(f32))[0] * gain_ref[...]).astype(bf)
            first_ref[...] = first
            q_ref[...] = (dot(first, w0[...]) * scale).astype(bf)

        for j, left, w_ref, out_ref in (
            (1, first_ref, w1, k1_ref),
            (2, first_ref, w2, v1_ref),
            (3, p_ref, w3, k2_ref),
            (4, p_ref, w4, v2_ref),
        ):

            @pl.when(i == j)
            def _(left=left, w_ref=w_ref, out_ref=out_ref):
                out_ref[...] = dot(left[...], w_ref[...]).astype(bf)

    return call(
        kernel,
        [x, gain, patches, *weights],
        [shape_of(x.shape)] * 4 + [shape_of(patches.shape)] * 2,
        (5,),
        flops=2 * 768 * (3 * x.size + 2 * patches.size),
        name="start",
    )


def project_far(x, gain, wk, wv):
    def kernel(x_ref, gain_ref, wk_ref, wv_ref, first_ref, k_ref, v_ref):
        first = (norm_parts(x_ref[...].astype(f32))[0] * gain_ref[...]).astype(bf)
        first_ref[...] = first
        k_ref[...] = dot(first, wk_ref[...]).astype(bf)
        v_ref[...] = dot(first, wv_ref[...]).astype(bf)

    return call(kernel, [x, gain, wk, wv], [shape_of(x.shape)] * 3, flops=4 * x.size * 768, name="project_far")


def project_patches(x, wk, wv):
    def kernel(x_ref, wk_ref, wv_ref, k_ref, v_ref):
        k_ref[...] = dot(x_ref[...], wk_ref[...]).astype(bf)
        v_ref[...] = dot(x_ref[...], wv_ref[...]).astype(bf)

    rows = pl.BlockSpec((x.shape[0] // 2, x.shape[1]), lambda i: (i, 0))
    return call(
        kernel, [x, wk, wv], [shape_of(x.shape)] * 2, (2,), [rows, None, None], [rows, rows],
        flops=4 * x.size * 768, name="project_patches",
    )


def between(x, o, w_out, gain, w_query, scale):
    def kernel(x_ref, o_ref, wo_ref, gain_ref, wq_ref, y_ref, n_ref, q_ref):
        y = x_ref[...].astype(f32) + dot(o_ref[...], wo_ref[...])
        y_ref[...] = y
        second = (norm_parts(y)[0] * gain_ref[...]).astype(bf)
        n_ref[...] = second
        q_ref[...] = (dot(second, wq_ref[...]) * scale).astype(bf)

    rows = pl.BlockSpec((x.shape[0] // 2, x.shape[1]), lambda i: (i, 0))
    return call(
        kernel, [x, o, w_out, gain, w_query], [shape_of(x.shape, f32), shape_of(x.shape), shape_of(x.shape)], (2,),
        [rows, rows, None, None, None], [rows] * 3, flops=4 * x.size * 768, name="between",
    )


def feed_forward(y1, o, w_out, gain, w_gate, w_up, w_down, dy):
    def kernel(y1_ref, o_ref, wo_ref, gain_ref, wg_ref, wu_ref, wd_ref, dy_ref, y2_ref, third_ref, h_ref, d_ref):
        @pl.when(pl.program_id(0) == 0)
        def _():
            y2 = y1_ref[...] + dot(o_ref[...], wo_ref[...])
            y2_ref[...] = y2
            third_ref[...] = (norm_parts(y2)[0] * gain_ref[...]).astype(bf)

        half = y1_ref.shape[0] // 2
        for i in range(2):
            at = slice(i * half, (i + 1) * half)
            third = third_ref[at, :]
            gate = dot(third, wg_ref[...])
            up = dot(third, wu_ref[...])
            dhidden = dot(dy_ref[at, :], wd_ref[...], NT)
            act, slope = gelu_parts(gate)
            h_ref[at, :] = (act * up).astype(bf)
            d_ref[0, at, :] = (dhidden * up * slope).astype(bf)
            d_ref[1, at, :] = (dhidden * act).astype(bf)

    rows, width = y1.shape
    hidden = w_gate.shape[1]
    column = pl.BlockSpec((width, 512), lambda i: (0, i))
    return call(
        kernel,
        [y1, o, w_out, gain, w_gate, w_up, w_down, dy],
        [shape_of(y1.shape, f32), shape_of(y1.shape), shape_of((rows, hidden)), shape_of((2, rows, hidden))],
        (hidden // 512,),
        [None, None, None, None, column, column, pl.BlockSpec((512, width), lambda i: (i, 0)), None],
        [None, None, pl.BlockSpec((rows, 512), lambda i: (0, i)), pl.BlockSpec((2, rows, 512), lambda i: (0, 0, i))],
        flops=2 * y1.size * (768 + 3 * hidden),
        name="feed_forward",
    )


def feed_back(d, w_gate, w_up, y2, gain, dy, w_out):
    def kernel(d_ref, wg_ref, wu_ref, y2_ref, gain_ref, dy_ref, wo_ref, dy2_ref, b_ref, do_ref, g_ref, acc_ref):
        i = pl.program_id(0)
        part = dot(d_ref[0], wg_ref[...], NT) + dot(d_ref[1], wu_ref[...], NT)

        @pl.when(i == 0)
        def _():
            acc_ref[...] = part

        @pl.when(i > 0)
        def _():
            acc_ref[...] += part

        @pl.when(i == pl.num_programs(0) - 1)
        def _():
            grad = acc_ref[...]
            unit, scale = norm_parts(y2_ref[...])
            dy2 = dy_ref[...].astype(f32) + norm_back(unit, scale, gain_ref[...], grad)
            dy2_ref[...] = dy2
            b_ref[...] = dy2.astype(bf)
            do_ref[...] = dot(b_ref[...], wo_ref[...], NT).astype(bf)
            g_ref[...] = jnp.sum(grad * unit, axis=0, keepdims=True)

    rows, width = y2.shape
    hidden = w_gate.shape[1]
    column = pl.BlockSpec((width, 512), lambda i: (0, i))
    return call(
        kernel,
        [d, w_gate, w_up, y2, gain, dy, w_out],
        [shape_of(y2.shape, f32), shape_of(y2.shape), shape_of(y2.shape), shape_of(gain.shape, f32)],
        (hidden // 512,),
        [pl.BlockSpec((2, rows, 512), lambda i: (0, 0, i)), column, column, None, None, None, None],
        scratch=[pltpu.VMEM((rows, width), f32)],
        flops=2 * y2.size * (768 + 2 * hidden),
        name="feed_back",
    )


def between_back(dq, w_query, y1, gain, dy2, w_out):
    def kernel(dq_ref, wq_ref, y_ref, gain_ref, dy_ref, wo_ref, dy1_ref, b_ref, do_ref, g_ref):
        grad = dot(dq_ref[...], wq_ref[...], NT)
        unit, scale = norm_parts(y_ref[...])
        dy1 = dy_ref[...] + norm_back(unit, scale, gain_ref[...], grad)
        dy1_ref[...] = dy1
        b_ref[...] = dy1.astype(bf)
        do_ref[...] = dot(b_ref[...], wo_ref[...], NT).astype(bf)
        sums = jnp.sum(grad * unit, axis=0, keepdims=True)

        @pl.when(pl.program_id(0) == 0)
        def _():
            g_ref[...] = sums

        @pl.when(pl.program_id(0) > 0)
        def _():
            g_ref[...] += sums

    rows = pl.BlockSpec((y1.shape[0] // 2, y1.shape[1]), lambda i: (i, 0))
    return call(
        kernel, [dq, w_query, y1, gain, dy2, w_out],
        [shape_of(y1.shape, f32), shape_of(y1.shape), shape_of(y1.shape), shape_of(gain.shape, f32)], (2,),
        [rows, None, rows, None, rows, None], [rows] * 3 + [None],
        flops=4 * y1.size * 768, name="between_back",
    )


def finish(d, wq, wk, wv, near, x, gain, dy1):
    def kernel(d_ref, wq_ref, wk_ref, wv_ref, near_ref, x_ref, gain_ref, dy_ref, out_ref, g_ref):
        grad = near_ref[...].astype(f32)
        for j, w_ref in enumerate((wq_ref, wk_ref, wv_ref)):
            grad = grad + dot(d_ref[j], w_ref[...], TT)
        unit, scale = norm_parts(x_ref[...].astype(f32))
        out_ref[...] = (dy_ref[...] + norm_back(unit, scale, gain_ref[...], grad)).astype(bf)
        g_ref[...] = jnp.sum(grad * unit, axis=0, keepdims=True)

    rows = x.shape[0]
    return call(
        kernel, [d, wq, wk, wv, near, x, gain, dy1], [shape_of(x.shape), shape_of(gain.shape, f32)], (1,),
        flops=6 * x.size * 768, name="finish",
    )


def output(y2, hidden, w_down):
    def kernel(y_ref, h_ref, w_ref, out_ref):
        out_ref[...] = (y_ref[...] + dot(h_ref[...], w_ref[...])).astype(bf)

    rows, width = y2.shape
    half = pl.BlockSpec((rows, width // 2), lambda i: (0, i))
    return call(
        kernel, [y2, hidden, w_down], [shape_of(y2.shape)], (2,),
        [half, None, pl.BlockSpec((hidden.shape[1], width // 2), lambda i: (0, i))], [half],
        flops=2 * hidden.size * width, name="output",
    )[0]


def key_value_back(d, wk, wv, near=()):
    keys = d.shape[2]
    half = keys // 2

    def kernel(d_ref, wk_ref, wv_ref, *refs):
        grad = dot(d_ref[0], wk_ref[...], TT) + dot(d_ref[1], wv_ref[...], TT)
        if near:
            refs[2][...] = (grad + jnp.where(pl.program_id(0) == 0, refs[0][...], refs[1][...]).astype(f32)).astype(bf)
            return
        for i in range(2):

            @pl.when(pl.program_id(0) == i)
            def _(i=i):
                refs[i][...] = grad.astype(bf)

    rows = pl.BlockSpec((half, wk.shape[0]), lambda i: (i, 0))
    part = pl.BlockSpec((2, d.shape[1], half), lambda i: (0, 0, i))
    shape = (half, wk.shape[0])
    out = call(
        kernel,
        [d, wk, wv, *near],
        [shape_of((keys, wk.shape[0]))] if near else [shape_of(shape)] * 2,
        (2,),
        [part] + [None] * (2 + len(near)),
        [rows] if near else None,
        flops=4 * keys * 768 * 768,
        name="key_value_back",
    )
    return out[0] if near else out


def ring_factors(groups):
    inner = 1
    while inner * inner * 4 <= groups:
        inner *= 2
    return inner, groups // inner


def places():
    total = lax.axis_size("plots")
    index = lax.axis_index("plots")
    inner, outer = ring_factors(total // 2)
    group = index // 2
    return total, inner, outer, group // inner, group % inner, index % 2


def core_swap(value):
    total = lax.axis_size("plots")
    return lax.ppermute(value, "plots", [(i, i ^ 1) for i in range(total)])


def outer_shift(value, k):
    total, inner, outer, *_ = places()
    stride = 2 * inner
    return lax.ppermute(value, "plots", [(i, ((i // stride + k) % outer) * stride + i % stride) for i in range(total)])


def inner_shift(value, k):
    total, inner, outer, *_ = places()

    def spot(i):
        y = (i // 2) % inner
        return i + ((y + k) % inner - y) * 2

    return lax.ppermute(value, "plots", [(i, spot(i)) for i in range(total)])


def hold(value, *tokens):
    return lax.optimization_barrier((value,) + tokens)[0]


def halves(send_refs, keep_ref, core, start, one, two):
    here = core == 0
    send = jnp.where(here, two, one).astype(bf)
    keep_ref[:, start : start + one.shape[1]] = jnp.where(here, one, two).astype(bf)
    wide = send_refs[0].shape[1]
    for c in range(0, one.shape[1], wide):
        send_refs[(start + c) // wide][...] = send[:, c : c + wide]


def core_scalar():
    return (lax.axis_index("plots") % 2).astype(jnp.int32)[None]


def combine(keep, pieces):
    outer, inner, share, columns = keep.shape

    def kernel(y_ref, keep_ref, *refs):
        *piece_refs, mine_ref, send_ref = refs
        y = y_ref[0]
        start = 0
        for ref in piece_refs:
            at = slice(start, start + ref.shape[3])
            start += ref.shape[3]
            one = keep_ref[0, 0, :, at].astype(f32) + ref[0, 0].astype(f32)
            two = keep_ref[0, 1, :, at].astype(f32) + ref[0, 1].astype(f32)
            mine_ref[0, :, at] = jnp.where(y == 0, one, two).astype(bf)
            send_ref[0, :, at] = jnp.where(y == 0, two, one).astype(bf)

    def block(a):
        return pl.BlockSpec((1,) + a.shape[1:], lambda i, s: (i,) + (0,) * (len(a.shape) - 1))

    args = [keep] + [p.reshape(outer, inner, share, p.shape[1]) for p in pieces]
    out = shape_of((outer, share, columns))
    return call(
        kernel, args, [out, out], (outer,), [block(a) for a in args], [block(out)] * 2,
        places()[4].astype(jnp.int32)[None], name="combine",
    )


class Sum:
    def __init__(self, sends, keep):
        self.token = sends[-1]
        self.mine = keep
        self.got = [core_swap(send) for send in sends]

    def inner_step(self, *tokens):
        total, inner, outer, z, y, core = places()
        split = (outer, inner, self.mine.shape[0] // (outer * inner), self.mine.shape[1])
        mine = self.mine.reshape(split)
        got = lax.optimization_barrier(tuple(self.got) + tokens)[: len(self.got)]
        if inner == 2:
            self.mine, self.token = combine(mine, got)
            self.got = lax.ppermute(self.token, "plots", [(i, i ^ 2) for i in range(total)])
        else:
            got = jnp.concatenate(got, 1).reshape(split)
            groups = [[(o * inner + i) * 2 + c for i in range(inner)] for o in range(outer) for c in range(2)]
            self.token = (mine.astype(f32) + got.astype(f32)).astype(bf)
            self.mine = None
            self.got = lax.all_to_all(self.token, "plots", 1, 1, axis_index_groups=groups, tiled=True)

    def outer_step(self, *tokens, gains=None):
        total, inner, outer, z, y, core = places()
        got = hold(self.got, *tokens)
        if gains is not None:
            gains = gains.reshape(3, outer, inner, -1)
            gains = lax.dynamic_index_in_dim(gains, y, 2, keepdims=False).transpose(1, 0, 2)
            gains = jnp.pad(gains, ((0, 0), (0, 13), (0, got.shape[-1] - gains.shape[2]))).astype(bf)

        def part(at):
            if self.mine is None:
                value = lax.dynamic_index_in_dim(got, at, 0, keepdims=False)
                value = jnp.sum(value.astype(f32), axis=0).astype(bf)
            else:
                one = lax.dynamic_index_in_dim(self.mine, at, 0, keepdims=False)
                two = lax.dynamic_index_in_dim(got, at, 0, keepdims=False)
                value = (one.astype(f32) + two.astype(f32)).astype(bf)
            if gains is not None:
                value = jnp.concatenate([value, lax.dynamic_index_in_dim(gains, at, 0, keepdims=False)], 0)
            return value

        self.parts = [part((z + k) % outer) for k in range(1, outer)]
        self.got = [outer_shift(value, k + 1) for k, value in enumerate(self.parts)]
        self.token = self.parts[-1]
        self.mine = part(z)

    def seq_step(self, *tokens):
        got = lax.optimization_barrier(tuple(self.got) + tokens)[: len(self.got)]
        self.mine = sum((g.astype(f32) for g in got), self.mine.astype(f32)).astype(bf)
        self.token = self.mine
        self.got = lax.ppermute(self.mine, "seq", SEQ_SWAP)

    def core_step(self, *tokens, gains=False):
        core = lax.axis_index("plots") % 2
        value = self.mine.astype(f32) + hold(self.got, *tokens).astype(f32)
        if gains:
            share = (value.shape[0] - 16) // 2
            extra = lax.dynamic_slice_in_dim(value[-16:-13], core * share, share, 1)
            self.gains = [extra[i] for i in range(3)]
            value = value[:-16]
        value = value.reshape((2, value.shape[0] // 2) + value.shape[1:])
        self.mine = lax.dynamic_index_in_dim(value, core, 0, keepdims=False)
        self.token = lax.dynamic_index_in_dim(value, 1 - core, 0, keepdims=False).astype(bf)
        self.got = core_swap(self.token)

    def done(self):
        core = lax.axis_index("plots") % 2
        other = self.got.astype(f32)
        return jnp.where(core == 0, self.mine, other), jnp.where(core == 0, other, self.mine)


def feed_grad(hidden, dy, third, d):
    total, inner, outer, *_ = places()
    groups = inner * outer
    tokens, wide = hidden.shape
    width = third.shape[1]
    share, turned = width // groups, wide // groups
    lanes = turned
    blocks = wide // lanes
    step = 512
    per = step // lanes

    def kernel(core_ref, h_ref, dy_ref, third_ref, d_ref, send_ref, keep_ref):
        i = pl.program_id(0)
        here = core_ref[0] == 0
        third = third_ref[...]
        gate, up = dot(third, d_ref[0], TN), dot(third, d_ref[1], TN)
        send, keep = jnp.where(here, up, gate).astype(bf), jnp.where(here, gate, up).astype(bf)
        for g in range(groups):
            rows = slice(g * share, (g + 1) * share)
            for c in range(per):
                at = pl.ds(pl.multiple_of((i * per + c) * share, share), share)
                send_ref[g, at, :] = send[rows, c * lanes : (c + 1) * lanes]
                keep_ref[g, at, :] = keep[rows, c * lanes : (c + 1) * lanes]
        down = dot(dy_ref[...], h_ref[...], TN)
        half = width // 2
        send, keep = jnp.where(here, down[half:], down[:half]), jnp.where(here, down[:half], down[half:])
        for c in range(per):
            at = slice(blocks * share, blocks * share + half)
            send_ref[i * per + c, at, :] = send[:, c * lanes : (c + 1) * lanes].astype(bf)
            keep_ref[i * per + c, at, :] = keep[:, c * lanes : (c + 1) * lanes].astype(bf)

    out = shape_of((groups, blocks * share + width // 2, lanes))
    column = pl.BlockSpec((tokens, step), lambda i, s: (0, i))
    return call(
        kernel, [hidden, dy, third, d], [out, out], (wide // step,),
        [column, None, None, pl.BlockSpec((2, tokens, step), lambda i, s: (0, 0, i))], scalars=core_scalar(),
        flops=6 * tokens * wide * width, name="feed_grad",
    )


class FeedSum:
    def __init__(self, send, keep):
        self.token = send
        self.mine = keep
        self.got = core_swap(send)

    def group_step(self, *tokens):
        total, inner, outer, *_ = places()
        value = (self.mine.astype(f32) + hold(self.got, *tokens).astype(f32)).astype(bf)
        pairs = [[2 * g + c for g in range(inner * outer)] for c in range(2)]
        self.token = value
        self.got = lax.psum_scatter(value, "plots", scatter_dimension=0, axis_index_groups=pairs, tiled=True)

    def seq_step(self, *tokens):
        self.mine = hold(self.got, *tokens)[0]
        self.token = self.mine
        self.got = lax.ppermute(self.mine, "seq", SEQ_SWAP)

    def core_step(self, share, blocks, *tokens):
        core = lax.axis_index("plots") % 2
        value = self.mine.astype(f32) + hold(self.got, *tokens).astype(f32)
        lanes = value.shape[1]
        gate = value[: blocks * share].reshape(blocks, 2, share // 2, lanes).transpose(1, 2, 0, 3)
        gate = gate.reshape(2, share // 2, blocks * lanes)
        down = value[blocks * share :].T.reshape(2, lanes // 2, value.shape[0] - blocks * share)

        def trade(a):
            mine = lax.dynamic_index_in_dim(a, core, 0, keepdims=False)
            got = core_swap(lax.dynamic_index_in_dim(a, 1 - core, 0, keepdims=False).astype(bf)).astype(f32)
            return jnp.where(core == 0, mine, got), jnp.where(core == 0, got, mine)

        gate, up = trade(gate)
        return gate, up, jnp.concatenate(trade(down), 1)


def cross_grad(patches, far_patches, d, far_d, second, dq, o2, b2, o1, b1):
    tokens, width = second.shape
    half = width // 2
    chunk = 512
    own, far = patches.shape[0] // chunk, far_patches.shape[0] // chunk

    def kernel(core_ref, p_ref, fp_ref, d_ref, fd_ref, n_ref, dq_ref, o2_ref, b2_ref, o1_ref, b1_ref, *refs):
        *send_refs, keep_ref, acc_ref = refs
        i = pl.program_id(0)
        core = core_ref[0]

        @pl.when(i == 0)
        def _():
            left = p_ref[...]
            acc_ref[0] = dot(left, d_ref[0], TT)
            acc_ref[1] = dot(left, d_ref[1], TT)

        @pl.when((i > 0) & (i < own))
        def _():
            left = p_ref[...]
            acc_ref[0] += dot(left, d_ref[0], TT)
            acc_ref[1] += dot(left, d_ref[1], TT)

        @pl.when((i >= own) & (i < own + far))
        def _():
            left = fp_ref[...]
            acc_ref[0] += dot(left, fd_ref[0], TT)
            acc_ref[1] += dot(left, fd_ref[1], TT)

        @pl.when(i == own + far)
        def _():
            halves(send_refs, keep_ref, core, 0, acc_ref[0], acc_ref[1])
            query, output = dot(n_ref[...], dq_ref[...], TN), dot(o2_ref[...], b2_ref[...], TN)
            halves(send_refs, keep_ref, core, width, query, output)
            value = dot(o1_ref[...], b1_ref[...], TN)
            halves(send_refs, keep_ref, core, 2 * width, value[:, :half], value[:, half:])

    def rows(first, count):
        return pl.BlockSpec((chunk, width), lambda i, s: (jnp.clip(i - first, 0, count - 1), 0))

    def columns(first, count):
        return pl.BlockSpec((2, width, chunk), lambda i, s: (0, 0, jnp.clip(i - first, 0, count - 1)))

    return call(
        kernel,
        [patches, far_patches, d, far_d, second, dq, o2, b2, o1, b1],
        [shape_of((width, half))] * 5 + [shape_of((width, 2 * width + half))],
        (own + far + 1,),
        [rows(0, own), rows(own, far), columns(0, own), columns(own, far)] + [None] * 6,
        scalars=core_scalar(),
        scratch=[pltpu.VMEM((2, width, width), f32)],
        flops=2 * width * width * (3 * tokens + 4 * patches.shape[0]),
        name="cross_grad",
    )


def per_device(
    decoder_states,
    encoder_patches,
    token_lengths,
    patch_counts,
    self_gain,
    cross_gain,
    mlp_gain,
    self_query,
    self_key,
    self_value,
    self_output,
    cross_query,
    cross_key,
    cross_value,
    cross_output,
    mlp_gate,
    mlp_up,
    mlp_down,
    output_grad,
):
    plots, rows, width = decoder_states.shape
    assert plots == 1 and width == 64 * HEADS
    patch_rows = encoder_patches.shape[1]
    place = lax.axis_index("seq")
    token = jnp.arange(rows, dtype=jnp.int32)
    slot = jnp.arange(patch_rows, dtype=jnp.int32)

    def length_bias(valid):
        return jnp.broadcast_to(jnp.where(valid, 0.0, MASKED)[None, :], (8, valid.shape[0]))

    self_bias = length_bias(
        jnp.concatenate([(token < token_lengths[0]) & (place == 1), token + place * rows < token_lengths[0]])
    )
    cross_own = length_bias(slot + place * patch_rows < patch_counts[0])
    cross_far = length_bias(slot + (1 - place) * patch_rows < patch_counts[0])
    gain_one, gain_two, gain_three = (g.astype(f32)[None, :] for g in (self_gain, cross_gain, mlp_gain))
    scale = 0.125 * LOG2E

    x = decoder_states[0]
    patches = encoder_patches[0]
    dy = output_grad[0]
    far_x = lax.ppermute(x, "seq", [(0, 1)])
    weights = [self_query, self_key, self_value, cross_key, cross_value]
    first, q1, k1, v1, k2, v2 = start(x, gain_one, patches, weights, scale)
    far_x = hold(far_x, k2)
    far_patches = lax.ppermute(hold(patches, far_x), "seq", SEQ_SWAP)
    far_first, far_k1, far_v1 = project_far(far_x, gain_one, self_key, self_value)
    e1, o1, f1 = attend(q1, [far_k1, k1], [far_v1, v1], self_bias, causal=True)
    y1, second, q2 = between(x, o1, self_output, gain_two, cross_query, scale)
    e2, part2 = attend(q2, [k2], [v2], cross_own)
    far_patches = hold(far_patches, part2)
    far_k2, far_v2 = project_patches(far_patches, cross_key, cross_value)
    far_e2, o2, f2, far_f2 = attend(q2, [far_k2], [far_v2], cross_far, before=part2, block=512)

    y2, third, hidden, dgu = feed_forward(y1, o2, cross_output, gain_three, mlp_gate, mlp_up, mlp_down, dy)
    feed = FeedSum(*feed_grad(hidden, dy, third, dgu))
    dgu = hold(dgu, feed.token)
    dy2, b2, do2, gain_three_grad = feed_back(dgu, mlp_gate, mlp_up, y2, gain_three, dy, cross_output)
    feed.group_step(do2)
    do2 = hold(do2, feed.token)
    far_dq2, far_d2 = attend_back(far_e2, do2, o2, far_f2, q2, [far_k2], [far_v2])
    far_patch_grad = key_value_back(far_d2, cross_key, cross_value)
    near_low = lax.ppermute(far_patch_grad[0], "seq", SEQ_SWAP)
    do2 = hold(do2, far_patch_grad[0])
    dq2, d2 = attend_back(e2, do2, o2, f2, q2, [k2], [v2], before=far_dq2)
    near_low = hold(near_low, d2)
    dq2 = hold(dq2, near_low)
    dy1, b1, do1, gain_two_grad = between_back(dq2, cross_query, y1, gain_two, dy2, self_output)
    near_high = lax.ppermute(hold(far_patch_grad[1], b1), "seq", SEQ_SWAP)
    *sends, keep = cross_grad(patches, far_patches, d2, far_d2, second, dq2, o2, b2, o1, b1)
    cross = Sum(sends, keep)
    near_high = hold(near_high, cross.token)
    patch_grad = key_value_back(d2, cross_key, cross_value, [near_low, near_high])
    cross.inner_step(patch_grad)
    do1 = hold(do1, cross.token)
    d1, *sends, keep, far_first_grad = self_back(
        e1, do1, o1, f1, q1, [far_k1, k1], [far_v1, v1], far_first, first, self_key, self_value
    )
    own = Sum(sends, keep)
    near_first_grad = lax.ppermute(far_first_grad, "seq", [(1, 0)])
    feed.seq_step(own.token)
    layer_output = output(y2, hold(hidden, own.token, feed.token), mlp_down)
    own.inner_step(layer_output)
    cross.outer_step(own.token)
    near_first_grad = hold(near_first_grad, cross.token)
    input_grad, gain_one_grad = finish(d1, self_query, self_key, self_value, near_first_grad, x, gain_one, dy1)
    groups = lax.axis_size("plots") // 2
    feed_sums = feed.core_step(width // groups, groups, cross.token)
    cross.seq_step(input_grad)
    gains = hold(jnp.concatenate([gain_one_grad, gain_two_grad, gain_three_grad], 0), cross.token)
    gains = gains + core_swap(gains)
    gains = sum((inner_shift(gains, k) for k in range(1, places()[1])), gains)
    own.outer_step(gains, gains=gains)
    cross.core_step(own.token)
    own.seq_step(cross.token)
    own.core_step(gains=True)
    gains = own.gains
    cross_one, cross_two = cross.done()
    self_one, self_two = own.done()
    gate_sum, up_sum, down_sum = feed_sums

    def joined(one, two, at):
        return jnp.concatenate([one[:, at:], two[:, at:]], 1)

    return (
        layer_output[None],
        input_grad[None],
        patch_grad[None],
        *gains,
        self_one[:, :width],
        self_two[:, :width],
        joined(self_one, self_two, width),
        joined(cross_one, cross_two, 2 * width),
        cross_one[:, width : 2 * width],
        cross_one[:, :width],
        cross_two[:, :width],
        cross_two[:, width : 2 * width],
        gate_sum,
        up_sum,
        down_sum,
    )


def solution(mesh):
    rows = P("plots", "seq", None)
    placed = (rows, rows, P("plots"), P("plots")) + (P(),) * 14 + (rows,)
    return jax.shard_map(
        per_device,
        mesh=mesh,
        in_specs=placed,
        out_specs=(rows, rows, rows) + (P("plots"),) * 3 + (P("plots", None),) * 11,
        check_vma=False,
    )
```

```python
import functools

import jax
import jax.numpy as jnp
from jax import lax
from jax.experimental import pallas as pl
from jax.experimental.pallas import tpu as pltpu
from jax.sharding import PartitionSpec as P

HEADS = 12
eps = 1e-06
bf = jnp.bfloat16
f32 = jnp.float32
LOG2E = 1.4426950408889634
LN2 = 0.6931471805599453
MASKED = -1e30
NN = (((1,), (0,)), ((), ()))
NT = (((1,), (1,)), ((), ()))
TN = (((0,), (0,)), ((), ()))
TT = (((0,), (1,)), ((), ()))
SEQ_SWAP = [(0, 1), (1, 0)]


def dot(left, right, dims=NN):
    return lax.dot_general(left, right, dims, preferred_element_type=f32)


def lane_of(shape):
    return lax.broadcasted_iota(jnp.int32, shape, len(shape) - 1)


def head_lanes(lane, half):
    return (lane < 64) if half == 0 else (lane >= 64)


def lane_rows(half):
    lane = lane_of((1, 128))
    inside = jnp.where(head_lanes(lane, half), 1.0, 0.0)
    return inside.astype(bf), jnp.where(lane == 64 - 64 * half, 1.0, 0.0).astype(bf)


ANY = pl.BlockSpec(memory_space=pl.ANY)


def shape_of(shape, dtype=bf):
    return jax.ShapeDtypeStruct(shape, dtype)


def call(kernel, args, outs, grid=(1,), in_specs=None, out_specs=None, scalars=None, scratch=(), flops=0, name=None):
    def whole(a):
        zeros = (0,) * len(a.shape)
        return pl.BlockSpec(a.shape, lambda *_: zeros, pipeline_mode=pl.Buffered(1))

    def specs(given, arrays):
        given = given or [None] * len(arrays)
        return [whole(a) if s is None else s for s, a in zip(given, arrays)]

    grid_spec = pltpu.PrefetchScalarGridSpec(
        num_scalar_prefetch=0 if scalars is None else 1,
        grid=grid,
        in_specs=specs(in_specs, args),
        out_specs=specs(out_specs, outs),
        scratch_shapes=scratch,
    )
    nbytes = sum(a.size * a.dtype.itemsize for a in args) + sum(a.size * a.dtype.itemsize for a in outs)
    if scalars is not None:
        args = [scalars] + list(args)
    return pl.pallas_call(
        kernel,
        grid_spec=grid_spec,
        out_shape=outs,
        compiler_params=pltpu.CompilerParams(vmem_limit_bytes=58 << 20),
        cost_estimate=pl.CostEstimate(flops=flops, bytes_accessed=nbytes, transcendentals=0),
        name=name,
    )(*args)


def attend_kernel(causal, merge, parts, block, q_ref, bias_ref, *refs):
    key_refs, value_refs = refs[:parts], refs[parts : 2 * parts]
    refs = refs[2 * parts :]
    if merge:
        before_ref, e_ref, o_ref, own_ref, new_ref = refs
    elif parts > 1:
        e_ref, o_ref, own_ref = refs
    else:
        e_ref, o_ref = refs
    rows = q_ref.shape[0]
    pairs = q_ref.shape[1] // 128
    lane_b = lane_of((block, 128))
    first = head_lanes(lane_b, 0)
    full = (block, 128)
    items = [(p, b, half) for p in range(pairs) for b in range(rows // block) for half in range(2)]
    kept = {}

    def reaches(b):
        offset, found = 0, []
        for i, k_ref in enumerate(key_refs):
            keys = k_ref.shape[0]
            seen = min(keys, (b + 1) * block) if causal and i == parts - 1 else keys
            found.append((offset, i, seen))
            offset += keys
        return found

    def scores(item):
        p, b, half = item
        lanes = slice(128 * p, 128 * p + 128)
        q = q_ref[b * block : (b + 1) * block, lanes] * lane_rows(half)[0]
        found = []
        for offset, i, seen in reaches(b):
            s = dot(q, key_refs[i][:seen, lanes], NT) + bias_ref[0:1, offset : offset + seen]
            if causal and i == parts - 1:
                row = lax.broadcasted_iota(jnp.int32, s.shape, 0) + b * block
                s = jnp.where(lane_of(s.shape) <= row, s, MASKED)
            found.append(s)
        return found

    def soften(item, found):
        p, b, half = item
        top = functools.reduce(jnp.maximum, [jnp.max(s, axis=1, keepdims=True) for s in found])
        es = []
        for (offset, i, seen), s in zip(reaches(b), found):
            e = jnp.exp2(s - top).astype(bf)
            e_ref[2 * p + half, b * block : (b + 1) * block, offset : offset + seen] = e
            es.append(e)
        return top, es

    def mix(item, top, es):
        p, b, half = item
        lanes = slice(128 * p, 128 * p + 128)
        at = slice(b * block, (b + 1) * block)
        inside, at0 = lane_rows(half)
        spare = 64 - 64 * half
        o = None
        for (offset, i, seen), e in zip(reaches(b), es):
            part = dot(e, value_refs[i][:seen, lanes] * inside + at0)
            o = part if o is None else o + part
        if not merge and parts == 1:
            o_ref[2 * p + half, at, :] = jnp.where(lane_b == spare + 1, top, o)
            return
        l_new = jnp.broadcast_to(o[:, spare : spare + 1], full)
        if merge:
            old = before_ref[2 * p + half, at, :]
            l_old = jnp.broadcast_to(old[:, spare : spare + 1], full)
            m_old = jnp.broadcast_to(old[:, spare + 1 : spare + 2], full)
            top = jnp.broadcast_to(top, full)
            m = jnp.maximum(m_old, top)
            w_old, w_new = jnp.exp2(m_old - m), jnp.exp2(top - m)
            turn = 1.0 / (l_old * w_old + l_new * w_new)
            f_old, f_new = w_old * turn, w_new * turn
            o = old * f_old + o * f_new
        else:
            f_old = f_new = 1.0 / l_new
            o = o * f_new
        if half == 0:
            kept[p, b] = (o, f_old, f_new)
        else:
            o0, old0, new0 = kept.pop((p, b))
            o_ref[at, lanes] = jnp.where(first, o0, o).astype(bf)
            own_ref[at, lanes] = jnp.where(first, old0, f_old)
            if merge:
                new_ref[at, lanes] = jnp.where(first, new0, f_new)

    s = scores(items[0])
    waiting = None
    for i, item in enumerate(items):
        following = scores(items[i + 1]) if i + 1 < len(items) else None
        if waiting is not None:
            mix(*waiting)
        top, es = soften(item, s)
        waiting = (item, top, es)
        s = following
    mix(*waiting)


def attend(q, keys, values, bias, causal=False, before=None, block=256, group=1):
    rows, width = q.shape
    pairs = width // 128
    merge = before is not None
    total = sum(k.shape[0] for k in keys)

    def column(a):
        return pl.BlockSpec((a.shape[0], 128 * group), lambda p: (0, p))

    tall = column(q)
    e_spec = pl.BlockSpec((2 * group, rows, total), lambda p: (p, 0, 0))
    o_spec = pl.BlockSpec((2 * group, rows, 128), lambda p: (p, 0, 0))
    outs, out_specs = [shape_of((2 * pairs, rows, total))], [e_spec]
    args = [q, bias, *keys, *values]
    in_specs = [tall, None] + [column(a) for a in args[2:]]
    if merge:
        args.append(before)
        in_specs.append(o_spec)
    if merge or len(keys) > 1:
        outs += [shape_of((rows, width))] + [shape_of((rows, width), f32)] * (2 if merge else 1)
        out_specs += [tall] * (3 if merge else 2)
    else:
        outs.append(shape_of((2 * pairs, rows, 128), f32))
        out_specs.append(o_spec)
    return call(
        functools.partial(attend_kernel, causal, merge, len(keys), block),
        args,
        outs,
        (pairs // group,),
        in_specs,
        out_specs,
        flops=16 * rows * total * width,
        name="attend",
    )


def attend_back_kernel(causal, last, parts, block, e_ref, do_ref, o_ref, f_ref, q_ref, *refs):
    key_refs, value_refs = refs[:parts], refs[parts : 2 * parts]
    refs = refs[2 * parts :]
    if last:
        before_ref, dq_ref, d_ref = refs
    elif len(refs) == 2:
        dq_ref, d_ref = refs
    else:
        dq_ref, d_ref = None, refs[0]
    base = d_ref.shape[0] - 2
    rows = q_ref.shape[0]
    pairs = q_ref.shape[1] // 128
    lane_b = lane_of((block, 128))
    items = [(p, half, b) for p in range(pairs) for half in range(2) for b in range(rows // block)]
    dq, dk, dv = {}, {}, {}

    def reaches(b):
        offset, found = 0, []
        for i, k_ref in enumerate(key_refs):
            keys = k_ref.shape[0]
            seen = min(keys, (b + 1) * block) if causal and i == parts - 1 else keys
            found.append((offset, i, seen))
            offset += keys
        return found

    def slopes(item):
        p, half, b = item
        lanes = slice(128 * p, 128 * p + 128)
        at = slice(b * block, (b + 1) * block)
        inb = head_lanes(lane_b, half)
        do = do_ref[at, lanes].astype(f32)
        f = f_ref[at, lanes]
        inner = jnp.sum(jnp.where(inb, do * o_ref[at, lanes].astype(f32), 0.0), axis=1, keepdims=True)
        off = inner * f[:, 64 * half : 64 * half + 1]
        dos = jnp.where(inb, do * f, 0.0).astype(bf)
        return dos, off, [dot(dos, value_refs[i][:seen, lanes], NT) for offset, i, seen in reaches(b)]

    def spread(item, dos, off, dps):
        p, half, b = item
        lanes = slice(128 * p, 128 * p + 128)
        at = slice(b * block, (b + 1) * block)
        q = q_ref[at, lanes]
        for (offset, i, seen), dp in zip(reaches(b), dps):
            e = e_ref[2 * p + half, at, offset : offset + seen]
            ds = (e.astype(f32) * (dp - off)).astype(bf)
            part = dot(ds, key_refs[i][:seen, lanes] * lane_rows(half)[0])
            dq[p, b] = part if (p, b) not in dq else dq[p, b] + part
            step = block if causal and i == parts - 1 else seen
            for c in range(0, seen, step):
                key = (p, half, offset + c)
                vt = dot(dos, e[:, c : c + step], TN)
                kt = dot(q, ds[:, c : c + step], TN)
                dv[key] = vt if key not in dv else dv[key] + vt
                dk[key] = kt if key not in dk else dk[key] + kt

    ready = slopes(items[0])
    for i, item in enumerate(items):
        following = slopes(items[i + 1]) if i + 1 < len(items) else None
        spread(item, *ready)
        ready = following
    for p, b in dq:
        lanes = slice(128 * p, 128 * p + 128)
        at = slice(b * block, (b + 1) * block)
        part = dq[p, b]
        if last:
            dq_ref[at, lanes] = ((part + before_ref[at, lanes]) * 0.125).astype(bf)
        elif base == 0:
            dq_ref[at, lanes] = part
        else:
            d_ref[0, lanes, d_ref.shape[2] - rows + b * block : d_ref.shape[2] - rows + (b + 1) * block] = (
                part.T * 0.125
            ).astype(bf)
    for p, half, c in dk:
        wide = dk[p, half, c].shape[1]
        inside = slice(64 * half, 64 * half + 64)
        at = slice(128 * p + 64 * half, 128 * p + 64 * half + 64)
        d_ref[base, at, c : c + wide] = (dk[p, half, c][inside] * LN2).astype(bf)
        d_ref[base + 1, at, c : c + wide] = dv[p, half, c][inside].astype(bf)


def attend_back(e, do, o, f, q, keys, values, causal=False, before=None, whole=False, block=256, group=1):
    rows, width = q.shape
    pairs = width // 128
    total = sum(k.shape[0] for k in keys)

    def column(a):
        return pl.BlockSpec((a.shape[0], 128 * group), lambda p: (0, p))

    tall = column(q)
    args = [e, do, o, f, q, *keys, *values]
    in_specs = [pl.BlockSpec((2 * group, rows, total), lambda p: (p, 0, 0))] + [column(a) for a in args[1:]]
    if before is not None:
        args.append(before)
        in_specs.append(tall)
    return call(
        functools.partial(attend_back_kernel, causal, before is not None, len(keys), block),
        args,
        ([] if whole else [shape_of((rows, width), f32 if before is None else bf)])
        + [shape_of((2 + whole, width, total))],
        (pairs // group,),
        in_specs,
        ([] if whole else [tall]) + [pl.BlockSpec((2 + whole, 128 * group, total), lambda p: (0, p, 0))],
        flops=16 * rows * total * width,
        name="attend_back",
    )


def late(refs, buffers, sems):
    copies = [pltpu.make_async_copy(ref, buffer, sems.at[i]) for i, (ref, buffer) in enumerate(zip(refs, buffers))]

    @pl.when(pl.program_id(0) == 0)
    def _():
        for copy in copies:
            copy.start()

    def fetch(i):
        copies[i].wait()
        return buffers[i]

    return fetch


def self_back(e, do, o, f, q, keys, values, far_first, first, wk, wv):
    rows, width = q.shape
    pairs = width // 128
    total = 2 * rows
    half = width // 2
    back = functools.partial(attend_back_kernel, True, False, 2, 256)

    def kernel(core_ref, *refs):
        blocks, (ff_ref, first_ref, wk_ref, wv_ref) = refs[:9], refs[9:13]
        d_ref, *send_refs, keep_ref, out_ref = refs[13:19]
        all_ref, part_ref, *buffers, sems = refs[19:]
        fetch = late([ff_ref, first_ref, wk_ref, wv_ref], buffers, sems)
        i = pl.program_id(0)
        core = core_ref[0]

        @pl.when(i < pairs)
        def _():
            back(*blocks, part_ref)
            d_ref[...] = part_ref[:, :, rows:]
            all_ref[:, pl.ds(pl.multiple_of(i * 128, 128), 128), :] = part_ref[...]

        @pl.when(i == pairs)
        def _():
            far, own = fetch(0)[...], fetch(1)[...]
            query = dot(own, all_ref[0, :, rows:], TT)
            key = dot(far, all_ref[1, :, :rows], TT) + dot(own, all_ref[1, :, rows:], TT)
            halves(send_refs, keep_ref, core, 0, query, key)

        @pl.when(i == pairs + 1)
        def _():
            far, own = buffers[0][...], buffers[1][...]
            value = dot(far, all_ref[2, :, :rows], TT) + dot(own, all_ref[2, :, rows:], TT)
            halves(send_refs, keep_ref, core, width, value[:, :half], value[:, half:])
            grad = dot(all_ref[1, :, :rows], fetch(2)[...], TT) + dot(all_ref[2, :, :rows], fetch(3)[...], TT)
            out_ref[...] = grad.astype(bf)

    def column(a):
        return pl.BlockSpec((a.shape[0], 128), lambda i, s: (0, jnp.minimum(i, pairs - 1)))

    args = [e, do, o, f, q, *keys, *values, far_first, first, wk, wv]
    in_specs = [pl.BlockSpec((2, rows, total), lambda i, s: (jnp.minimum(i, pairs - 1), 0, 0))]
    in_specs += [column(a) for a in args[1:9]] + [pl.BlockSpec(memory_space=pl.ANY)] * 4
    own = pl.BlockSpec((3, 128, rows), lambda i, s: (0, jnp.minimum(i, pairs - 1), 0))
    return call(
        kernel,
        args,
        [shape_of((3, width, rows))]
        + [shape_of((width, half))] * 3
        + [shape_of((width, width + half)), shape_of((rows, width))],
        (pairs + 2,),
        in_specs,
        [own] + [None] * 5,
        core_scalar(),
        scratch=[pltpu.VMEM((3, width, total), bf), pltpu.VMEM((3, 128, total), bf)]
        + [pltpu.VMEM(a.shape, bf) for a in args[9:]]
        + [pltpu.SemaphoreType.DMA((4,))],
        flops=16 * rows * total * width + 12 * rows * width * width,
        name="self_back",
    )


def cross_back_far(e, do, o, f, q, k, v, wk, wv):
    rows, width = q.shape
    pairs = width // 128
    keys = k.shape[0]
    half = keys // 2

    def kernel(*refs):
        blocks, (wk_ref, wv_ref), (dq_ref, d_ref, low_ref, high_ref) = refs[:7], refs[7:9], refs[9:13]
        all_ref, *buffers, sems = refs[13:]
        fetch = late([wk_ref, wv_ref], buffers, sems)
        i = pl.program_id(0)

        @pl.when(i < pairs)
        def _():
            attend_back_kernel(False, False, 1, 256, *blocks, dq_ref, d_ref)
            all_ref[:, pl.ds(pl.multiple_of(i * 128, 128), 128), :] = d_ref[...]

        @pl.when(i == pairs)
        def _():
            fetch(0), fetch(1)

        @pl.when(i >= pairs)
        def _():
            at = pl.ds(pl.multiple_of((i - pairs) * half, half), half)
            grad = dot(all_ref[0, :, at], buffers[0][...], TT) + dot(all_ref[1, :, at], buffers[1][...], TT)
            grad = grad.astype(bf)

            @pl.when(i == pairs)
            def _():
                low_ref[...] = grad

            @pl.when(i > pairs)
            def _():
                high_ref[...] = grad

    def spot(i):
        return jnp.minimum(i, pairs - 1)

    def column(a):
        return pl.BlockSpec((a.shape[0], 128), lambda i: (0, spot(i)))

    args = [e, do, o, f, q, k, v, wk, wv]
    part = shape_of((half, width))
    return call(
        kernel,
        args,
        [shape_of((rows, width), f32), shape_of((2, width, keys)), part, part],
        (pairs + 2,),
        [pl.BlockSpec((2, rows, keys), lambda i: (spot(i), 0, 0))] + [column(a) for a in args[1:7]] + [ANY] * 2,
        [column(q), pl.BlockSpec((2, 128, keys), lambda i: (0, spot(i), 0)), None, None],
        scratch=[pltpu.VMEM((2, width, keys), bf)] + [pltpu.VMEM(wk.shape, bf)] * 2 + [pltpu.SemaphoreType.DMA((2,))],
        flops=16 * rows * keys * width + 4 * keys * width * width,
        name="cross_back_far",
    )


def cross_back_own(e, do, o, f, q, k, v, before, gain, wq, y1, dy2, wo, patches, far_patches, far_d, second, b2, o1):
    rows, width = q.shape
    pairs = width // 128
    keys = k.shape[0]
    half = width // 2
    chunk = 512
    parts = keys // chunk

    def kernel(core_ref, *refs):
        blocks, gain_ref, late_refs = refs[:8], refs[8], refs[9:20]
        d_ref, dy1_ref, do1_ref, *send_refs, keep_ref = refs[20:29]
        all_ref, dq_ref, acc_ref, b1_ref, *buffers, sems = refs[29:]
        fetch = late(late_refs, buffers, sems)
        i = pl.program_id(0)
        core = core_ref[0]

        @pl.when(i < pairs)
        def _():
            at = pl.ds(pl.multiple_of(i * 128, 128), 128)
            attend_back_kernel(False, True, 1, 256, *blocks, dq_ref.at[:, at], d_ref)
            all_ref[:, at, :] = d_ref[...]

        @pl.when(i == pairs)
        def _():
            for j in range(11):
                fetch(j)
            grad = dot(dq_ref[...], buffers[0][...], NT)
            unit, scale = norm_parts(buffers[1][...])
            dy1 = buffers[2][...] + norm_back(unit, scale, gain_ref[...], grad)
            dy1_ref[...] = dy1
            b1_ref[...] = dy1.astype(bf)
            do1_ref[...] = dot(b1_ref[...], buffers[3][...], NT).astype(bf)
            acc_ref[...] = jnp.zeros_like(acc_ref)

        @pl.when((i > pairs) & (i <= pairs + parts))
        def _():
            at = pl.ds(pl.multiple_of((i - pairs - 1) * chunk, chunk), chunk)
            left, far = buffers[4][at, :], buffers[5][at, :]
            for j in range(2):
                acc_ref[j] += dot(left, all_ref[j, :, at], TT) + dot(far, buffers[6][j, :, at], TT)

        @pl.when(i == pairs + parts + 1)
        def _():
            halves(send_refs, keep_ref, core, 0, acc_ref[0], acc_ref[1])
            query, output = dot(buffers[7][...], dq_ref[...], TN), dot(buffers[10][...], buffers[8][...], TN)
            halves(send_refs, keep_ref, core, width, query, output)
            value = dot(buffers[9][...], b1_ref[...], TN)
            halves(send_refs, keep_ref, core, 2 * width, value[:, :half], value[:, half:])

    def spot(i):
        return jnp.minimum(i, pairs - 1)

    def column(a):
        return pl.BlockSpec((a.shape[0], 128), lambda i, s: (0, spot(i)))

    lates = [wq, y1, dy2, wo, patches, far_patches, far_d, second, b2, o1, o]
    args = [e, do, o, f, q, k, v, before, gain] + lates
    full = shape_of((rows, width), f32)
    return call(
        kernel,
        args,
        [shape_of((2, width, keys)), full, shape_of((rows, width))]
        + [shape_of((width, half))] * 5
        + [shape_of((width, 2 * width + half))],
        (pairs + parts + 2,),
        [pl.BlockSpec((2, rows, keys), lambda i, s: (spot(i), 0, 0))]
        + [column(a) for a in args[1:8]]
        + [None]
        + [ANY] * 11,
        [pl.BlockSpec((2, 128, keys), lambda i, s: (0, spot(i), 0))] + [None] * 8,
        core_scalar(),
        scratch=[
            pltpu.VMEM((2, width, keys), bf),
            pltpu.VMEM((rows, width), bf),
            pltpu.VMEM((2, width, width), f32),
            pltpu.VMEM((rows, width), bf),
        ]
        + [pltpu.VMEM(a.shape, a.dtype) for a in lates]
        + [pltpu.SemaphoreType.DMA((11,))],
        flops=16 * rows * keys * width + 2 * width * width * (5 * rows + 4 * keys),
        name="cross_back_own",
    )


def norm_parts(value):
    scale = lax.rsqrt(jnp.mean(value * value, axis=-1, keepdims=True) + eps)
    return value * scale, scale


def norm_back(unit, scale, gain, grad):
    inner = gain * grad
    return scale * (inner - unit * jnp.mean(inner * unit, axis=-1, keepdims=True))


def gelu_parts(u):
    t = jnp.tanh(0.7978845608028654 * (u + 0.044715 * u * u * u))
    value = 0.5 * u * (1.0 + t)
    slope = 0.5 * (1.0 + t) + 0.5 * u * (1.0 - t * t) * (0.7978845608028654 * (1.0 + 3 * 0.044715 * u * u))
    return value, slope


def start(x, gain, patches, weights, scale):
    def kernel(gain_ref, x_ref, w0, w1, w2, p_ref, w3, w4, *refs):
        outs, refs = refs[:6], refs[6:]
        ins, results, in_sems, out_sems = refs[:7], refs[7:13], refs[13], refs[14]
        loads = [
            pltpu.make_async_copy(ref, buffer, in_sems.at[i])
            for i, (ref, buffer) in enumerate(zip((x_ref, w0, w1, w2, p_ref, w3, w4), ins))
        ]
        stores = [
            pltpu.make_async_copy(buffer, ref, out_sems.at[i]) for i, (buffer, ref) in enumerate(zip(results, outs))
        ]
        loads[0].start()
        loads[1].start()
        loads[0].wait()
        for load in loads[2:]:
            load.start()
        first = (norm_parts(ins[0][...].astype(f32))[0] * gain_ref[...]).astype(bf)
        results[0][...] = first
        stores[0].start()
        for j in range(3):
            loads[1 + j].wait()
            value = dot(results[0][...], ins[1 + j][...])
            results[1 + j][...] = (value * scale if j == 0 else value).astype(bf)
            stores[1 + j].start()
        loads[4].wait()
        for j in range(2):
            loads[5 + j].wait()
            results[4 + j][...] = dot(ins[4][...], ins[5 + j][...]).astype(bf)
            stores[4 + j].start()
        for store in stores:
            store.wait()

    args = [gain, x, *weights[:3], patches, *weights[3:]]
    outs = [shape_of(x.shape)] * 4 + [shape_of(patches.shape)] * 2
    return call(
        kernel,
        args,
        outs,
        in_specs=[None] + [ANY] * 7,
        out_specs=[ANY] * 6,
        scratch=[pltpu.VMEM(a.shape, bf) for a in args[1:] + outs]
        + [pltpu.SemaphoreType.DMA((7,)), pltpu.SemaphoreType.DMA((6,))],
        flops=2 * 768 * (3 * x.size + 2 * patches.size),
        name="start",
    )


def self_forward(q, k, v, bias, far_x, gain, wk, wv, x, w_out, next_gain, w_query, scale):
    rows, width = q.shape
    pairs = width // 128
    total = 2 * rows

    def kernel(q_ref, k_ref, v_ref, bias_ref, fx_ref, gain_ref, wk_ref, wv_ref, ng_ref, x_ref, wo_ref, wq_ref, *refs):
        e_ref, f_ref, o_ref, y_ref, n_ref, q2_ref, *far_out = refs[:9]
        far_first, far_k, far_v, *buffers, sems, out_sems = refs[9:]
        fetch = late([x_ref, wo_ref, wq_ref], buffers, sems)
        stores = [
            pltpu.make_async_copy(buffer, ref, out_sems.at[j])
            for j, (buffer, ref) in enumerate(zip((far_first, far_k, far_v), far_out))
        ]
        i = pl.program_id(0)

        @pl.when(i == 0)
        def _():
            far_first[...] = (norm_parts(fx_ref[...].astype(f32))[0] * gain_ref[...]).astype(bf)
            far_k[...] = dot(far_first[...], wk_ref[...]).astype(bf)
            far_v[...] = dot(far_first[...], wv_ref[...]).astype(bf)
            for store in stores:
                store.start()

        @pl.when((i > 0) & (i <= pairs))
        def _():
            at = pl.ds(pl.multiple_of((i - 1) * 128, 128), 128)
            refs = far_k.at[:, at], k_ref, far_v.at[:, at], v_ref
            attend_kernel(True, False, 2, 256, q_ref, bias_ref, *refs, e_ref, o_ref.at[:, at], f_ref)

        @pl.when(i == pairs + 1)
        def _():
            y = fetch(0)[...].astype(f32) + dot(o_ref[...], fetch(1)[...])
            y_ref[...] = y
            n_ref[...] = (norm_parts(y)[0] * ng_ref[...]).astype(bf)
            q2_ref[...] = (dot(n_ref[...], fetch(2)[...]) * scale).astype(bf)
            for store in stores:
                store.wait()

    def spot(i):
        return jnp.clip(i - 1, 0, pairs - 1)

    column = pl.BlockSpec((rows, 128), lambda i: (0, spot(i)))
    args = [q, k, v, bias, far_x, gain, wk, wv, next_gain, x, w_out, w_query]
    flat = shape_of((rows, width))
    return call(
        kernel,
        args,
        [shape_of((2 * pairs, rows, total)), shape_of((rows, width), f32), flat, shape_of((rows, width), f32)]
        + [flat] * 5,
        (pairs + 2,),
        [column] * 3 + [None] * 6 + [ANY] * 3,
        [pl.BlockSpec((2, rows, total), lambda i: (spot(i), 0, 0)), column] + [None] * 4 + [ANY] * 3,
        scratch=[pltpu.VMEM((rows, width), bf)] * 3
        + [pltpu.VMEM(a.shape, bf) for a in args[9:]]
        + [pltpu.SemaphoreType.DMA((3,)), pltpu.SemaphoreType.DMA((3,))],
        flops=16 * rows * total * width + 8 * rows * width * width,
        name="self_forward",
    )


def cross_forward(q, patches, wk, wv, bias, before, y1, w_out, gain, w_gate, w_up, w_down, dy):
    total, inner, outer, *_ = places()
    groups = inner * outer
    rows, width = q.shape
    keys = patches.shape[0]
    pairs = width // 128
    hidden = w_gate.shape[1]
    share, lanes = width // groups, hidden // groups
    blocks, step = hidden // lanes, 512
    per, chunks = step // lanes, hidden // step
    half = width // 2
    grouped = lanes % 128 == 0 and share % 16 == 0

    def kernel(core_ref, q_ref, bias_ref, before_ref, gain_ref, p_ref, wk_ref, wv_ref, *refs):
        late_refs, refs = refs[:6], refs[6:]
        e_ref, own_ref, new_ref, o_ref, y2_ref, third_ref, h_ref, d_ref, *outs = refs[:12]
        k_ref, v_ref, send_ref, keep_ref, *buffers, sems, out_sems = refs[12:]
        fetch = late(late_refs, buffers, sems)
        stores = [
            pltpu.make_async_copy(buffer, ref, out_sems.at[j])
            for j, (buffer, ref) in enumerate(zip((k_ref, v_ref, send_ref, keep_ref), outs))
        ]
        i = pl.program_id(0)
        here = core_ref[0] == 0

        @pl.when(i == 0)
        def _():
            k_ref[...] = dot(p_ref[...], wk_ref[...]).astype(bf)
            v_ref[...] = dot(p_ref[...], wv_ref[...]).astype(bf)
            stores[0].start()
            stores[1].start()

        @pl.when((i > 0) & (i <= pairs))
        def _():
            at = pl.ds(pl.multiple_of((i - 1) * 128, 128), 128)
            refs = k_ref.at[:, at], v_ref.at[:, at], before_ref, e_ref, o_ref.at[:, at], own_ref, new_ref
            attend_kernel(False, True, 1, rows, q_ref, bias_ref, *refs)

        @pl.when(i == pairs + 1)
        def _():
            y2 = fetch(0)[...] + dot(o_ref[...], fetch(1)[...])
            y2_ref[...] = y2
            third_ref[...] = (norm_parts(y2)[0] * gain_ref[...]).astype(bf)
            for j in range(2, 6):
                fetch(j)

        @pl.when(i > pairs)
        def _():
            c = i - pairs - 1
            at = pl.ds(pl.multiple_of(c * step, step), step)
            wg_ref, wu_ref, wd_ref, dy_ref = buffers[2:]
            low = rows // 2

            @pl.loop(0, 2)
            def _(r):
                part = pl.ds(pl.multiple_of(r * low, low), low)
                third = third_ref[part, :]
                gate = dot(third, wg_ref[:, at])
                up = dot(third, wu_ref[:, at])
                dhidden = dot(dy_ref[part, :], wd_ref[at, :], NT)
                act, slope = gelu_parts(gate)
                h_ref[part, :] = (act * up).astype(bf)
                d_ref[0, part, :] = (dhidden * up * slope).astype(bf)
                d_ref[1, part, :] = (dhidden * act).astype(bf)

            third = third_ref[...]
            gate, up = dot(third, d_ref[0], TN), dot(third, d_ref[1], TN)
            send, keep = jnp.where(here, up, gate).astype(bf), jnp.where(here, gate, up).astype(bf)
            for g in range(groups if grouped else 0):
                from_rows = slice(g * share, (g + 1) * share)
                for j in range(per):
                    to = pl.ds(pl.multiple_of((c * per + j) * share, share), share)
                    send_ref[g, to, :] = send[from_rows, j * lanes : (j + 1) * lanes]
                    keep_ref[g, to, :] = keep[from_rows, j * lanes : (j + 1) * lanes]
            if not grouped:
                send_ref[:width, at] = send
                keep_ref[:width, at] = keep
            down = dot(dy_ref[...], h_ref[...], TN)
            send, keep = jnp.where(here, down[half:], down[:half]), jnp.where(here, down[:half], down[half:])
            if not grouped:
                send_ref[width:, at] = send.astype(bf)
                keep_ref[width:, at] = keep.astype(bf)
            to = slice(blocks * share, blocks * share + half)
            for j in range(per if grouped else 0):
                send_ref[c * per + j, to, :] = send[:, j * lanes : (j + 1) * lanes].astype(bf)
                keep_ref[c * per + j, to, :] = keep[:, j * lanes : (j + 1) * lanes].astype(bf)

        @pl.when(i == pairs + chunks)
        def _():
            stores[2].start()
            stores[3].start()
            for store in stores:
                store.wait()

    def spot(i):
        return jnp.clip(i - 1, 0, pairs - 1)

    def chunk(i):
        return jnp.clip(i - 1 - pairs, 0, chunks - 1)

    column = pl.BlockSpec((rows, 128), lambda i, s: (0, spot(i)))
    args = [q, bias, before, gain, patches, wk, wv, y1, w_out, w_gate, w_up, w_down, dy]
    flat, key, full = shape_of((rows, width)), shape_of((keys, width)), shape_of((rows, width), f32)
    grads = shape_of((groups, blocks * share + half, lanes) if grouped else (width + half, hidden))
    *outs, send, keep = call(
        kernel,
        args,
        [shape_of((2 * pairs, rows, keys)), full, full, flat, full, flat]
        + [shape_of((rows, hidden)), shape_of((2, rows, hidden)), key, key, grads, grads],
        (pairs + 1 + chunks,),
        [column, None, pl.BlockSpec((2, rows, 128), lambda i, s: (spot(i), 0, 0))] + [None] * 4 + [ANY] * 6,
        [pl.BlockSpec((2, rows, keys), lambda i, s: (spot(i), 0, 0)), column, column, None, None, None]
        + [pl.BlockSpec((rows, step), lambda i, s: (0, chunk(i)))]
        + [pl.BlockSpec((2, rows, step), lambda i, s: (0, 0, chunk(i)))]
        + [ANY] * 4,
        core_scalar(),
        scratch=[pltpu.VMEM(a.shape, bf) for a in (key, key, grads, grads)]
        + [pltpu.VMEM(a.shape, a.dtype) for a in args[7:]]
        + [pltpu.SemaphoreType.DMA((6,)), pltpu.SemaphoreType.DMA((4,))],
        flops=16 * rows * keys * width + 4 * keys * width * width + 12 * rows * width * hidden,
        name="cross_forward",
    )

    def group(value):
        if grouped:
            return value
        gate = value[:width].reshape(groups, share, blocks, lanes).swapaxes(1, 2).reshape(groups, -1, lanes)
        return jnp.concatenate([gate, value[width:].reshape(half, groups, lanes).swapaxes(0, 1)], 1)

    return *outs, group(send), group(keep)


def feed_back(d, w_gate, w_up, y2, gain, dy, w_out):
    def kernel(d_ref, wg_ref, wu_ref, gain_ref, y2_ref, dy_ref, wo_ref, dy2_ref, b_ref, do_ref, acc_ref, *refs):
        *buffers, sems = refs
        fetch = late([y2_ref, dy_ref, wo_ref], buffers, sems)
        i = pl.program_id(0)
        part = dot(d_ref[0], wg_ref[...], NT) + dot(d_ref[1], wu_ref[...], NT)

        @pl.when(i == 0)
        def _():
            acc_ref[...] = part

        @pl.when(i > 0)
        def _():
            acc_ref[...] += part

        @pl.when(i == pl.num_programs(0) - 1)
        def _():
            grad = acc_ref[...]
            unit, scale = norm_parts(fetch(0)[...])
            dy2 = fetch(1)[...].astype(f32) + norm_back(unit, scale, gain_ref[...], grad)
            dy2_ref[...] = dy2
            b_ref[...] = dy2.astype(bf)
            do_ref[...] = dot(b_ref[...], fetch(2)[...], NT).astype(bf)

    rows, width = y2.shape
    hidden = w_gate.shape[1]
    column = pl.BlockSpec((width, 512), lambda i: (0, i))
    return call(
        kernel,
        [d, w_gate, w_up, gain, y2, dy, w_out],
        [shape_of(y2.shape, f32), shape_of(y2.shape), shape_of(y2.shape)],
        (hidden // 512,),
        [pl.BlockSpec((2, rows, 512), lambda i: (0, 0, i)), column, column, None, ANY, ANY, ANY],
        scratch=[pltpu.VMEM((rows, width), f32)]
        + [pltpu.VMEM(a.shape, a.dtype) for a in (y2, dy, w_out)]
        + [pltpu.SemaphoreType.DMA((3,))],
        flops=2 * y2.size * (768 + 2 * hidden),
        name="feed_back",
    )


def finish(d, wq, wk, wv, near, x, gain, dy1):
    def kernel(d_ref, wq_ref, wk_ref, wv_ref, near_ref, x_ref, gain_ref, dy_ref, out_ref):
        grad = near_ref[...].astype(f32)
        for j, w_ref in enumerate((wq_ref, wk_ref, wv_ref)):
            grad = grad + dot(d_ref[j], w_ref[...], TT)
        unit, scale = norm_parts(x_ref[...].astype(f32))
        out_ref[...] = (dy_ref[...] + norm_back(unit, scale, gain_ref[...], grad)).astype(bf)

    rows = x.shape[0]
    return call(
        kernel, [d, wq, wk, wv, near, x, gain, dy1], [shape_of(x.shape)], (1,),
        flops=6 * x.size * 768, name="finish",
    )[0]


def output(y2, hidden, w_down):
    def kernel(y_ref, h_ref, w_ref, out_ref):
        out_ref[...] = (y_ref[...] + dot(h_ref[...], w_ref[...])).astype(bf)

    rows, width = y2.shape
    half = pl.BlockSpec((rows, width // 2), lambda i: (0, i))
    return call(
        kernel, [y2, hidden, w_down], [shape_of(y2.shape)], (2,),
        [half, None, pl.BlockSpec((hidden.shape[1], width // 2), lambda i: (0, i))], [half],
        flops=2 * hidden.size * width, name="output",
    )[0]


def key_value_back(d, wk, wv, near=()):
    keys = d.shape[2]
    half = keys // 2

    def kernel(d_ref, wk_ref, wv_ref, *refs):
        grad = dot(d_ref[0], wk_ref[...], TT) + dot(d_ref[1], wv_ref[...], TT)
        if near:
            refs[2][...] = (grad + jnp.where(pl.program_id(0) == 0, refs[0][...], refs[1][...]).astype(f32)).astype(bf)
            return
        for i in range(2):

            @pl.when(pl.program_id(0) == i)
            def _(i=i):
                refs[i][...] = grad.astype(bf)

    rows = pl.BlockSpec((half, wk.shape[0]), lambda i: (i, 0))
    part = pl.BlockSpec((2, d.shape[1], half), lambda i: (0, 0, i))
    shape = (half, wk.shape[0])
    out = call(
        kernel,
        [d, wk, wv, *near],
        [shape_of((keys, wk.shape[0]))] if near else [shape_of(shape)] * 2,
        (2,),
        [part] + [None] * (2 + len(near)),
        [rows] if near else None,
        flops=4 * keys * 768 * 768,
        name="key_value_back",
    )
    return out[0] if near else out


def ring_factors(groups):
    inner = 1
    while inner * inner * 4 <= groups:
        inner *= 2
    return inner, groups // inner


def places():
    total = lax.axis_size("plots")
    index = lax.axis_index("plots")
    inner, outer = ring_factors(total // 2)
    group = index // 2
    return total, inner, outer, group // inner, group % inner, index % 2


def core_swap(value):
    total = lax.axis_size("plots")
    return lax.ppermute(value, "plots", [(i, i ^ 1) for i in range(total)])


def outer_shift(value, k):
    total, inner, outer, *_ = places()
    stride = 2 * inner
    return lax.ppermute(value, "plots", [(i, ((i // stride + k) % outer) * stride + i % stride) for i in range(total)])


def inner_shift(value, k):
    total, inner, outer, *_ = places()

    def spot(i):
        y = (i // 2) % inner
        return i + ((y + k) % inner - y) * 2

    return lax.ppermute(value, "plots", [(i, spot(i)) for i in range(total)])


def hold(value, *tokens):
    return lax.optimization_barrier((value,) + tokens)[0]


def halves(send_refs, keep_ref, core, start, one, two):
    here = core == 0
    send = jnp.where(here, two, one).astype(bf)
    keep_ref[:, start : start + one.shape[1]] = jnp.where(here, one, two).astype(bf)
    wide = send_refs[0].shape[1]
    for c in range(0, one.shape[1], wide):
        send_refs[(start + c) // wide][...] = send[:, c : c + wide]


def core_scalar():
    return (lax.axis_index("plots") % 2).astype(jnp.int32)[None]


def combine(keep, pieces, spot):
    outer, inner, share, columns = keep.shape

    def kernel(y_ref, keep_ref, *refs):
        *piece_refs, mine_ref, send_ref = refs
        y = y_ref[0]

        @pl.loop(0, outer // steps)
        def _(i):
            start = 0
            for ref in piece_refs:
                at = slice(start, start + ref.shape[3])
                start += ref.shape[3]
                one = keep_ref[i, 0, :, at].astype(f32) + ref[i, 0].astype(f32)
                two = keep_ref[i, 1, :, at].astype(f32) + ref[i, 1].astype(f32)
                mine_ref[i, :, at] = jnp.where(y == 0, one, two).astype(bf)
                send_ref[i, :, at] = jnp.where(y == 0, two, one).astype(bf)

    steps = 2

    def block(a):
        return pl.BlockSpec((outer // steps,) + a.shape[1:], lambda i, s: (i,) + (0,) * (len(a.shape) - 1))

    args = [keep] + [p.reshape(outer, inner, share, p.shape[1]) for p in pieces]
    out = shape_of((outer, share, columns))
    return call(
        kernel, args, [out, out], (steps,), [block(a) for a in args], [block(out)] * 2,
        spot.astype(jnp.int32)[None], name="combine",
    )


class Sum:
    def __init__(self, sends, keep):
        self.token = sends[-1]
        self.mine = keep
        self.got = [core_swap(send) for send in sends]

    def inner_step(self, *tokens):
        total, inner, outer, z, y, core = places()
        split = (outer, inner, self.mine.shape[0] // (outer * inner), self.mine.shape[1])
        mine = self.mine.reshape(split)
        got = lax.optimization_barrier(tuple(self.got) + tokens)[: len(self.got)]
        if inner == 2:
            self.mine, self.token = combine(mine, got, y)
            self.got = lax.ppermute(self.token, "plots", [(i, i ^ 2) for i in range(total)])
        else:
            got = jnp.concatenate(got, 1).reshape(split)
            groups = [[(o * inner + i) * 2 + c for i in range(inner)] for o in range(outer) for c in range(2)]
            self.token = (mine.astype(f32) + got.astype(f32)).astype(bf)
            self.mine = None
            self.got = lax.all_to_all(self.token, "plots", 1, 1, axis_index_groups=groups, tiled=True)

    def outer_step(self, *tokens):
        total, inner, outer, z, y, core = places()
        got = hold(self.got, *tokens)

        def part(at):
            if self.mine is None:
                value = lax.dynamic_index_in_dim(got, at, 0, keepdims=False)
                return jnp.sum(value.astype(f32), axis=0).astype(bf)
            one = lax.dynamic_index_in_dim(self.mine, at, 0, keepdims=False)
            two = lax.dynamic_index_in_dim(got, at, 0, keepdims=False)
            return (one.astype(f32) + two.astype(f32)).astype(bf)

        self.parts = [part((z + k) % outer) for k in range(1, outer)]
        self.got = [outer_shift(value, k + 1) for k, value in enumerate(self.parts)]
        self.token = self.parts[-1]
        self.mine = part(z)

    def seq_step(self, *tokens):
        got = lax.optimization_barrier(tuple(self.got) + tokens)[: len(self.got)]
        self.mine = sum((g.astype(f32) for g in got), self.mine.astype(f32)).astype(bf)
        self.token = self.mine
        self.got = lax.ppermute(self.mine, "seq", SEQ_SWAP)

    def core_step(self, *tokens):
        core = lax.axis_index("plots") % 2
        value = self.mine.astype(f32) + hold(self.got, *tokens).astype(f32)
        value = value.reshape((2, value.shape[0] // 2) + value.shape[1:])
        self.mine = lax.dynamic_index_in_dim(value, core, 0, keepdims=False)
        self.token = lax.dynamic_index_in_dim(value, 1 - core, 0, keepdims=False).astype(bf)
        self.got = core_swap(self.token)

    def done(self):
        core = lax.axis_index("plots") % 2
        other = self.got.astype(f32)
        return jnp.where(core == 0, self.mine, other), jnp.where(core == 0, other, self.mine)


class SeqFirstSum(Sum):
    def seq_first_step(self, *tokens):
        total, inner, outer, *_ = places()
        split = (outer * inner, 2, self.mine.shape[0] // (outer * inner * 2), self.mine.shape[1])
        got = lax.optimization_barrier(tuple(self.got) + tokens)[: len(self.got)]
        self.mine, self.token = combine(self.mine.reshape(split), got, lax.axis_index("seq"))
        self.got = lax.ppermute(self.token, "seq", SEQ_SWAP)

    def inner_step(self, *tokens):
        total, inner, outer, z, y, core = places()
        split = (outer, inner) + self.mine.shape[1:]
        mine, got = self.mine.reshape(split), hold(self.got, *tokens).reshape(split)

        def part(at):
            one = lax.dynamic_index_in_dim(mine, at, 1, keepdims=False)
            two = lax.dynamic_index_in_dim(got, at, 1, keepdims=False)
            return (one.astype(f32) + two.astype(f32)).astype(bf)

        if inner == 2:
            self.token = part(1 - y)
            self.got = lax.ppermute(self.token, "plots", [(i, i ^ 2) for i in range(total)])
            self.mine = part(y)
        else:
            groups = [[(o * inner + i) * 2 + c for i in range(inner)] for o in range(outer) for c in range(2)]
            self.token = (mine.astype(f32) + got.astype(f32)).astype(bf)
            self.mine = None
            self.got = lax.all_to_all(self.token, "plots", 1, 1, axis_index_groups=groups, tiled=True)

    def core_step(self, *tokens):
        core = lax.axis_index("plots") % 2
        got = hold(self.got, *tokens)
        own = lax.axis_index("seq") == core
        self.token = jnp.where(own, got, self.mine)
        self.mine = jnp.where(own, self.mine, got)
        self.got = core_swap(self.token)


def weight_rows(*weights):
    share = weights[0].shape[0] // lax.axis_size("plots")
    at = lax.axis_index("plots") * share
    return jnp.concatenate([lax.dynamic_slice_in_dim(w, at, share, 0) for w in weights], 1)


def finalize(sums, widths, rows, picks, gain):
    share, columns = sums.mine.shape
    pairs = len(widths)
    half = columns - sum(widths)

    def kernel(core_ref, mine_ref, other_ref, rows_ref, gain_ref, *refs):
        here = core_ref[0] == 0
        mine, other = mine_ref[...].astype(f32), other_ref[...].astype(f32)
        one, two = jnp.where(here, mine, other), jnp.where(here, other, mine)
        start = 0
        for j, wide in enumerate(widths):
            refs[2 * j][...] = one[:, start : start + wide]
            refs[2 * j + 1][...] = two[:, start : start + wide]
            start += wide
        refs[2 * pairs][:, :half] = one[:, start:]
        refs[2 * pairs][:, half:] = two[:, start:]
        total, start = 0.0, 0
        for j in picks:
            value = refs[j][...]
            product = value * rows_ref[:, start : start + value.shape[1]].astype(f32)
            total = total + jnp.sum(product, axis=1, keepdims=True)
            start += value.shape[1]
        refs[-1][...] = total / gain_ref[...]

    outs = [shape_of((share, wide), f32) for wide in widths for _ in range(2)]
    outs += [shape_of((share, 2 * half), f32), shape_of((share, 1), f32)]
    args = [sums.mine, sums.got, rows, gain[:, None].astype(f32)]
    return call(kernel, args, outs, scalars=core_scalar(), name="finalize")


class FeedSum:
    def __init__(self, send, keep):
        self.token = send
        self.mine = keep
        self.got = core_swap(send)

    def group_step(self, *tokens):
        total, inner, outer, *_ = places()
        value = (self.mine.astype(f32) + hold(self.got, *tokens).astype(f32)).astype(bf)
        pairs = [[2 * g + c for g in range(inner * outer)] for c in range(2)]
        self.token = value
        self.got = lax.psum_scatter(value, "plots", scatter_dimension=0, axis_index_groups=pairs, tiled=True)

    def seq_step(self, *tokens):
        self.mine = hold(self.got, *tokens)[0]
        self.token = self.mine
        self.got = lax.ppermute(self.mine, "seq", SEQ_SWAP)

    def core_step(self, share, blocks, *tokens):
        core = lax.axis_index("plots") % 2
        value = self.mine.astype(f32) + hold(self.got, *tokens).astype(f32)
        lanes = value.shape[1]
        gate = value[: blocks * share].reshape(blocks, 2, share // 2, lanes).transpose(1, 2, 0, 3)
        gate = gate.reshape(2, share // 2, blocks * lanes)
        down = value[blocks * share :].T.reshape(2, lanes // 2, value.shape[0] - blocks * share)

        def trade(a):
            mine = lax.dynamic_index_in_dim(a, core, 0, keepdims=False)
            got = core_swap(lax.dynamic_index_in_dim(a, 1 - core, 0, keepdims=False).astype(bf)).astype(f32)
            return jnp.where(core == 0, mine, got), jnp.where(core == 0, got, mine)

        gate, up = trade(gate)
        return gate, up, jnp.concatenate(trade(down), 1)


def per_device(
    decoder_states,
    encoder_patches,
    token_lengths,
    patch_counts,
    self_gain,
    cross_gain,
    mlp_gain,
    self_query,
    self_key,
    self_value,
    self_output,
    cross_query,
    cross_key,
    cross_value,
    cross_output,
    mlp_gate,
    mlp_up,
    mlp_down,
    output_grad,
):
    plots, rows, width = decoder_states.shape
    assert plots == 1 and width == 64 * HEADS
    patch_rows = encoder_patches.shape[1]
    place = lax.axis_index("seq")
    token = jnp.arange(rows, dtype=jnp.int32)
    slot = jnp.arange(patch_rows, dtype=jnp.int32)

    def length_bias(valid):
        return jnp.broadcast_to(jnp.where(valid, 0.0, MASKED)[None, :], (8, valid.shape[0]))

    self_bias = length_bias(
        jnp.concatenate([(token < token_lengths[0]) & (place == 1), token + place * rows < token_lengths[0]])
    )
    cross_own = length_bias(slot + place * patch_rows < patch_counts[0])
    cross_far = length_bias(slot + (1 - place) * patch_rows < patch_counts[0])
    gain_one, gain_two, gain_three = (g.astype(f32)[None, :] for g in (self_gain, cross_gain, mlp_gain))
    scale = 0.125 * LOG2E

    x = decoder_states[0]
    patches = encoder_patches[0]
    dy = output_grad[0]
    far_x = lax.ppermute(x, "seq", [(0, 1)])
    self_rows = weight_rows(self_query, self_key, self_value)
    cross_rows = weight_rows(cross_query)
    feed_rows = weight_rows(mlp_gate, mlp_up)
    share = width // lax.axis_size("plots")
    spot = lax.axis_index("plots") * share
    self_part, cross_part, feed_part = (
        lax.dynamic_slice_in_dim(g, spot, share, 0) for g in (self_gain, cross_gain, mlp_gain)
    )
    small = [self_rows, cross_rows, feed_rows, self_bias, cross_own, cross_far, gain_two, gain_three]
    x, self_rows, cross_rows, feed_rows, self_bias, cross_own, cross_far, gain_two, gain_three = (
        lax.optimization_barrier((x, *small))
    )
    weights = [self_query, self_key, self_value, cross_key, cross_value]
    first, q1, k1, v1, k2, v2 = start(x, gain_one, patches, weights, scale)
    far_x = hold(far_x, k2)
    far_patches = lax.ppermute(hold(patches, far_x), "seq", SEQ_SWAP)
    e1, f1, o1, y1, second, q2, far_first, far_k1, far_v1 = self_forward(
        q1, k1, v1, self_bias, far_x, gain_one, self_key, self_value, x, self_output, gain_two, cross_query, scale
    )
    e2, part2 = attend(q2, [k2], [v2], cross_own)
    far_patches = hold(far_patches, part2)
    far_e2, f2, far_f2, o2, y2, third, hidden, dgu, far_k2, far_v2, send, keep = cross_forward(
        q2, far_patches, cross_key, cross_value, cross_far, part2, y1, cross_output, gain_three, mlp_gate, mlp_up,
        mlp_down, dy,
    )
    feed = FeedSum(send, keep)
    dgu = hold(dgu, feed.token)
    dy2, b2, do2 = feed_back(dgu, mlp_gate, mlp_up, y2, gain_three, dy, cross_output)
    feed.group_step(do2)
    do2 = hold(do2, feed.token)
    far_dq2, far_d2, low, high = cross_back_far(far_e2, do2, o2, far_f2, q2, far_k2, far_v2, cross_key, cross_value)
    near_low = lax.ppermute(low, "seq", SEQ_SWAP)
    near_high = lax.ppermute(high, "seq", SEQ_SWAP)
    d2, dy1, do1, *sends, keep = cross_back_own(
        e2, hold(do2, high), o2, f2, q2, k2, v2, far_dq2, gain_two, cross_query, y1, dy2, self_output, patches,
        far_patches, far_d2, second, b2, o1,
    )
    near_low = hold(near_low, dy1)
    cross = Sum(sends, keep)
    near_high = hold(near_high, cross.token)
    patch_grad = key_value_back(d2, cross_key, cross_value, [near_low, near_high])
    cross.inner_step(patch_grad)
    do1 = hold(do1, cross.token)
    d1, *sends, keep, far_first_grad = self_back(
        e1, do1, o1, f1, q1, [far_k1, k1], [far_v1, v1], far_first, first, self_key, self_value
    )
    own = SeqFirstSum(sends, keep)
    feed.seq_step(own.token)
    layer_output = output(y2, hold(hidden, own.token, feed.token), mlp_down)
    own.seq_first_step(layer_output)
    feed.got = hold(feed.got, own.token)
    cross.outer_step(own.token, feed.got)
    own.inner_step(cross.token)
    near_first_grad = lax.ppermute(hold(far_first_grad, own.token), "seq", [(1, 0)])
    cross.seq_step(own.token)
    own.outer_step(cross.token)
    near_first_grad = hold(near_first_grad, own.token)
    input_grad = finish(d1, self_query, self_key, self_value, near_first_grad, x, gain_one, dy1)
    own.seq_step(input_grad)
    cross.core_step(own.token)
    groups = lax.axis_size("plots") // 2
    gate_sum, up_sum, down_sum = feed.core_step(width // groups, groups, cross.token)
    cross_key_grad, cross_value_grad, cross_query_grad, cross_output_grad, self_output_grad, cross_gain_grad = finalize(
        cross, [width, width], cross_rows, [2], cross_part
    )
    own.core_step(cross_gain_grad)
    query_grad, key_grad, value_grad, self_gain_grad = finalize(own, [width], self_rows, [0, 1, 2], self_part)
    feed_gain_grad = jnp.sum(feed_rows.astype(f32) * jnp.concatenate([gate_sum, up_sum], 1), axis=1)
    return (
        layer_output[None],
        input_grad[None],
        patch_grad[None],
        self_gain_grad.reshape(-1),
        cross_gain_grad.reshape(-1),
        feed_gain_grad / feed_part.astype(f32),
        query_grad,
        key_grad,
        value_grad,
        self_output_grad,
        cross_query_grad,
        cross_key_grad,
        cross_value_grad,
        cross_output_grad,
        gate_sum,
        up_sum,
        down_sum,
    )


def solution(mesh):
    rows = P("plots", "seq", None)
    placed = (rows, rows, P("plots"), P("plots")) + (P(),) * 14 + (rows,)
    return jax.shard_map(
        per_device,
        mesh=mesh,
        in_specs=placed,
        out_specs=(rows, rows, rows) + (P("plots"),) * 3 + (P("plots", None),) * 11,
        check_vma=False,
    )
```

```python
import functools

import jax
import jax.numpy as jnp
from jax import lax
from jax.experimental import pallas as pl
from jax.experimental.pallas import tpu as pltpu
from jax.sharding import PartitionSpec as P

HEADS = 12
eps = 1e-06
bf = jnp.bfloat16
f32 = jnp.float32
LOG2E = 1.4426950408889634
LN2 = 0.6931471805599453
MASKED = -1e30
NN = (((1,), (0,)), ((), ()))
NT = (((1,), (1,)), ((), ()))
TN = (((0,), (0,)), ((), ()))
TT = (((0,), (1,)), ((), ()))
SEQ_SWAP = [(0, 1), (1, 0)]


def dot(left, right, dims=NN):
    return lax.dot_general(left, right, dims, preferred_element_type=f32)


def lane_of(shape):
    return lax.broadcasted_iota(jnp.int32, shape, len(shape) - 1)


def head_lanes(lane, half):
    return (lane < 64) if half == 0 else (lane >= 64)


def lane_rows(half):
    lane = lane_of((1, 128))
    inside = jnp.where(head_lanes(lane, half), 1.0, 0.0)
    return inside.astype(bf), jnp.where(lane == 64 - 64 * half, 1.0, 0.0).astype(bf)


ANY = pl.BlockSpec(memory_space=pl.ANY)


def shape_of(shape, dtype=bf):
    return jax.ShapeDtypeStruct(shape, dtype)


def call(kernel, args, outs, grid=(1,), in_specs=None, out_specs=None, scalars=None, scratch=(), flops=0, name=None):
    def whole(a):
        zeros = (0,) * len(a.shape)
        return pl.BlockSpec(a.shape, lambda *_: zeros, pipeline_mode=pl.Buffered(1))

    def specs(given, arrays):
        given = given or [None] * len(arrays)
        return [whole(a) if s is None else s for s, a in zip(given, arrays)]

    grid_spec = pltpu.PrefetchScalarGridSpec(
        num_scalar_prefetch=0 if scalars is None else 1,
        grid=grid,
        in_specs=specs(in_specs, args),
        out_specs=specs(out_specs, outs),
        scratch_shapes=scratch,
    )
    nbytes = sum(a.size * a.dtype.itemsize for a in args) + sum(a.size * a.dtype.itemsize for a in outs)
    if scalars is not None:
        args = [scalars] + list(args)
    return pl.pallas_call(
        kernel,
        grid_spec=grid_spec,
        out_shape=outs,
        compiler_params=pltpu.CompilerParams(vmem_limit_bytes=58 << 20),
        cost_estimate=pl.CostEstimate(flops=flops, bytes_accessed=nbytes, transcendentals=0),
        name=name,
    )(*args)


def attend_kernel(causal, merge, parts, block, q_ref, bias_ref, *refs):
    key_refs, value_refs = refs[:parts], refs[parts : 2 * parts]
    refs = refs[2 * parts :]
    if merge:
        before_ref, e_ref, o_ref, own_ref, new_ref = refs
    elif parts > 1:
        e_ref, o_ref, own_ref = refs
    else:
        e_ref, o_ref = refs
    rows = q_ref.shape[0]
    pairs = q_ref.shape[1] // 128
    lane_b = lane_of((block, 128))
    first = head_lanes(lane_b, 0)
    full = (block, 128)
    items = [(p, b, half) for p in range(pairs) for b in range(rows // block) for half in range(2)]
    kept = {}

    def reaches(b):
        offset, found = 0, []
        for i, k_ref in enumerate(key_refs):
            keys = k_ref.shape[0]
            seen = min(keys, (b + 1) * block) if causal and i == parts - 1 else keys
            found.append((offset, i, seen))
            offset += keys
        return found

    def scores(item):
        p, b, half = item
        lanes = slice(128 * p, 128 * p + 128)
        q = q_ref[b * block : (b + 1) * block, lanes] * lane_rows(half)[0]
        found = []
        for offset, i, seen in reaches(b):
            s = dot(q, key_refs[i][:seen, lanes], NT) + bias_ref[0:1, offset : offset + seen]
            if causal and i == parts - 1:
                row = lax.broadcasted_iota(jnp.int32, s.shape, 0) + b * block
                s = jnp.where(lane_of(s.shape) <= row, s, MASKED)
            found.append(s)
        return found

    def soften(item, found):
        p, b, half = item
        top = functools.reduce(jnp.maximum, [jnp.max(s, axis=1, keepdims=True) for s in found])
        es = []
        for (offset, i, seen), s in zip(reaches(b), found):
            e = jnp.exp2(s - top).astype(bf)
            e_ref[2 * p + half, b * block : (b + 1) * block, offset : offset + seen] = e
            es.append(e)
        return top, es

    def mix(item, top, es):
        p, b, half = item
        lanes = slice(128 * p, 128 * p + 128)
        at = slice(b * block, (b + 1) * block)
        inside, at0 = lane_rows(half)
        spare = 64 - 64 * half
        o = None
        for (offset, i, seen), e in zip(reaches(b), es):
            part = dot(e, value_refs[i][:seen, lanes] * inside + at0)
            o = part if o is None else o + part
        if not merge and parts == 1:
            o_ref[2 * p + half, at, :] = jnp.where(lane_b == spare + 1, top, o)
            return
        l_new = jnp.broadcast_to(o[:, spare : spare + 1], full)
        if merge:
            old = before_ref[2 * p + half, at, :]
            l_old = jnp.broadcast_to(old[:, spare : spare + 1], full)
            m_old = jnp.broadcast_to(old[:, spare + 1 : spare + 2], full)
            top = jnp.broadcast_to(top, full)
            m = jnp.maximum(m_old, top)
            w_old, w_new = jnp.exp2(m_old - m), jnp.exp2(top - m)
            turn = 1.0 / (l_old * w_old + l_new * w_new)
            f_old, f_new = w_old * turn, w_new * turn
            o = old * f_old + o * f_new
        else:
            f_old = f_new = 1.0 / l_new
            o = o * f_new
        if half == 0:
            kept[p, b] = (o, f_old, f_new)
        else:
            o0, old0, new0 = kept.pop((p, b))
            o_ref[at, lanes] = jnp.where(first, o0, o).astype(bf)
            own_ref[at, lanes] = jnp.where(first, old0, f_old)
            if merge:
                new_ref[at, lanes] = jnp.where(first, new0, f_new)

    s = scores(items[0])
    waiting = None
    for i, item in enumerate(items):
        following = scores(items[i + 1]) if i + 1 < len(items) else None
        if waiting is not None:
            mix(*waiting)
        top, es = soften(item, s)
        waiting = (item, top, es)
        s = following
    mix(*waiting)


def attend(q, keys, values, bias, causal=False, before=None, block=256, group=1):
    rows, width = q.shape
    pairs = width // 128
    merge = before is not None
    total = sum(k.shape[0] for k in keys)

    def column(a):
        return pl.BlockSpec((a.shape[0], 128 * group), lambda p: (0, p))

    tall = column(q)
    e_spec = pl.BlockSpec((2 * group, rows, total), lambda p: (p, 0, 0))
    o_spec = pl.BlockSpec((2 * group, rows, 128), lambda p: (p, 0, 0))
    outs, out_specs = [shape_of((2 * pairs, rows, total))], [e_spec]
    args = [q, bias, *keys, *values]
    in_specs = [tall, None] + [column(a) for a in args[2:]]
    if merge:
        args.append(before)
        in_specs.append(o_spec)
    if merge or len(keys) > 1:
        outs += [shape_of((rows, width))] + [shape_of((rows, width), f32)] * (2 if merge else 1)
        out_specs += [tall] * (3 if merge else 2)
    else:
        outs.append(shape_of((2 * pairs, rows, 128), f32))
        out_specs.append(o_spec)
    return call(
        functools.partial(attend_kernel, causal, merge, len(keys), block),
        args,
        outs,
        (pairs // group,),
        in_specs,
        out_specs,
        flops=16 * rows * total * width,
        name="attend",
    )


def attend_back_kernel(causal, last, parts, block, e_ref, do_ref, o_ref, f_ref, q_ref, *refs):
    key_refs, value_refs = refs[:parts], refs[parts : 2 * parts]
    refs = refs[2 * parts :]
    if last:
        before_ref, dq_ref, d_ref = refs
    elif len(refs) == 2:
        dq_ref, d_ref = refs
    else:
        dq_ref, d_ref = None, refs[0]
    base = d_ref.shape[0] - 2
    rows = q_ref.shape[0]
    pairs = q_ref.shape[1] // 128
    lane_b = lane_of((block, 128))
    items = [(p, half, b) for p in range(pairs) for half in range(2) for b in range(rows // block)]
    dq, dk, dv = {}, {}, {}

    def reaches(b):
        offset, found = 0, []
        for i, k_ref in enumerate(key_refs):
            keys = k_ref.shape[0]
            seen = min(keys, (b + 1) * block) if causal and i == parts - 1 else keys
            found.append((offset, i, seen))
            offset += keys
        return found

    def slopes(item):
        p, half, b = item
        lanes = slice(128 * p, 128 * p + 128)
        at = slice(b * block, (b + 1) * block)
        inb = head_lanes(lane_b, half)
        do = do_ref[at, lanes].astype(f32)
        f = f_ref[at, lanes]
        inner = jnp.sum(jnp.where(inb, do * o_ref[at, lanes].astype(f32), 0.0), axis=1, keepdims=True)
        off = inner * f[:, 64 * half : 64 * half + 1]
        dos = jnp.where(inb, do * f, 0.0).astype(bf)
        return dos, off, [dot(dos, value_refs[i][:seen, lanes], NT) for offset, i, seen in reaches(b)]

    def spread(item, dos, off, dps):
        p, half, b = item
        lanes = slice(128 * p, 128 * p + 128)
        at = slice(b * block, (b + 1) * block)
        q = q_ref[at, lanes]
        for (offset, i, seen), dp in zip(reaches(b), dps):
            e = e_ref[2 * p + half, at, offset : offset + seen]
            ds = (e.astype(f32) * (dp - off)).astype(bf)
            part = dot(ds, key_refs[i][:seen, lanes] * lane_rows(half)[0])
            dq[p, b] = part if (p, b) not in dq else dq[p, b] + part
            step = block if causal and i == parts - 1 else seen
            for c in range(0, seen, step):
                key = (p, half, offset + c)
                vt = dot(dos, e[:, c : c + step], TN)
                kt = dot(q, ds[:, c : c + step], TN)
                dv[key] = vt if key not in dv else dv[key] + vt
                dk[key] = kt if key not in dk else dk[key] + kt

    ready = slopes(items[0])
    for i, item in enumerate(items):
        following = slopes(items[i + 1]) if i + 1 < len(items) else None
        spread(item, *ready)
        ready = following
    for p, b in dq:
        lanes = slice(128 * p, 128 * p + 128)
        at = slice(b * block, (b + 1) * block)
        part = dq[p, b]
        if last:
            dq_ref[at, lanes] = ((part + before_ref[at, lanes]) * 0.125).astype(bf)
        elif base == 0:
            dq_ref[at, lanes] = part
        else:
            d_ref[0, lanes, d_ref.shape[2] - rows + b * block : d_ref.shape[2] - rows + (b + 1) * block] = (
                part.T * 0.125
            ).astype(bf)
    for p, half, c in dk:
        wide = dk[p, half, c].shape[1]
        inside = slice(64 * half, 64 * half + 64)
        at = slice(128 * p + 64 * half, 128 * p + 64 * half + 64)
        d_ref[base, at, c : c + wide] = (dk[p, half, c][inside] * LN2).astype(bf)
        d_ref[base + 1, at, c : c + wide] = dv[p, half, c][inside].astype(bf)


def attend_back(e, do, o, f, q, keys, values, causal=False, before=None, whole=False, block=256, group=1):
    rows, width = q.shape
    pairs = width // 128
    total = sum(k.shape[0] for k in keys)

    def column(a):
        return pl.BlockSpec((a.shape[0], 128 * group), lambda p: (0, p))

    tall = column(q)
    args = [e, do, o, f, q, *keys, *values]
    in_specs = [pl.BlockSpec((2 * group, rows, total), lambda p: (p, 0, 0))] + [column(a) for a in args[1:]]
    if before is not None:
        args.append(before)
        in_specs.append(tall)
    return call(
        functools.partial(attend_back_kernel, causal, before is not None, len(keys), block),
        args,
        ([] if whole else [shape_of((rows, width), f32 if before is None else bf)])
        + [shape_of((2 + whole, width, total))],
        (pairs // group,),
        in_specs,
        ([] if whole else [tall]) + [pl.BlockSpec((2 + whole, 128 * group, total), lambda p: (0, p, 0))],
        flops=16 * rows * total * width,
        name="attend_back",
    )


def late(refs, buffers, sems):
    copies = [pltpu.make_async_copy(ref, buffer, sems.at[i]) for i, (ref, buffer) in enumerate(zip(refs, buffers))]

    @pl.when(pl.program_id(0) == 0)
    def _():
        for copy in copies:
            copy.start()

    def fetch(i):
        copies[i].wait()
        return buffers[i]

    return fetch


def self_back(e, do, o, f, q, keys, values, far_first, first, wk, wv):
    rows, width = q.shape
    pairs = width // 128
    total = 2 * rows
    half = width // 2
    pieces = (width + half) // 128
    back = functools.partial(attend_back_kernel, True, False, 2, 256)

    def kernel(core_ref, *refs):
        blocks, (ff_ref, first_ref, wk_ref, wv_ref) = refs[:9], refs[9:13]
        d_ref, *send_refs, keep_ref, out_ref = refs[13 : 16 + pieces]
        all_ref, part_ref, *buffers, sems = refs[16 + pieces :]
        fetch = late([ff_ref, first_ref, wk_ref, wv_ref], buffers, sems)
        i = pl.program_id(0)
        core = core_ref[0]

        @pl.when(i < pairs)
        def _():
            back(*blocks, part_ref)
            d_ref[...] = part_ref[:, :, rows:]
            all_ref[:, pl.ds(pl.multiple_of(i * 128, 128), 128), :] = part_ref[...]

        @pl.when(i == pairs)
        def _():
            far, own = fetch(0)[...], fetch(1)[...]
            query = dot(own, all_ref[0, :, rows:], TT)
            key = dot(far, all_ref[1, :, :rows], TT) + dot(own, all_ref[1, :, rows:], TT)
            halves(send_refs, keep_ref, core, 0, query, key)

        @pl.when(i == pairs + 1)
        def _():
            far, own = buffers[0][...], buffers[1][...]
            value = dot(far, all_ref[2, :, :rows], TT) + dot(own, all_ref[2, :, rows:], TT)
            halves(send_refs, keep_ref, core, width, value[:, :half], value[:, half:])
            grad = dot(all_ref[1, :, :rows], fetch(2)[...], TT) + dot(all_ref[2, :, :rows], fetch(3)[...], TT)
            out_ref[...] = grad.astype(bf)

    def column(a):
        return pl.BlockSpec((a.shape[0], 128), lambda i, s: (0, jnp.minimum(i, pairs - 1)))

    args = [e, do, o, f, q, *keys, *values, far_first, first, wk, wv]
    in_specs = [pl.BlockSpec((2, rows, total), lambda i, s: (jnp.minimum(i, pairs - 1), 0, 0))]
    in_specs += [column(a) for a in args[1:9]] + [pl.BlockSpec(memory_space=pl.ANY)] * 4
    own = pl.BlockSpec((3, 128, rows), lambda i, s: (0, jnp.minimum(i, pairs - 1), 0))
    return call(
        kernel,
        args,
        [shape_of((3, width, rows))]
        + [shape_of((width, 128))] * pieces
        + [shape_of((width, width + half)), shape_of((rows, width))],
        (pairs + 2,),
        in_specs,
        [own] + [None] * (pieces + 2),
        core_scalar(),
        scratch=[pltpu.VMEM((3, width, total), bf), pltpu.VMEM((3, 128, total), bf)]
        + [pltpu.VMEM(a.shape, bf) for a in args[9:]]
        + [pltpu.SemaphoreType.DMA((4,))],
        flops=16 * rows * total * width + 12 * rows * width * width,
        name="self_back",
    )


def cross_back_far(e, do, o, f, q, k, v, wk, wv):
    rows, width = q.shape
    pairs = width // 128
    keys = k.shape[0]
    half = keys // 2

    def kernel(*refs):
        blocks, (wk_ref, wv_ref), (dq_ref, d_ref, out_ref) = refs[:7], refs[7:9], refs[9:12]
        all_ref, *buffers, sems = refs[12:]
        fetch = late([wk_ref, wv_ref], buffers, sems)
        i = pl.program_id(0)

        @pl.when(i < pairs)
        def _():
            attend_back_kernel(False, False, 1, 256, *blocks, dq_ref, d_ref)
            all_ref[:, pl.ds(pl.multiple_of(i * 128, 128), 128), :] = d_ref[...]

        @pl.when(i == pairs)
        def _():
            fetch(0), fetch(1)

        @pl.when(i >= pairs)
        def _():
            at = pl.ds(pl.multiple_of((i - pairs) * half, half), half)
            grad = dot(all_ref[0, :, at], buffers[0][...], TT) + dot(all_ref[1, :, at], buffers[1][...], TT)
            out_ref[...] = grad.astype(bf)

    def spot(i):
        return jnp.minimum(i, pairs - 1)

    def column(a):
        return pl.BlockSpec((a.shape[0], 128), lambda i: (0, spot(i)))

    args = [e, do, o, f, q, k, v, wk, wv]
    return call(
        kernel,
        args,
        [shape_of((rows, width), f32), shape_of((2, width, keys)), shape_of((keys, width))],
        (pairs + 2,),
        [pl.BlockSpec((2, rows, keys), lambda i: (spot(i), 0, 0))] + [column(a) for a in args[1:7]] + [ANY] * 2,
        [column(q), pl.BlockSpec((2, 128, keys), lambda i: (0, spot(i), 0))]
        + [pl.BlockSpec((half, width), lambda i: (jnp.maximum(i - pairs, 0), 0))],
        scratch=[pltpu.VMEM((2, width, keys), bf)] + [pltpu.VMEM(wk.shape, bf)] * 2 + [pltpu.SemaphoreType.DMA((2,))],
        flops=16 * rows * keys * width + 4 * keys * width * width,
        name="cross_back_far",
    )


def cross_back_own(e, do, o, f, q, k, v, before, gain, wq, y1, dy2, wo, patches, far_patches, far_d, second, b2, o1):
    rows, width = q.shape
    pairs = width // 128
    keys = k.shape[0]
    half = width // 2
    chunk = 512
    parts = keys // chunk

    def kernel(core_ref, *refs):
        blocks, gain_ref, late_refs = refs[:8], refs[8], refs[9:20]
        d_ref, dy1_ref, do1_ref, *send_refs, keep_ref = refs[20:29]
        all_ref, dq_ref, acc_ref, b1_ref, *buffers, sems = refs[29:]
        fetch = late(late_refs, buffers, sems)
        i = pl.program_id(0)
        core = core_ref[0]

        @pl.when(i < pairs)
        def _():
            at = pl.ds(pl.multiple_of(i * 128, 128), 128)
            attend_back_kernel(False, True, 1, 256, *blocks, dq_ref.at[:, at], d_ref)
            all_ref[:, at, :] = d_ref[...]

        @pl.when(i == pairs)
        def _():
            for j in range(11):
                fetch(j)
            grad = dot(dq_ref[...], buffers[0][...], NT)
            unit, scale = norm_parts(buffers[1][...])
            dy1 = buffers[2][...] + norm_back(unit, scale, gain_ref[...], grad)
            dy1_ref[...] = dy1
            b1_ref[...] = dy1.astype(bf)
            do1_ref[...] = dot(b1_ref[...], buffers[3][...], NT).astype(bf)
            acc_ref[...] = jnp.zeros_like(acc_ref)

        @pl.when((i > pairs) & (i <= pairs + parts))
        def _():
            at = pl.ds(pl.multiple_of((i - pairs - 1) * chunk, chunk), chunk)

            @pl.loop(0, 2)
            def _(j):
                left, far = buffers[4][at, :], buffers[5][at, :]
                acc_ref[j] += dot(left, all_ref[j, :, at], TT) + dot(far, buffers[6][j, :, at], TT)

        @pl.when(i == pairs + parts + 1)
        def _():
            halves(send_refs, keep_ref, core, 0, acc_ref[0], acc_ref[1])
            query, output = dot(buffers[7][...], dq_ref[...], TN), dot(buffers[10][...], buffers[8][...], TN)
            halves(send_refs, keep_ref, core, width, query, output)
            value = dot(buffers[9][...], b1_ref[...], TN)
            halves(send_refs, keep_ref, core, 2 * width, value[:, :half], value[:, half:])

    def spot(i):
        return jnp.minimum(i, pairs - 1)

    def column(a):
        return pl.BlockSpec((a.shape[0], 128), lambda i, s: (0, spot(i)))

    lates = [wq, y1, dy2, wo, patches, far_patches, far_d, second, b2, o1, o]
    args = [e, do, o, f, q, k, v, before, gain] + lates
    full = shape_of((rows, width), f32)
    return call(
        kernel,
        args,
        [shape_of((2, width, keys)), full, shape_of((rows, width))]
        + [shape_of((width, half))] * 5
        + [shape_of((width, 2 * width + half))],
        (pairs + parts + 2,),
        [pl.BlockSpec((2, rows, keys), lambda i, s: (spot(i), 0, 0))]
        + [column(a) for a in args[1:8]]
        + [None]
        + [ANY] * 11,
        [pl.BlockSpec((2, 128, keys), lambda i, s: (0, spot(i), 0))] + [None] * 8,
        core_scalar(),
        scratch=[
            pltpu.VMEM((2, width, keys), bf),
            pltpu.VMEM((rows, width), bf),
            pltpu.VMEM((2, width, width), f32),
            pltpu.VMEM((rows, width), bf),
        ]
        + [pltpu.VMEM(a.shape, a.dtype) for a in lates]
        + [pltpu.SemaphoreType.DMA((11,))],
        flops=16 * rows * keys * width + 2 * width * width * (5 * rows + 4 * keys),
        name="cross_back_own",
    )


def rows_loop(out_ref, left_ref, w_ref, finish=lambda v: v):
    @pl.loop(0, left_ref.shape[0] // 256)
    def _(i):
        at = pl.ds(pl.multiple_of(i * 256, 256), 256)
        out_ref[at, :] = finish(dot(left_ref[at, :], w_ref[...])).astype(out_ref.dtype)


def norm_parts(value):
    scale = lax.rsqrt(jnp.mean(value * value, axis=-1, keepdims=True) + eps)
    return value * scale, scale


def norm_back(unit, scale, gain, grad):
    inner = gain * grad
    return scale * (inner - unit * jnp.mean(inner * unit, axis=-1, keepdims=True))


def gelu_parts(u):
    t = jnp.tanh(0.7978845608028654 * (u + 0.044715 * u * u * u))
    value = 0.5 * u * (1.0 + t)
    slope = 0.5 * (1.0 + t) + 0.5 * u * (1.0 - t * t) * (0.7978845608028654 * (1.0 + 3 * 0.044715 * u * u))
    return value, slope


def start(x, gain, patches, weights, scale):
    def kernel(gain_ref, x_ref, w0, w1, w2, p_ref, w3, w4, *refs):
        outs, refs = refs[:6], refs[6:]
        ins, results, in_sems, out_sems = refs[:7], refs[7:13], refs[13], refs[14]
        loads = [
            pltpu.make_async_copy(ref, buffer, in_sems.at[i])
            for i, (ref, buffer) in enumerate(zip((x_ref, w0, w1, w2, p_ref, w3, w4), ins))
        ]
        stores = [
            pltpu.make_async_copy(buffer, ref, out_sems.at[i]) for i, (buffer, ref) in enumerate(zip(results, outs))
        ]
        loads[0].start()
        loads[1].start()
        loads[0].wait()
        for load in loads[2:]:
            load.start()
        first = (norm_parts(ins[0][...].astype(f32))[0] * gain_ref[...]).astype(bf)
        results[0][...] = first
        stores[0].start()
        for j in range(3):
            loads[1 + j].wait()
            rows_loop(results[1 + j], results[0], ins[1 + j], (lambda v: v * scale) if j == 0 else (lambda v: v))
            stores[1 + j].start()
        loads[4].wait()
        for j in range(2):
            loads[5 + j].wait()
            rows_loop(results[4 + j], ins[4], ins[5 + j])
            stores[4 + j].start()
        for store in stores:
            store.wait()

    args = [gain, x, *weights[:3], patches, *weights[3:]]
    outs = [shape_of(x.shape)] * 4 + [shape_of(patches.shape)] * 2
    return call(
        kernel,
        args,
        outs,
        in_specs=[None] + [ANY] * 7,
        out_specs=[ANY] * 6,
        scratch=[pltpu.VMEM(a.shape, bf) for a in args[1:] + outs]
        + [pltpu.SemaphoreType.DMA((7,)), pltpu.SemaphoreType.DMA((6,))],
        flops=2 * 768 * (3 * x.size + 2 * patches.size),
        name="start",
    )


def self_forward(q, k, v, bias, far_x, gain, wk, wv, x, w_out, next_gain, w_query, scale):
    rows, width = q.shape
    pairs = width // 128
    total = 2 * rows

    def kernel(q_ref, k_ref, v_ref, bias_ref, fx_ref, gain_ref, wk_ref, wv_ref, ng_ref, x_ref, wo_ref, wq_ref, *refs):
        e_ref, f_ref, o_ref, y_ref, n_ref, q2_ref, *far_out = refs[:9]
        far_first, far_k, far_v, *buffers, sems, out_sems = refs[9:]
        fetch = late([x_ref, wo_ref, wq_ref], buffers, sems)
        stores = [
            pltpu.make_async_copy(buffer, ref, out_sems.at[j])
            for j, (buffer, ref) in enumerate(zip((far_first, far_k, far_v), far_out))
        ]
        i = pl.program_id(0)

        @pl.when(i == 0)
        def _():
            far_first[...] = (norm_parts(fx_ref[...].astype(f32))[0] * gain_ref[...]).astype(bf)
            rows_loop(far_k, far_first, wk_ref)
            rows_loop(far_v, far_first, wv_ref)
            for store in stores:
                store.start()

        @pl.when((i > 0) & (i <= pairs))
        def _():
            at = pl.ds(pl.multiple_of((i - 1) * 128, 128), 128)
            refs = far_k.at[:, at], k_ref, far_v.at[:, at], v_ref
            attend_kernel(True, False, 2, 256, q_ref, bias_ref, *refs, e_ref, o_ref.at[:, at], f_ref)

        @pl.when(i == pairs + 1)
        def _():
            y = fetch(0)[...].astype(f32) + dot(o_ref[...], fetch(1)[...])
            y_ref[...] = y
            n_ref[...] = (norm_parts(y)[0] * ng_ref[...]).astype(bf)
            q2_ref[...] = (dot(n_ref[...], fetch(2)[...]) * scale).astype(bf)
            for store in stores:
                store.wait()

    def spot(i):
        return jnp.clip(i - 1, 0, pairs - 1)

    column = pl.BlockSpec((rows, 128), lambda i: (0, spot(i)))
    args = [q, k, v, bias, far_x, gain, wk, wv, next_gain, x, w_out, w_query]
    flat = shape_of((rows, width))
    return call(
        kernel,
        args,
        [shape_of((2 * pairs, rows, total)), shape_of((rows, width), f32), flat, shape_of((rows, width), f32)]
        + [flat] * 5,
        (pairs + 2,),
        [column] * 3 + [None] * 6 + [ANY] * 3,
        [pl.BlockSpec((2, rows, total), lambda i: (spot(i), 0, 0)), column] + [None] * 4 + [ANY] * 3,
        scratch=[pltpu.VMEM((rows, width), bf)] * 3
        + [pltpu.VMEM(a.shape, bf) for a in args[9:]]
        + [pltpu.SemaphoreType.DMA((3,)), pltpu.SemaphoreType.DMA((3,))],
        flops=16 * rows * total * width + 8 * rows * width * width,
        name="self_forward",
    )


def cross_forward(q, patches, wk, wv, bias, before, y1, w_out, gain, w_gate, w_up, w_down, dy):
    total, inner, outer, *_ = places()
    groups = inner * outer
    rows, width = q.shape
    keys = patches.shape[0]
    pairs = width // 128
    hidden = w_gate.shape[1]
    share, lanes = width // groups, hidden // groups
    blocks, step = hidden // lanes, 512
    per, chunks = step // lanes, hidden // step
    half = width // 2
    grouped = lanes % 128 == 0 and share % 16 == 0

    def kernel(core_ref, q_ref, bias_ref, before_ref, gain_ref, p_ref, wk_ref, wv_ref, *refs):
        late_refs, refs = refs[:6], refs[6:]
        e_ref, own_ref, new_ref, o_ref, y2_ref, third_ref, h_ref, d_ref, *outs = refs[:12]
        k_ref, v_ref, send_ref, keep_ref, *buffers, sems, out_sems = refs[12:]
        fetch = late(late_refs, buffers, sems)
        stores = [
            pltpu.make_async_copy(buffer, ref, out_sems.at[j])
            for j, (buffer, ref) in enumerate(zip((k_ref, v_ref, send_ref, keep_ref), outs))
        ]
        i = pl.program_id(0)
        here = core_ref[0] == 0

        @pl.when(i == 0)
        def _():
            rows_loop(k_ref, p_ref, wk_ref)
            rows_loop(v_ref, p_ref, wv_ref)
            stores[0].start()
            stores[1].start()

        @pl.when((i > 0) & (i <= pairs))
        def _():
            at = pl.ds(pl.multiple_of((i - 1) * 128, 128), 128)
            refs = k_ref.at[:, at], v_ref.at[:, at], before_ref, e_ref, o_ref.at[:, at], own_ref, new_ref
            attend_kernel(False, True, 1, rows, q_ref, bias_ref, *refs)

        @pl.when(i == pairs + 1)
        def _():
            y2 = fetch(0)[...] + dot(o_ref[...], fetch(1)[...])
            y2_ref[...] = y2
            third_ref[...] = (norm_parts(y2)[0] * gain_ref[...]).astype(bf)
            for j in range(2, 6):
                fetch(j)

        @pl.when(i > pairs)
        def _():
            c = i - pairs - 1
            at = pl.ds(pl.multiple_of(c * step, step), step)
            wg_ref, wu_ref, wd_ref, dy_ref = buffers[2:]
            low = rows // 2

            @pl.loop(0, 2)
            def _(r):
                part = pl.ds(pl.multiple_of(r * low, low), low)
                third = third_ref[part, :]
                gate = dot(third, wg_ref[:, at])
                up = dot(third, wu_ref[:, at])
                dhidden = dot(dy_ref[part, :], wd_ref[at, :], NT)
                act, slope = gelu_parts(gate)
                h_ref[part, :] = (act * up).astype(bf)
                d_ref[0, part, :] = (dhidden * up * slope).astype(bf)
                d_ref[1, part, :] = (dhidden * act).astype(bf)

            third = third_ref[...]
            gate, up = dot(third, d_ref[0], TN), dot(third, d_ref[1], TN)
            send, keep = jnp.where(here, up, gate).astype(bf), jnp.where(here, gate, up).astype(bf)
            for g in range(groups if grouped else 0):
                from_rows = slice(g * share, (g + 1) * share)
                for j in range(per):
                    to = pl.ds(pl.multiple_of((c * per + j) * share, share), share)
                    send_ref[g, to, :] = send[from_rows, j * lanes : (j + 1) * lanes]
                    keep_ref[g, to, :] = keep[from_rows, j * lanes : (j + 1) * lanes]
            if not grouped:
                send_ref[:width, at] = send
                keep_ref[:width, at] = keep
            down = dot(dy_ref[...], h_ref[...], TN)
            send, keep = jnp.where(here, down[half:], down[:half]), jnp.where(here, down[:half], down[half:])
            if not grouped:
                send_ref[width:, at] = send.astype(bf)
                keep_ref[width:, at] = keep.astype(bf)
            to = slice(blocks * share, blocks * share + half)
            for j in range(per if grouped else 0):
                send_ref[c * per + j, to, :] = send[:, j * lanes : (j + 1) * lanes].astype(bf)
                keep_ref[c * per + j, to, :] = keep[:, j * lanes : (j + 1) * lanes].astype(bf)

        @pl.when(i == pairs + chunks)
        def _():
            stores[2].start()
            stores[3].start()
            for store in stores:
                store.wait()

    def spot(i):
        return jnp.clip(i - 1, 0, pairs - 1)

    def chunk(i):
        return jnp.clip(i - 1 - pairs, 0, chunks - 1)

    column = pl.BlockSpec((rows, 128), lambda i, s: (0, spot(i)))
    args = [q, bias, before, gain, patches, wk, wv, y1, w_out, w_gate, w_up, w_down, dy]
    flat, key, full = shape_of((rows, width)), shape_of((keys, width)), shape_of((rows, width), f32)
    grads = shape_of((groups, blocks * share + half, lanes) if grouped else (width + half, hidden))
    *outs, send, keep = call(
        kernel,
        args,
        [shape_of((2 * pairs, rows, keys)), full, full, flat, full, flat]
        + [shape_of((rows, hidden)), shape_of((2, rows, hidden)), key, key, grads, grads],
        (pairs + 1 + chunks,),
        [column, None, pl.BlockSpec((2, rows, 128), lambda i, s: (spot(i), 0, 0))] + [None] * 4 + [ANY] * 6,
        [pl.BlockSpec((2, rows, keys), lambda i, s: (spot(i), 0, 0)), column, column, None, None, None]
        + [pl.BlockSpec((rows, step), lambda i, s: (0, chunk(i)))]
        + [pl.BlockSpec((2, rows, step), lambda i, s: (0, 0, chunk(i)))]
        + [ANY] * 4,
        core_scalar(),
        scratch=[pltpu.VMEM(a.shape, bf) for a in (key, key, grads, grads)]
        + [pltpu.VMEM(a.shape, a.dtype) for a in args[7:]]
        + [pltpu.SemaphoreType.DMA((6,)), pltpu.SemaphoreType.DMA((4,))],
        flops=16 * rows * keys * width + 4 * keys * width * width + 12 * rows * width * hidden,
        name="cross_forward",
    )

    def group(value):
        if grouped:
            return value
        gate = value[:width].reshape(groups, share, blocks, lanes).swapaxes(1, 2).reshape(groups, -1, lanes)
        return jnp.concatenate([gate, value[width:].reshape(half, groups, lanes).swapaxes(0, 1)], 1)

    return *outs, group(send), group(keep)


def feed_back(d, w_gate, w_up, y2, gain, dy, w_out):
    def kernel(d_ref, wg_ref, wu_ref, gain_ref, y2_ref, dy_ref, wo_ref, dy2_ref, b_ref, do_ref, acc_ref, *refs):
        *buffers, sems = refs
        fetch = late([y2_ref, dy_ref, wo_ref], buffers, sems)
        i = pl.program_id(0)
        part = dot(d_ref[0], wg_ref[...], NT) + dot(d_ref[1], wu_ref[...], NT)

        @pl.when(i == 0)
        def _():
            acc_ref[...] = part

        @pl.when(i > 0)
        def _():
            acc_ref[...] += part

        @pl.when(i == pl.num_programs(0) - 1)
        def _():
            grad = acc_ref[...]
            unit, scale = norm_parts(fetch(0)[...])
            dy2 = fetch(1)[...].astype(f32) + norm_back(unit, scale, gain_ref[...], grad)
            dy2_ref[...] = dy2
            b_ref[...] = dy2.astype(bf)
            do_ref[...] = dot(b_ref[...], fetch(2)[...], NT).astype(bf)

    rows, width = y2.shape
    hidden = w_gate.shape[1]
    column = pl.BlockSpec((width, 512), lambda i: (0, i))
    return call(
        kernel,
        [d, w_gate, w_up, gain, y2, dy, w_out],
        [shape_of(y2.shape, f32), shape_of(y2.shape), shape_of(y2.shape)],
        (hidden // 512,),
        [pl.BlockSpec((2, rows, 512), lambda i: (0, 0, i)), column, column, None, ANY, ANY, ANY],
        scratch=[pltpu.VMEM((rows, width), f32)]
        + [pltpu.VMEM(a.shape, a.dtype) for a in (y2, dy, w_out)]
        + [pltpu.SemaphoreType.DMA((3,))],
        flops=2 * y2.size * (768 + 2 * hidden),
        name="feed_back",
    )


def finish(d, wq, wk, wv, near, x, gain, dy1):
    def kernel(d_ref, wq_ref, wk_ref, wv_ref, near_ref, x_ref, gain_ref, dy_ref, out_ref):
        grad = near_ref[...].astype(f32)
        for j, w_ref in enumerate((wq_ref, wk_ref, wv_ref)):
            grad = grad + dot(d_ref[j], w_ref[...], TT)
        unit, scale = norm_parts(x_ref[...].astype(f32))
        out_ref[...] = (dy_ref[...] + norm_back(unit, scale, gain_ref[...], grad)).astype(bf)

    rows = x.shape[0]
    return call(
        kernel, [d, wq, wk, wv, near, x, gain, dy1], [shape_of(x.shape)], (1,),
        flops=6 * x.size * 768, name="finish",
    )[0]


def output(y2, hidden, w_down):
    def kernel(y_ref, h_ref, w_ref, out_ref):
        out_ref[...] = (y_ref[...] + dot(h_ref[...], w_ref[...])).astype(bf)

    rows, width = y2.shape
    half = pl.BlockSpec((rows, width // 2), lambda i: (0, i))
    return call(
        kernel, [y2, hidden, w_down], [shape_of(y2.shape)], (2,),
        [half, None, pl.BlockSpec((hidden.shape[1], width // 2), lambda i: (0, i))], [half],
        flops=2 * hidden.size * width, name="output",
    )[0]


def key_value_back(d, wk, wv, near):
    keys = d.shape[2]
    half = keys // 2

    def kernel(d_ref, wk_ref, wv_ref, near_ref, out_ref):
        grad = dot(d_ref[0], wk_ref[...], TT) + dot(d_ref[1], wv_ref[...], TT)
        out_ref[...] = (grad + near_ref[...].astype(f32)).astype(bf)

    rows = pl.BlockSpec((half, wk.shape[0]), lambda i: (i, 0))
    part = pl.BlockSpec((2, d.shape[1], half), lambda i: (0, 0, i))
    return call(
        kernel, [d, wk, wv, near], [shape_of((keys, wk.shape[0]))], (2,), [part, None, None, rows], [rows],
        flops=4 * keys * 768 * 768, name="key_value_back",
    )[0]


def ring_factors(groups):
    inner = 1
    while inner * inner * 4 <= groups:
        inner *= 2
    return inner, groups // inner


def places():
    total = lax.axis_size("plots")
    index = lax.axis_index("plots")
    inner, outer = ring_factors(total // 2)
    group = index // 2
    return total, inner, outer, group // inner, group % inner, index % 2


def core_swap(value):
    total = lax.axis_size("plots")
    return lax.ppermute(value, "plots", [(i, i ^ 1) for i in range(total)])


def outer_shift(value, k):
    total, inner, outer, *_ = places()
    stride = 2 * inner
    return lax.ppermute(value, "plots", [(i, ((i // stride + k) % outer) * stride + i % stride) for i in range(total)])


def inner_shift(value, k):
    total, inner, outer, *_ = places()

    def spot(i):
        y = (i // 2) % inner
        return i + ((y + k) % inner - y) * 2

    return lax.ppermute(value, "plots", [(i, spot(i)) for i in range(total)])


def hold(value, *tokens):
    return lax.optimization_barrier((value,) + tokens)[0]


def halves(send_refs, keep_ref, core, start, one, two):
    here = core == 0
    send = jnp.where(here, two, one).astype(bf)
    keep_ref[:, start : start + one.shape[1]] = jnp.where(here, one, two).astype(bf)
    wide = send_refs[0].shape[1]
    for c in range(0, one.shape[1], wide):
        send_refs[(start + c) // wide][...] = send[:, c : c + wide]


def core_scalar():
    return (lax.axis_index("plots") % 2).astype(jnp.int32)[None]


def combine(keep, pieces, spot):
    outer, inner, share, columns = keep.shape

    def kernel(y_ref, keep_ref, *refs):
        *piece_refs, mine_ref, send_ref = refs
        y = y_ref[0]

        @pl.loop(0, outer // steps)
        def _(i):
            start = 0
            for ref in piece_refs:
                at = slice(start, start + ref.shape[3])
                start += ref.shape[3]
                one = keep_ref[i, 0, :, at].astype(f32) + ref[i, 0].astype(f32)
                two = keep_ref[i, 1, :, at].astype(f32) + ref[i, 1].astype(f32)
                mine_ref[i, :, at] = jnp.where(y == 0, one, two).astype(bf)
                send_ref[i, :, at] = jnp.where(y == 0, two, one).astype(bf)

    steps = 2

    def block(a):
        return pl.BlockSpec((outer // steps,) + a.shape[1:], lambda i, s: (i,) + (0,) * (len(a.shape) - 1))

    args = [keep] + [p.reshape(outer, inner, share, p.shape[1]) for p in pieces]
    out = shape_of((outer, share, columns))
    return call(
        kernel, args, [out, out], (steps,), [block(a) for a in args], [block(out)] * 2,
        spot.astype(jnp.int32)[None], name="combine",
    )


class Sum:
    def __init__(self, sends, keep):
        self.token = sends[-1]
        self.mine = keep
        self.got = [core_swap(send) for send in sends]

    def inner_step(self, *tokens):
        total, inner, outer, z, y, core = places()
        split = (outer, inner, self.mine.shape[0] // (outer * inner), self.mine.shape[1])
        mine = self.mine.reshape(split)
        got = lax.optimization_barrier(tuple(self.got) + tokens)[: len(self.got)]
        if inner == 2:
            self.mine, self.token = combine(mine, got, y)
            self.got = lax.ppermute(self.token, "plots", [(i, i ^ 2) for i in range(total)])
        else:
            got = jnp.concatenate(got, 1).reshape(split)
            groups = [[(o * inner + i) * 2 + c for i in range(inner)] for o in range(outer) for c in range(2)]
            self.token = (mine.astype(f32) + got.astype(f32)).astype(bf)
            self.mine = None
            self.got = lax.all_to_all(self.token, "plots", 1, 1, axis_index_groups=groups, tiled=True)

    def outer_step(self, *tokens):
        total, inner, outer, z, y, core = places()
        got = hold(self.got, *tokens)

        def part(at):
            if self.mine is None:
                value = lax.dynamic_index_in_dim(got, at, 0, keepdims=False)
                return jnp.sum(value.astype(f32), axis=0).astype(bf)
            one = lax.dynamic_index_in_dim(self.mine, at, 0, keepdims=False)
            two = lax.dynamic_index_in_dim(got, at, 0, keepdims=False)
            return (one.astype(f32) + two.astype(f32)).astype(bf)

        self.parts = [part((z + k) % outer) for k in range(1, outer)]
        self.got = [outer_shift(value, k + 1) for k, value in enumerate(self.parts)]
        self.token = self.parts[-1]
        self.mine = part(z)

    def seq_step(self, *tokens):
        got = lax.optimization_barrier(tuple(self.got) + tokens)[: len(self.got)]
        self.mine = sum((g.astype(f32) for g in got), self.mine.astype(f32)).astype(bf)
        self.token = self.mine
        self.got = lax.ppermute(self.mine, "seq", SEQ_SWAP)

    def core_step(self, *tokens):
        core = lax.axis_index("plots") % 2
        value = self.mine.astype(f32) + hold(self.got, *tokens).astype(f32)
        value = value.reshape((2, value.shape[0] // 2) + value.shape[1:])
        self.mine = lax.dynamic_index_in_dim(value, core, 0, keepdims=False)
        self.token = lax.dynamic_index_in_dim(value, 1 - core, 0, keepdims=False).astype(bf)
        self.got = core_swap(self.token)

    def done(self):
        core = lax.axis_index("plots") % 2
        other = self.got.astype(f32)
        return jnp.where(core == 0, self.mine, other), jnp.where(core == 0, other, self.mine)


class SeqFirstSum(Sum):
    def seq_first_step(self, *tokens):
        total, inner, outer, *_ = places()
        split = (outer * inner, 2, self.mine.shape[0] // (outer * inner * 2), self.mine.shape[1])
        got = lax.optimization_barrier(tuple(self.got) + tokens)[: len(self.got)]
        self.mine, self.token = combine(self.mine.reshape(split), got, lax.axis_index("seq"))
        self.got = lax.ppermute(self.token, "seq", SEQ_SWAP)

    def inner_step(self, *tokens):
        total, inner, outer, z, y, core = places()
        split = (outer, inner) + self.mine.shape[1:]
        mine, got = self.mine.reshape(split), hold(self.got, *tokens).reshape(split)

        def part(at):
            one = lax.dynamic_index_in_dim(mine, at, 1, keepdims=False)
            two = lax.dynamic_index_in_dim(got, at, 1, keepdims=False)
            return (one.astype(f32) + two.astype(f32)).astype(bf)

        if inner == 2:
            self.token = part(1 - y)
            self.got = lax.ppermute(self.token, "plots", [(i, i ^ 2) for i in range(total)])
            self.mine = part(y)
        else:
            groups = [[(o * inner + i) * 2 + c for i in range(inner)] for o in range(outer) for c in range(2)]
            self.token = (mine.astype(f32) + got.astype(f32)).astype(bf)
            self.mine = None
            self.got = lax.all_to_all(self.token, "plots", 1, 1, axis_index_groups=groups, tiled=True)

    def core_step(self, *tokens):
        core = lax.axis_index("plots") % 2
        got = hold(self.got, *tokens)
        own = lax.axis_index("seq") == core
        self.token = jnp.where(own, got, self.mine)
        self.mine = jnp.where(own, self.mine, got)
        self.got = core_swap(self.token)


def weight_rows(*weights):
    share = weights[0].shape[0] // lax.axis_size("plots")
    at = lax.axis_index("plots") * share
    return jnp.concatenate([lax.dynamic_slice_in_dim(w, at, share, 0) for w in weights], 1)


def finalize(sums, widths, rows, picks, gain):
    share, columns = sums.mine.shape
    pairs = len(widths)
    half = columns - sum(widths)

    def kernel(core_ref, mine_ref, other_ref, rows_ref, gain_ref, *refs):
        here = core_ref[0] == 0
        mine, other = mine_ref[...].astype(f32), other_ref[...].astype(f32)
        one, two = jnp.where(here, mine, other), jnp.where(here, other, mine)
        start = 0
        for j, wide in enumerate(widths):
            refs[2 * j][...] = one[:, start : start + wide]
            refs[2 * j + 1][...] = two[:, start : start + wide]
            start += wide
        refs[2 * pairs][:, :half] = one[:, start:]
        refs[2 * pairs][:, half:] = two[:, start:]
        total, start = 0.0, 0
        for j in picks:
            value = refs[j][...]
            product = value * rows_ref[:, start : start + value.shape[1]].astype(f32)
            high = product.astype(bf)
            ones = jnp.ones((8, value.shape[1]), bf)
            total = total + dot(ones, high, NT) + dot(ones, (product - high.astype(f32)).astype(bf), NT)
            start += value.shape[1]
        refs[-1][...] = total[0:1] / gain_ref[...]

    outs = [shape_of((share, wide), f32) for wide in widths for _ in range(2)]
    outs += [shape_of((share, 2 * half), f32), shape_of((1, share), f32)]
    args = [sums.mine, sums.got, rows, gain[None, :].astype(f32)]
    return call(kernel, args, outs, scalars=core_scalar(), name="finalize")


def combine_rows(keep, got, spot, low):
    outer, inner, rows, lanes = keep.shape

    def kernel(y_ref, keep_ref, got_ref, *refs):
        y = y_ref[0]
        for j, at in enumerate((slice(0, low), slice(low, rows))):
            one = keep_ref[0, 0, at, :].astype(f32) + got_ref[0, 0, at, :].astype(f32)
            two = keep_ref[0, 1, at, :].astype(f32) + got_ref[0, 1, at, :].astype(f32)
            refs[2 * j][0] = jnp.where(y == 0, one, two).astype(bf)
            refs[2 * j + 1][0] = jnp.where(y == 0, two, one).astype(bf)

    outs = [shape_of((outer, low, lanes))] * 2 + [shape_of((outer, rows - low, lanes))] * 2
    block = pl.BlockSpec((1, 2, rows, lanes), lambda i, s: (i, 0, 0, 0))
    out_specs = [pl.BlockSpec((1,) + o.shape[1:], lambda i, s: (i, 0, 0)) for o in outs]
    scalars = spot.astype(jnp.int32)[None]
    return call(kernel, [keep, got], outs, (outer,), [block] * 2, out_specs, scalars, name="combine_rows")


class FeedSum:
    def __init__(self, send, keep):
        self.token = send
        self.mine = keep
        self.got = core_swap(send)

    def first_step(self, *tokens):
        total, inner, outer, z, y, core = places()
        got = hold(self.got, *tokens)
        groups, rows, lanes = got.shape
        self.ring = inner == 2
        if self.ring:
            split = (outer, inner, rows, lanes)
            low = rows * 2 // 5 // 16 * 16
            self.a, self.token, self.b, self.last = combine_rows(self.mine.reshape(split), got.reshape(split), y, low)
            self.got = lax.ppermute(self.token, "plots", [(i, i ^ 2) for i in range(total)])
        else:
            value = (self.mine.astype(f32) + got.astype(f32)).astype(bf)
            pairs = [[2 * g + c for g in range(groups)] for c in range(2)]
            self.token = value
            self.got = lax.psum_scatter(value, "plots", scatter_dimension=0, axis_index_groups=pairs, tiled=True)

    def outer_parts(self, mine, got):
        total, inner, outer, z, y, core = places()

        def part(at):
            one = lax.dynamic_index_in_dim(mine, at, 0, keepdims=False)
            two = lax.dynamic_index_in_dim(got, at, 0, keepdims=False)
            return (one.astype(f32) + two.astype(f32)).astype(bf)

        parts = [part((z + k) % outer) for k in range(1, outer)]
        self.token = parts[-1]
        return [part(z)] + [outer_shift(value, k + 1) for k, value in enumerate(parts)]

    def second_step(self, *tokens):
        if self.ring:
            self.a = self.outer_parts(self.a, hold(self.got, *tokens))
            total = lax.axis_size("plots")
            self.got = lax.ppermute(hold(self.last, self.token), "plots", [(i, i ^ 2) for i in range(total)])

    def third_step(self, *tokens):
        if self.ring:
            parts = lax.optimization_barrier((*self.a, *tokens))[: len(self.a)]
            self.a = sum(p.astype(f32) for p in parts).astype(bf)
            self.b = self.outer_parts(self.b, hold(self.got, self.a))

    def seq_step(self, *tokens):
        if self.ring:
            parts = lax.optimization_barrier((*self.b, *tokens))[: len(self.b)]
            self.mine = jnp.concatenate([self.a, sum(p.astype(f32) for p in parts).astype(bf)], 0)
        else:
            self.mine = hold(self.got, *tokens)[0]
        self.token = self.mine
        self.got = lax.ppermute(self.mine, "seq", SEQ_SWAP)

    def core_step(self, share, blocks, *tokens):
        core = lax.axis_index("plots") % 2
        value = self.mine.astype(f32) + hold(self.got, *tokens).astype(f32)
        lanes = value.shape[1]
        gate = value[: blocks * share].reshape(blocks, 2, share // 2, lanes).transpose(1, 2, 0, 3)
        gate = gate.reshape(2, share // 2, blocks * lanes)
        down = value[blocks * share :].T.reshape(2, lanes // 2, value.shape[0] - blocks * share)

        def trade(a):
            mine = lax.dynamic_index_in_dim(a, core, 0, keepdims=False)
            got = core_swap(lax.dynamic_index_in_dim(a, 1 - core, 0, keepdims=False).astype(bf)).astype(f32)
            return jnp.where(core == 0, mine, got), jnp.where(core == 0, got, mine)

        gate, up = trade(gate)
        return gate, up, jnp.concatenate(trade(down), 1)


def per_device(
    decoder_states,
    encoder_patches,
    token_lengths,
    patch_counts,
    self_gain,
    cross_gain,
    mlp_gain,
    self_query,
    self_key,
    self_value,
    self_output,
    cross_query,
    cross_key,
    cross_value,
    cross_output,
    mlp_gate,
    mlp_up,
    mlp_down,
    output_grad,
):
    plots, rows, width = decoder_states.shape
    assert plots == 1 and width == 64 * HEADS
    patch_rows = encoder_patches.shape[1]
    place = lax.axis_index("seq")
    token = jnp.arange(rows, dtype=jnp.int32)
    slot = jnp.arange(patch_rows, dtype=jnp.int32)

    def length_bias(valid):
        return jnp.broadcast_to(jnp.where(valid, 0.0, MASKED)[None, :], (8, valid.shape[0]))

    self_bias = length_bias(
        jnp.concatenate([(token < token_lengths[0]) & (place == 1), token + place * rows < token_lengths[0]])
    )
    cross_own = length_bias(slot + place * patch_rows < patch_counts[0])
    cross_far = length_bias(slot + (1 - place) * patch_rows < patch_counts[0])
    gain_one, gain_two, gain_three = (g.astype(f32)[None, :] for g in (self_gain, cross_gain, mlp_gain))
    scale = 0.125 * LOG2E

    x = decoder_states[0]
    patches = encoder_patches[0]
    dy = output_grad[0]
    far_x = lax.ppermute(x, "seq", [(0, 1)])
    self_rows = weight_rows(self_query, self_key, self_value)
    cross_rows = weight_rows(cross_query)
    feed_rows = weight_rows(mlp_gate, mlp_up)
    share = width // lax.axis_size("plots")
    spot = lax.axis_index("plots") * share
    self_part, cross_part, feed_part = (
        lax.dynamic_slice_in_dim(g, spot, share, 0) for g in (self_gain, cross_gain, mlp_gain)
    )
    x, self_bias, gain_two = lax.optimization_barrier((x, self_bias, gain_two))
    weights = [self_query, self_key, self_value, cross_key, cross_value]
    first, q1, k1, v1, k2, v2 = start(x, gain_one, patches, weights, scale)
    far_x = hold(far_x, k2)
    far_patches = lax.ppermute(hold(patches, k2), "seq", SEQ_SWAP)
    e1, f1, o1, y1, second, q2, far_first, far_k1, far_v1 = self_forward(
        q1, k1, v1, self_bias, far_x, gain_one, self_key, self_value, x, self_output, gain_two, cross_query, scale
    )
    e2, part2 = attend(q2, [k2], [v2], cross_own)
    far_patches = hold(far_patches, part2)
    part2, self_rows, cross_rows, feed_rows, cross_far, gain_three = lax.optimization_barrier(
        (part2, self_rows, cross_rows, feed_rows, cross_far, gain_three)
    )
    far_e2, f2, far_f2, o2, y2, third, hidden, dgu, far_k2, far_v2, send, keep = cross_forward(
        q2, far_patches, cross_key, cross_value, cross_far, part2, y1, cross_output, gain_three, mlp_gate, mlp_up,
        mlp_down, dy,
    )
    feed = FeedSum(send, keep)
    dgu = hold(dgu, feed.token)
    dy2, b2, do2 = feed_back(dgu, mlp_gate, mlp_up, y2, gain_three, dy, cross_output)
    feed.first_step(do2)
    do2 = hold(do2, feed.token)
    far_dq2, far_d2, far_patch_grad = cross_back_far(far_e2, do2, o2, far_f2, q2, far_k2, far_v2, cross_key, cross_value)
    feed.second_step(far_patch_grad)
    do2 = hold(do2, feed.token)
    near_patch_grad = lax.ppermute(far_patch_grad, "seq", SEQ_SWAP)
    d2, dy1, do1, *sends, keep = cross_back_own(
        e2, hold(do2, far_patch_grad), o2, f2, q2, k2, v2, far_dq2, gain_two, cross_query, y1, dy2, self_output, patches,
        far_patches, far_d2, second, b2, o1,
    )
    near_patch_grad = hold(near_patch_grad, dy1)
    cross = Sum(sends, keep)
    feed.third_step(dy1)
    layer_output = output(y2, hold(hidden, cross.token, feed.token), mlp_down)
    cross.inner_step(layer_output, near_patch_grad)
    do1 = hold(do1, cross.token)
    d1, *sends, keep, far_first_grad = self_back(
        e1, do1, o1, f1, q1, [far_k1, k1], [far_v1, v1], far_first, first, self_key, self_value
    )
    own = SeqFirstSum(sends, keep)
    feed.seq_step(own.token)
    own.seq_first_step(feed.token)
    feed.got = hold(feed.got, own.token)
    cross.outer_step(own.token, feed.got)
    patch_grad = key_value_back(hold(d2, cross.token), cross_key, cross_value, near_patch_grad)
    own.inner_step(patch_grad)
    near_first_grad = lax.ppermute(hold(far_first_grad, own.token), "seq", [(1, 0)])
    cross.seq_step(own.token)
    own.outer_step(cross.token)
    near_first_grad = hold(near_first_grad, own.token)
    input_grad = finish(d1, self_query, self_key, self_value, near_first_grad, x, gain_one, dy1)
    own.seq_step(input_grad)
    cross.core_step(own.token)
    groups = lax.axis_size("plots") // 2
    gate_sum, up_sum, down_sum = feed.core_step(width // groups, groups, cross.token)
    cross_key_grad, cross_value_grad, cross_query_grad, cross_output_grad, self_output_grad, cross_gain_grad = finalize(
        cross, [width, width], cross_rows, [2], cross_part
    )
    own.core_step(cross_gain_grad)
    query_grad, key_grad, value_grad, self_gain_grad = finalize(own, [width], self_rows, [0, 1, 2], self_part)
    feed_gain_grad = jnp.sum(feed_rows.astype(f32) * jnp.concatenate([gate_sum, up_sum], 1), axis=1)
    return (
        layer_output[None],
        input_grad[None],
        patch_grad[None],
        self_gain_grad.reshape(-1),
        cross_gain_grad.reshape(-1),
        feed_gain_grad / feed_part.astype(f32),
        query_grad,
        key_grad,
        value_grad,
        self_output_grad,
        cross_query_grad,
        cross_key_grad,
        cross_value_grad,
        cross_output_grad,
        gate_sum,
        up_sum,
        down_sum,
    )


def solution(mesh):
    rows = P("plots", "seq", None)
    placed = (rows, rows, P("plots"), P("plots")) + (P(),) * 14 + (rows,)
    return jax.shard_map(
        per_device,
        mesh=mesh,
        in_specs=placed,
        out_specs=(rows, rows, rows) + (P("plots"),) * 3 + (P("plots", None),) * 11,
        check_vma=False,
    )
```

```python
import functools

import jax
import jax.numpy as jnp
from jax import lax
from jax.experimental import pallas as pl
from jax.experimental.pallas import tpu as pltpu
from jax.sharding import PartitionSpec as P

HEADS = 12
eps = 1e-06
bf = jnp.bfloat16
f32 = jnp.float32
LOG2E = 1.4426950408889634
LN2 = 0.6931471805599453
MASKED = -1e30
NN = (((1,), (0,)), ((), ()))
NT = (((1,), (1,)), ((), ()))
TN = (((0,), (0,)), ((), ()))
TT = (((0,), (1,)), ((), ()))
SEQ_SWAP = [(0, 1), (1, 0)]


def dot(left, right, dims=NN):
    return lax.dot_general(left, right, dims, preferred_element_type=f32)


def lane_of(shape):
    return lax.broadcasted_iota(jnp.int32, shape, len(shape) - 1)


def head_lanes(lane, half):
    return (lane < 64) if half == 0 else (lane >= 64)


def lane_rows(half):
    lane = lane_of((1, 128))
    inside = jnp.where(head_lanes(lane, half), 1.0, 0.0)
    return inside.astype(bf), jnp.where(lane == 64 - 64 * half, 1.0, 0.0).astype(bf)


ANY = pl.BlockSpec(memory_space=pl.ANY)


def shape_of(shape, dtype=bf):
    return jax.ShapeDtypeStruct(shape, dtype)


def call(kernel, args, outs, grid=(1,), in_specs=None, out_specs=None, scalars=None, scratch=(), flops=0, name=None):
    def whole(a):
        zeros = (0,) * len(a.shape)
        return pl.BlockSpec(a.shape, lambda *_: zeros, pipeline_mode=pl.Buffered(1))

    def specs(given, arrays):
        given = given or [None] * len(arrays)
        return [whole(a) if s is None else s for s, a in zip(given, arrays)]

    grid_spec = pltpu.PrefetchScalarGridSpec(
        num_scalar_prefetch=0 if scalars is None else 1,
        grid=grid,
        in_specs=specs(in_specs, args),
        out_specs=specs(out_specs, outs),
        scratch_shapes=scratch,
    )
    nbytes = sum(a.size * a.dtype.itemsize for a in args) + sum(a.size * a.dtype.itemsize for a in outs)
    if scalars is not None:
        args = [scalars] + list(args)
    return pl.pallas_call(
        kernel,
        grid_spec=grid_spec,
        out_shape=outs,
        compiler_params=pltpu.CompilerParams(vmem_limit_bytes=58 << 20),
        cost_estimate=pl.CostEstimate(flops=flops, bytes_accessed=nbytes, transcendentals=0),
        name=name,
    )(*args)


def attend_kernel(causal, merge, parts, block, q_ref, bias_ref, *refs):
    key_refs, value_refs = refs[:parts], refs[parts : 2 * parts]
    refs = refs[2 * parts :]
    if merge:
        before_ref, e_ref, o_ref, own_ref, new_ref = refs
    elif parts > 1:
        e_ref, o_ref, own_ref = refs
    else:
        e_ref, o_ref = refs
    rows = q_ref.shape[0]
    pairs = q_ref.shape[1] // 128
    lane_b = lane_of((block, 128))
    first = head_lanes(lane_b, 0)
    full = (block, 128)
    items = [(p, b, half) for p in range(pairs) for b in range(rows // block) for half in range(2)]
    kept = {}

    def reaches(b):
        offset, found = 0, []
        for i, k_ref in enumerate(key_refs):
            keys = k_ref.shape[0]
            seen = min(keys, (b + 1) * block) if causal and i == parts - 1 else keys
            found.append((offset, i, seen))
            offset += keys
        return found

    def scores(item):
        p, b, half = item
        lanes = slice(128 * p, 128 * p + 128)
        q = q_ref[b * block : (b + 1) * block, lanes] * lane_rows(half)[0]
        found = []
        for offset, i, seen in reaches(b):
            s = dot(q, key_refs[i][:seen, lanes], NT) + bias_ref[0:1, offset : offset + seen]
            if causal and i == parts - 1:
                row = lax.broadcasted_iota(jnp.int32, s.shape, 0) + b * block
                s = jnp.where(lane_of(s.shape) <= row, s, MASKED)
            found.append(s)
        return found

    def soften(item, found):
        p, b, half = item
        top = functools.reduce(jnp.maximum, [jnp.max(s, axis=1, keepdims=True) for s in found])
        es = []
        for (offset, i, seen), s in zip(reaches(b), found):
            e = jnp.exp2(s - top).astype(bf)
            e_ref[2 * p + half, b * block : (b + 1) * block, offset : offset + seen] = e
            es.append(e)
        return top, es

    def mix(item, top, es):
        p, b, half = item
        lanes = slice(128 * p, 128 * p + 128)
        at = slice(b * block, (b + 1) * block)
        inside, at0 = lane_rows(half)
        spare = 64 - 64 * half
        o = None
        for (offset, i, seen), e in zip(reaches(b), es):
            part = dot(e, value_refs[i][:seen, lanes] * inside + at0)
            o = part if o is None else o + part
        if not merge and parts == 1:
            o_ref[2 * p + half, at, :] = jnp.where(lane_b == spare + 1, top, o)
            return
        l_new = jnp.broadcast_to(o[:, spare : spare + 1], full)
        if merge:
            old = before_ref[2 * p + half, at, :]
            l_old = jnp.broadcast_to(old[:, spare : spare + 1], full)
            m_old = jnp.broadcast_to(old[:, spare + 1 : spare + 2], full)
            top = jnp.broadcast_to(top, full)
            m = jnp.maximum(m_old, top)
            w_old, w_new = jnp.exp2(m_old - m), jnp.exp2(top - m)
            turn = 1.0 / (l_old * w_old + l_new * w_new)
            f_old, f_new = w_old * turn, w_new * turn
            o = old * f_old + o * f_new
        else:
            f_old = f_new = 1.0 / l_new
            o = o * f_new
        if half == 0:
            kept[p, b] = (o, f_old, f_new)
        else:
            o0, old0, new0 = kept.pop((p, b))
            o_ref[at, lanes] = jnp.where(first, o0, o).astype(bf)
            own_ref[at, lanes] = jnp.where(first, old0, f_old)
            if merge:
                new_ref[at, lanes] = jnp.where(first, new0, f_new)

    s = scores(items[0])
    waiting = None
    for i, item in enumerate(items):
        following = scores(items[i + 1]) if i + 1 < len(items) else None
        if waiting is not None:
            mix(*waiting)
        top, es = soften(item, s)
        waiting = (item, top, es)
        s = following
    mix(*waiting)


def attend(q, keys, values, bias, causal=False, before=None, block=256, group=1):
    rows, width = q.shape
    pairs = width // 128
    merge = before is not None
    total = sum(k.shape[0] for k in keys)

    def column(a):
        return pl.BlockSpec((a.shape[0], 128 * group), lambda p: (0, p))

    tall = column(q)
    e_spec = pl.BlockSpec((2 * group, rows, total), lambda p: (p, 0, 0))
    o_spec = pl.BlockSpec((2 * group, rows, 128), lambda p: (p, 0, 0))
    outs, out_specs = [shape_of((2 * pairs, rows, total))], [e_spec]
    args = [q, bias, *keys, *values]
    in_specs = [tall, None] + [column(a) for a in args[2:]]
    if merge:
        args.append(before)
        in_specs.append(o_spec)
    if merge or len(keys) > 1:
        outs += [shape_of((rows, width))] + [shape_of((rows, width), f32)] * (2 if merge else 1)
        out_specs += [tall] * (3 if merge else 2)
    else:
        outs.append(shape_of((2 * pairs, rows, 128), f32))
        out_specs.append(o_spec)
    return call(
        functools.partial(attend_kernel, causal, merge, len(keys), block),
        args,
        outs,
        (pairs // group,),
        in_specs,
        out_specs,
        flops=16 * rows * total * width,
        name="attend",
    )


def attend_back_kernel(causal, last, parts, block, e_ref, do_ref, o_ref, f_ref, q_ref, *refs):
    key_refs, value_refs = refs[:parts], refs[parts : 2 * parts]
    refs = refs[2 * parts :]
    if last:
        before_ref, dq_ref, d_ref = refs
    elif len(refs) == 2:
        dq_ref, d_ref = refs
    else:
        dq_ref, d_ref = None, refs[0]
    base = d_ref.shape[0] - 2
    rows = q_ref.shape[0]
    pairs = q_ref.shape[1] // 128
    lane_b = lane_of((block, 128))
    items = [(p, half, b) for p in range(pairs) for half in range(2) for b in range(rows // block)]
    dq, dk, dv = {}, {}, {}

    def reaches(b):
        offset, found = 0, []
        for i, k_ref in enumerate(key_refs):
            keys = k_ref.shape[0]
            seen = min(keys, (b + 1) * block) if causal and i == parts - 1 else keys
            found.append((offset, i, seen))
            offset += keys
        return found

    def slopes(item):
        p, half, b = item
        lanes = slice(128 * p, 128 * p + 128)
        at = slice(b * block, (b + 1) * block)
        inb = head_lanes(lane_b, half)
        do = do_ref[at, lanes].astype(f32)
        f = f_ref[at, lanes]
        inner = jnp.sum(jnp.where(inb, do * o_ref[at, lanes].astype(f32), 0.0), axis=1, keepdims=True)
        off = inner * f[:, 64 * half : 64 * half + 1]
        dos = jnp.where(inb, do * f, 0.0).astype(bf)
        return dos, off, [dot(dos, value_refs[i][:seen, lanes], NT) for offset, i, seen in reaches(b)]

    def spread(item, dos, off, dps):
        p, half, b = item
        lanes = slice(128 * p, 128 * p + 128)
        at = slice(b * block, (b + 1) * block)
        q = q_ref[at, lanes]
        for (offset, i, seen), dp in zip(reaches(b), dps):
            e = e_ref[2 * p + half, at, offset : offset + seen]
            ds = (e.astype(f32) * (dp - off)).astype(bf)
            part = dot(ds, key_refs[i][:seen, lanes] * lane_rows(half)[0])
            dq[p, b] = part if (p, b) not in dq else dq[p, b] + part
            step = block if causal and i == parts - 1 else seen
            for c in range(0, seen, step):
                key = (p, half, offset + c)
                vt = dot(dos, e[:, c : c + step], TN)
                kt = dot(q, ds[:, c : c + step], TN)
                dv[key] = vt if key not in dv else dv[key] + vt
                dk[key] = kt if key not in dk else dk[key] + kt

    ready = slopes(items[0])
    for i, item in enumerate(items):
        following = slopes(items[i + 1]) if i + 1 < len(items) else None
        spread(item, *ready)
        ready = following
    for p, b in dq:
        lanes = slice(128 * p, 128 * p + 128)
        at = slice(b * block, (b + 1) * block)
        part = dq[p, b]
        if last:
            dq_ref[at, lanes] = ((part + before_ref[at, lanes]) * 0.125).astype(bf)
        elif base == 0:
            dq_ref[at, lanes] = part
        else:
            d_ref[0, lanes, d_ref.shape[2] - rows + b * block : d_ref.shape[2] - rows + (b + 1) * block] = (
                part.T * 0.125
            ).astype(bf)
    for p, half, c in dk:
        wide = dk[p, half, c].shape[1]
        inside = slice(64 * half, 64 * half + 64)
        at = slice(128 * p + 64 * half, 128 * p + 64 * half + 64)
        d_ref[base, at, c : c + wide] = (dk[p, half, c][inside] * LN2).astype(bf)
        d_ref[base + 1, at, c : c + wide] = dv[p, half, c][inside].astype(bf)


def attend_back(e, do, o, f, q, keys, values, causal=False, before=None, whole=False, block=256, group=1):
    rows, width = q.shape
    pairs = width // 128
    total = sum(k.shape[0] for k in keys)

    def column(a):
        return pl.BlockSpec((a.shape[0], 128 * group), lambda p: (0, p))

    tall = column(q)
    args = [e, do, o, f, q, *keys, *values]
    in_specs = [pl.BlockSpec((2 * group, rows, total), lambda p: (p, 0, 0))] + [column(a) for a in args[1:]]
    if before is not None:
        args.append(before)
        in_specs.append(tall)
    return call(
        functools.partial(attend_back_kernel, causal, before is not None, len(keys), block),
        args,
        ([] if whole else [shape_of((rows, width), f32 if before is None else bf)])
        + [shape_of((2 + whole, width, total))],
        (pairs // group,),
        in_specs,
        ([] if whole else [tall]) + [pl.BlockSpec((2 + whole, 128 * group, total), lambda p: (0, p, 0))],
        flops=16 * rows * total * width,
        name="attend_back",
    )


def late(refs, buffers, sems):
    copies = [pltpu.make_async_copy(ref, buffer, sems.at[i]) for i, (ref, buffer) in enumerate(zip(refs, buffers))]

    @pl.when(pl.program_id(0) == 0)
    def _():
        for copy in copies:
            copy.start()

    def fetch(i):
        copies[i].wait()
        return buffers[i]

    return fetch


def self_back(e, do, o, f, q, keys, values, far_first, first, wk, wv):
    rows, width = q.shape
    pairs = width // 128
    total = 2 * rows
    half = width // 2
    pieces = (width + half) // 128
    back = functools.partial(attend_back_kernel, True, False, 2, 256)

    def kernel(core_ref, *refs):
        blocks, (ff_ref, first_ref, wk_ref, wv_ref) = refs[:9], refs[9:13]
        d_ref, *send_refs, keep_ref, out_ref = refs[13 : 16 + pieces]
        all_ref, part_ref, *buffers, sems = refs[16 + pieces :]
        fetch = late([ff_ref, first_ref, wk_ref, wv_ref], buffers, sems)
        i = pl.program_id(0)
        core = core_ref[0]

        @pl.when(i < pairs)
        def _():
            back(*blocks, part_ref)
            d_ref[...] = part_ref[:, :, rows:]
            all_ref[:, pl.ds(pl.multiple_of(i * 128, 128), 128), :] = part_ref[...]

        @pl.when(i == pairs)
        def _():
            far, own = fetch(0)[...], fetch(1)[...]
            query = dot(own, all_ref[0, :, rows:], TT)
            key = dot(far, all_ref[1, :, :rows], TT) + dot(own, all_ref[1, :, rows:], TT)
            halves(send_refs, keep_ref, core, 0, query, key)

        @pl.when(i == pairs + 1)
        def _():
            far, own = buffers[0][...], buffers[1][...]
            value = dot(far, all_ref[2, :, :rows], TT) + dot(own, all_ref[2, :, rows:], TT)
            halves(send_refs, keep_ref, core, width, value[:, :half], value[:, half:])
            grad = dot(all_ref[1, :, :rows], fetch(2)[...], TT) + dot(all_ref[2, :, :rows], fetch(3)[...], TT)
            out_ref[...] = grad.astype(bf)

    def column(a):
        return pl.BlockSpec((a.shape[0], 128), lambda i, s: (0, jnp.minimum(i, pairs - 1)))

    args = [e, do, o, f, q, *keys, *values, far_first, first, wk, wv]
    in_specs = [pl.BlockSpec((2, rows, total), lambda i, s: (jnp.minimum(i, pairs - 1), 0, 0))]
    in_specs += [column(a) for a in args[1:9]] + [pl.BlockSpec(memory_space=pl.ANY)] * 4
    own = pl.BlockSpec((3, 128, rows), lambda i, s: (0, jnp.minimum(i, pairs - 1), 0))
    return call(
        kernel,
        args,
        [shape_of((3, width, rows))]
        + [shape_of((width, 128))] * pieces
        + [shape_of((width, width + half)), shape_of((rows, width))],
        (pairs + 2,),
        in_specs,
        [own] + [None] * (pieces + 2),
        core_scalar(),
        scratch=[pltpu.VMEM((3, width, total), bf), pltpu.VMEM((3, 128, total), bf)]
        + [pltpu.VMEM(a.shape, bf) for a in args[9:]]
        + [pltpu.SemaphoreType.DMA((4,))],
        flops=16 * rows * total * width + 12 * rows * width * width,
        name="self_back",
    )


def cross_back_far(e, do, o, f, q, k, v, wk, wv):
    rows, width = q.shape
    pairs = width // 128
    keys = k.shape[0]
    half = keys // 2

    def kernel(*refs):
        blocks, (wk_ref, wv_ref), (dq_ref, d_ref, out_ref) = refs[:7], refs[7:9], refs[9:12]
        all_ref, *buffers, sems = refs[12:]
        fetch = late([wk_ref, wv_ref], buffers, sems)
        i = pl.program_id(0)

        @pl.when(i < pairs)
        def _():
            attend_back_kernel(False, False, 1, 512, *blocks, dq_ref, d_ref)
            all_ref[:, pl.ds(pl.multiple_of(i * 128, 128), 128), :] = d_ref[...]

        @pl.when(i == pairs)
        def _():
            fetch(0), fetch(1)

        @pl.when(i >= pairs)
        def _():
            at = pl.ds(pl.multiple_of((i - pairs) * half, half), half)
            grad = dot(all_ref[0, :, at], buffers[0][...], TT) + dot(all_ref[1, :, at], buffers[1][...], TT)
            out_ref[...] = grad.astype(bf)

    def spot(i):
        return jnp.minimum(i, pairs - 1)

    def column(a):
        return pl.BlockSpec((a.shape[0], 128), lambda i: (0, spot(i)))

    args = [e, do, o, f, q, k, v, wk, wv]
    return call(
        kernel,
        args,
        [shape_of((rows, width), f32), shape_of((2, width, keys)), shape_of((keys, width))],
        (pairs + 2,),
        [pl.BlockSpec((2, rows, keys), lambda i: (spot(i), 0, 0))] + [column(a) for a in args[1:7]] + [ANY] * 2,
        [column(q), pl.BlockSpec((2, 128, keys), lambda i: (0, spot(i), 0))]
        + [pl.BlockSpec((half, width), lambda i: (jnp.maximum(i - pairs, 0), 0))],
        scratch=[pltpu.VMEM((2, width, keys), bf)] + [pltpu.VMEM(wk.shape, bf)] * 2 + [pltpu.SemaphoreType.DMA((2,))],
        flops=16 * rows * keys * width + 4 * keys * width * width,
        name="cross_back_far",
    )


def cross_back_own(e, do, o, f, q, k, v, before, gain, wq, y1, dy2, wo, patches, far_patches, far_d, second, b2, o1):
    rows, width = q.shape
    pairs = width // 128
    keys = k.shape[0]
    half = width // 2
    chunk = 512
    parts = keys // chunk

    def kernel(core_ref, *refs):
        blocks, gain_ref, late_refs = refs[:8], refs[8], refs[9:20]
        d_ref, dy1_ref, do1_ref, *send_refs, keep_ref = refs[20:29]
        all_ref, dq_ref, acc_ref, b1_ref, *buffers, sems = refs[29:]
        fetch = late(late_refs, buffers, sems)
        i = pl.program_id(0)
        core = core_ref[0]

        @pl.when(i < pairs)
        def _():
            at = pl.ds(pl.multiple_of(i * 128, 128), 128)
            attend_back_kernel(False, True, 1, 256, *blocks, dq_ref.at[:, at], d_ref)
            all_ref[:, at, :] = d_ref[...]

        @pl.when(i == pairs)
        def _():
            for j in range(11):
                fetch(j)
            grad = dot(dq_ref[...], buffers[0][...], NT)
            unit, scale = norm_parts(buffers[1][...])
            dy1 = buffers[2][...] + norm_back(unit, scale, gain_ref[...], grad)
            dy1_ref[...] = dy1
            b1_ref[...] = dy1.astype(bf)
            do1_ref[...] = dot(b1_ref[...], buffers[3][...], NT).astype(bf)
            acc_ref[...] = jnp.zeros_like(acc_ref)

        @pl.when((i > pairs) & (i <= pairs + parts))
        def _():
            at = pl.ds(pl.multiple_of((i - pairs - 1) * chunk, chunk), chunk)

            @pl.loop(0, 2)
            def _(j):
                left, far = buffers[4][at, :], buffers[5][at, :]
                acc_ref[j] += dot(left, all_ref[j, :, at], TT) + dot(far, buffers[6][j, :, at], TT)

        @pl.when(i == pairs + parts + 1)
        def _():
            halves(send_refs, keep_ref, core, 0, acc_ref[0], acc_ref[1])
            query, output = dot(buffers[7][...], dq_ref[...], TN), dot(buffers[10][...], buffers[8][...], TN)
            halves(send_refs, keep_ref, core, width, query, output)
            value = dot(buffers[9][...], b1_ref[...], TN)
            halves(send_refs, keep_ref, core, 2 * width, value[:, :half], value[:, half:])

    def spot(i):
        return jnp.minimum(i, pairs - 1)

    def column(a):
        return pl.BlockSpec((a.shape[0], 128), lambda i, s: (0, spot(i)))

    lates = [wq, y1, dy2, wo, patches, far_patches, far_d, second, b2, o1, o]
    args = [e, do, o, f, q, k, v, before, gain] + lates
    full = shape_of((rows, width), f32)
    return call(
        kernel,
        args,
        [shape_of((2, width, keys)), full, shape_of((rows, width))]
        + [shape_of((width, half))] * 5
        + [shape_of((width, 2 * width + half))],
        (pairs + parts + 2,),
        [pl.BlockSpec((2, rows, keys), lambda i, s: (spot(i), 0, 0))]
        + [column(a) for a in args[1:8]]
        + [None]
        + [ANY] * 11,
        [pl.BlockSpec((2, 128, keys), lambda i, s: (0, spot(i), 0))] + [None] * 8,
        core_scalar(),
        scratch=[
            pltpu.VMEM((2, width, keys), bf),
            pltpu.VMEM((rows, width), bf),
            pltpu.VMEM((2, width, width), f32),
            pltpu.VMEM((rows, width), bf),
        ]
        + [pltpu.VMEM(a.shape, a.dtype) for a in lates]
        + [pltpu.SemaphoreType.DMA((11,))],
        flops=16 * rows * keys * width + 2 * width * width * (5 * rows + 4 * keys),
        name="cross_back_own",
    )


def rows_loop(out_ref, left_ref, w_ref, finish=lambda v: v):
    @pl.loop(0, left_ref.shape[0] // 256)
    def _(i):
        at = pl.ds(pl.multiple_of(i * 256, 256), 256)
        out_ref[at, :] = finish(dot(left_ref[at, :], w_ref[...])).astype(out_ref.dtype)


def norm_parts(value):
    scale = lax.rsqrt(jnp.mean(value * value, axis=-1, keepdims=True) + eps)
    return value * scale, scale


def norm_back(unit, scale, gain, grad):
    inner = gain * grad
    return scale * (inner - unit * jnp.mean(inner * unit, axis=-1, keepdims=True))


def gelu_parts(u):
    t = jnp.tanh(0.7978845608028654 * (u + 0.044715 * u * u * u))
    value = 0.5 * u * (1.0 + t)
    slope = 0.5 * (1.0 + t) + 0.5 * u * (1.0 - t * t) * (0.7978845608028654 * (1.0 + 3 * 0.044715 * u * u))
    return value, slope


def start(x, gain, patches, weights, scale):
    def kernel(gain_ref, x_ref, w0, w1, w2, p_ref, w3, w4, *refs):
        outs, refs = refs[:6], refs[6:]
        ins, results, in_sems, out_sems = refs[:7], refs[7:13], refs[13], refs[14]
        loads = [
            pltpu.make_async_copy(ref, buffer, in_sems.at[i])
            for i, (ref, buffer) in enumerate(zip((x_ref, w0, w1, w2, p_ref, w3, w4), ins))
        ]
        stores = [
            pltpu.make_async_copy(buffer, ref, out_sems.at[i]) for i, (buffer, ref) in enumerate(zip(results, outs))
        ]
        loads[0].start()
        loads[1].start()
        loads[0].wait()
        for load in loads[2:]:
            load.start()
        first = (norm_parts(ins[0][...].astype(f32))[0] * gain_ref[...]).astype(bf)
        results[0][...] = first
        stores[0].start()
        for j in range(3):
            loads[1 + j].wait()
            rows_loop(results[1 + j], results[0], ins[1 + j], (lambda v: v * scale) if j == 0 else (lambda v: v))
            stores[1 + j].start()
        loads[4].wait()
        for j in range(2):
            loads[5 + j].wait()
            rows_loop(results[4 + j], ins[4], ins[5 + j])
            stores[4 + j].start()
        for store in stores:
            store.wait()

    args = [gain, x, *weights[:3], patches, *weights[3:]]
    outs = [shape_of(x.shape)] * 4 + [shape_of(patches.shape)] * 2
    return call(
        kernel,
        args,
        outs,
        in_specs=[None] + [ANY] * 7,
        out_specs=[ANY] * 6,
        scratch=[pltpu.VMEM(a.shape, bf) for a in args[1:] + outs]
        + [pltpu.SemaphoreType.DMA((7,)), pltpu.SemaphoreType.DMA((6,))],
        flops=2 * 768 * (3 * x.size + 2 * patches.size),
        name="start",
    )


def self_forward(q, k, v, bias, far_x, gain, wk, wv, x, w_out, next_gain, w_query, scale):
    rows, width = q.shape
    pairs = width // 128
    total = 2 * rows

    def kernel(q_ref, k_ref, v_ref, bias_ref, fx_ref, gain_ref, wk_ref, wv_ref, ng_ref, x_ref, wo_ref, wq_ref, *refs):
        e_ref, f_ref, o_ref, y_ref, n_ref, q2_ref, *far_out = refs[:9]
        far_first, far_k, far_v, *buffers, sems, out_sems = refs[9:]
        fetch = late([x_ref, wo_ref, wq_ref], buffers, sems)
        stores = [
            pltpu.make_async_copy(buffer, ref, out_sems.at[j])
            for j, (buffer, ref) in enumerate(zip((far_first, far_k, far_v), far_out))
        ]
        i = pl.program_id(0)

        @pl.when(i == 0)
        def _():
            far_first[...] = (norm_parts(fx_ref[...].astype(f32))[0] * gain_ref[...]).astype(bf)
            rows_loop(far_k, far_first, wk_ref)
            rows_loop(far_v, far_first, wv_ref)
            for store in stores:
                store.start()

        @pl.when((i > 0) & (i <= pairs))
        def _():
            at = pl.ds(pl.multiple_of((i - 1) * 128, 128), 128)
            refs = far_k.at[:, at], k_ref, far_v.at[:, at], v_ref
            attend_kernel(True, False, 2, 256, q_ref, bias_ref, *refs, e_ref, o_ref.at[:, at], f_ref)

        @pl.when(i == pairs + 1)
        def _():
            y = fetch(0)[...].astype(f32) + dot(o_ref[...], fetch(1)[...])
            y_ref[...] = y
            n_ref[...] = (norm_parts(y)[0] * ng_ref[...]).astype(bf)
            q2_ref[...] = (dot(n_ref[...], fetch(2)[...]) * scale).astype(bf)
            for store in stores:
                store.wait()

    def spot(i):
        return jnp.clip(i - 1, 0, pairs - 1)

    column = pl.BlockSpec((rows, 128), lambda i: (0, spot(i)))
    args = [q, k, v, bias, far_x, gain, wk, wv, next_gain, x, w_out, w_query]
    flat = shape_of((rows, width))
    return call(
        kernel,
        args,
        [shape_of((2 * pairs, rows, total)), shape_of((rows, width), f32), flat, shape_of((rows, width), f32)]
        + [flat] * 5,
        (pairs + 2,),
        [column] * 3 + [None] * 6 + [ANY] * 3,
        [pl.BlockSpec((2, rows, total), lambda i: (spot(i), 0, 0)), column] + [None] * 4 + [ANY] * 3,
        scratch=[pltpu.VMEM((rows, width), bf)] * 3
        + [pltpu.VMEM(a.shape, bf) for a in args[9:]]
        + [pltpu.SemaphoreType.DMA((3,)), pltpu.SemaphoreType.DMA((3,))],
        flops=16 * rows * total * width + 8 * rows * width * width,
        name="self_forward",
    )


def cross_forward(q, patches, wk, wv, bias, before, y1, w_out, gain, w_gate, w_up, w_down, dy):
    total, inner, outer, *_ = places()
    groups = inner * outer
    rows, width = q.shape
    keys = patches.shape[0]
    pairs = width // 128
    hidden = w_gate.shape[1]
    share, lanes = width // groups, hidden // groups
    blocks, step = hidden // lanes, 512
    per, chunks = step // lanes, hidden // step
    half = width // 2
    grouped = lanes % 128 == 0 and share % 16 == 0

    def kernel(core_ref, q_ref, bias_ref, before_ref, gain_ref, p_ref, wk_ref, wv_ref, *refs):
        late_refs, refs = refs[:6], refs[6:]
        e_ref, own_ref, new_ref, o_ref, y2_ref, third_ref, h_ref, d_ref, *outs = refs[:12]
        k_ref, v_ref, send_ref, keep_ref, *buffers, sems, out_sems, grad_sems = refs[12:]
        fetch = late(late_refs, buffers, sems)
        stores = [
            pltpu.make_async_copy(buffer, ref, out_sems.at[j])
            for j, (buffer, ref) in enumerate(zip((k_ref, v_ref), outs))
        ]
        i = pl.program_id(0)
        here = core_ref[0] == 0

        def grad_stores(c):
            if grouped:
                rows = pl.ds(pl.multiple_of(c * per * share, per * share), per * share)
                regions = [(slice(None), rows), (pl.ds(c * per, per), slice(blocks * share, blocks * share + half))]
            else:
                regions = [(slice(None), pl.ds(pl.multiple_of(c * step, step), step))]
            return [
                pltpu.make_async_copy(buffer.at[at], ref.at[at], grad_sems.at[c, 2 * j + k])
                for j, (buffer, ref) in enumerate(zip((send_ref, keep_ref), outs[2:]))
                for k, at in enumerate(regions)
            ]

        @pl.when(i == 0)
        def _():
            rows_loop(k_ref, p_ref, wk_ref)
            rows_loop(v_ref, p_ref, wv_ref)
            stores[0].start()
            stores[1].start()

        @pl.when((i > 0) & (i <= pairs))
        def _():
            at = pl.ds(pl.multiple_of((i - 1) * 128, 128), 128)
            refs = k_ref.at[:, at], v_ref.at[:, at], before_ref, e_ref, o_ref.at[:, at], own_ref, new_ref
            attend_kernel(False, True, 1, rows, q_ref, bias_ref, *refs)

        @pl.when(i == pairs + 1)
        def _():
            y2 = fetch(0)[...] + dot(o_ref[...], fetch(1)[...])
            y2_ref[...] = y2
            third_ref[...] = (norm_parts(y2)[0] * gain_ref[...]).astype(bf)
            for j in range(2, 6):
                fetch(j)

        @pl.when(i > pairs)
        def _():
            c = i - pairs - 1
            at = pl.ds(pl.multiple_of(c * step, step), step)
            wg_ref, wu_ref, wd_ref, dy_ref = buffers[2:]
            low = rows // 2

            @pl.loop(0, 2)
            def _(r):
                part = pl.ds(pl.multiple_of(r * low, low), low)
                third = third_ref[part, :]
                gate = dot(third, wg_ref[:, at])
                up = dot(third, wu_ref[:, at])
                dhidden = dot(dy_ref[part, :], wd_ref[at, :], NT)
                act, slope = gelu_parts(gate)
                h_ref[part, :] = (act * up).astype(bf)
                d_ref[0, part, :] = (dhidden * up * slope).astype(bf)
                d_ref[1, part, :] = (dhidden * act).astype(bf)

            third = third_ref[...]
            gate, up = dot(third, d_ref[0], TN), dot(third, d_ref[1], TN)
            send, keep = jnp.where(here, up, gate).astype(bf), jnp.where(here, gate, up).astype(bf)
            for g in range(groups if grouped else 0):
                from_rows = slice(g * share, (g + 1) * share)
                for j in range(per):
                    to = pl.ds(pl.multiple_of((c * per + j) * share, share), share)
                    send_ref[g, to, :] = send[from_rows, j * lanes : (j + 1) * lanes]
                    keep_ref[g, to, :] = keep[from_rows, j * lanes : (j + 1) * lanes]
            if not grouped:
                send_ref[:width, at] = send
                keep_ref[:width, at] = keep
            down = dot(dy_ref[...], h_ref[...], TN)
            send, keep = jnp.where(here, down[half:], down[:half]), jnp.where(here, down[:half], down[half:])
            if not grouped:
                send_ref[width:, at] = send.astype(bf)
                keep_ref[width:, at] = keep.astype(bf)
            to = slice(blocks * share, blocks * share + half)
            for j in range(per if grouped else 0):
                send_ref[c * per + j, to, :] = send[:, j * lanes : (j + 1) * lanes].astype(bf)
                keep_ref[c * per + j, to, :] = keep[:, j * lanes : (j + 1) * lanes].astype(bf)
            for store in grad_stores(c):
                store.start()

        @pl.when(i == pairs + chunks)
        def _():
            for store in stores:
                store.wait()
            for c in range(chunks):
                for store in grad_stores(c):
                    store.wait()

    def spot(i):
        return jnp.clip(i - 1, 0, pairs - 1)

    def chunk(i):
        return jnp.clip(i - 1 - pairs, 0, chunks - 1)

    column = pl.BlockSpec((rows, 128), lambda i, s: (0, spot(i)))
    args = [q, bias, before, gain, patches, wk, wv, y1, w_out, w_gate, w_up, w_down, dy]
    flat, key, full = shape_of((rows, width)), shape_of((keys, width)), shape_of((rows, width), f32)
    grads = shape_of((groups, blocks * share + half, lanes) if grouped else (width + half, hidden))
    *outs, send, keep = call(
        kernel,
        args,
        [shape_of((2 * pairs, rows, keys)), full, full, flat, full, flat]
        + [shape_of((rows, hidden)), shape_of((2, rows, hidden)), key, key, grads, grads],
        (pairs + 1 + chunks,),
        [column, None, pl.BlockSpec((2, rows, 128), lambda i, s: (spot(i), 0, 0))] + [None] * 4 + [ANY] * 6,
        [pl.BlockSpec((2, rows, keys), lambda i, s: (spot(i), 0, 0)), column, column, None, None, None]
        + [pl.BlockSpec((rows, step), lambda i, s: (0, chunk(i)))]
        + [pl.BlockSpec((2, rows, step), lambda i, s: (0, 0, chunk(i)))]
        + [ANY] * 4,
        core_scalar(),
        scratch=[pltpu.VMEM(a.shape, bf) for a in (key, key, grads, grads)]
        + [pltpu.VMEM(a.shape, a.dtype) for a in args[7:]]
        + [pltpu.SemaphoreType.DMA((6,)), pltpu.SemaphoreType.DMA((2,)), pltpu.SemaphoreType.DMA((chunks, 4))],
        flops=16 * rows * keys * width + 4 * keys * width * width + 12 * rows * width * hidden,
        name="cross_forward",
    )

    def group(value):
        if grouped:
            return value
        gate = value[:width].reshape(groups, share, blocks, lanes).swapaxes(1, 2).reshape(groups, -1, lanes)
        return jnp.concatenate([gate, value[width:].reshape(half, groups, lanes).swapaxes(0, 1)], 1)

    return *outs, group(send), group(keep)


def feed_back(d, w_gate, w_up, y2, gain, dy, w_out):
    def kernel(d_ref, wg_ref, wu_ref, gain_ref, y2_ref, dy_ref, wo_ref, dy2_ref, b_ref, do_ref, acc_ref, *refs):
        *buffers, sems = refs
        fetch = late([y2_ref, dy_ref, wo_ref], buffers, sems)
        i = pl.program_id(0)
        part = dot(d_ref[0], wg_ref[...], NT) + dot(d_ref[1], wu_ref[...], NT)

        @pl.when(i == 0)
        def _():
            acc_ref[...] = part

        @pl.when(i > 0)
        def _():
            acc_ref[...] += part

        @pl.when(i == pl.num_programs(0) - 1)
        def _():
            grad = acc_ref[...]
            unit, scale = norm_parts(fetch(0)[...])
            dy2 = fetch(1)[...].astype(f32) + norm_back(unit, scale, gain_ref[...], grad)
            dy2_ref[...] = dy2
            b_ref[...] = dy2.astype(bf)
            do_ref[...] = dot(b_ref[...], fetch(2)[...], NT).astype(bf)

    rows, width = y2.shape
    hidden = w_gate.shape[1]
    column = pl.BlockSpec((width, 512), lambda i: (0, i))
    return call(
        kernel,
        [d, w_gate, w_up, gain, y2, dy, w_out],
        [shape_of(y2.shape, f32), shape_of(y2.shape), shape_of(y2.shape)],
        (hidden // 512,),
        [pl.BlockSpec((2, rows, 512), lambda i: (0, 0, i)), column, column, None, ANY, ANY, ANY],
        scratch=[pltpu.VMEM((rows, width), f32)]
        + [pltpu.VMEM(a.shape, a.dtype) for a in (y2, dy, w_out)]
        + [pltpu.SemaphoreType.DMA((3,))],
        flops=2 * y2.size * (768 + 2 * hidden),
        name="feed_back",
    )


def finish(d, wq, wk, wv, near, x, gain, dy1):
    def kernel(d_ref, wq_ref, wk_ref, wv_ref, near_ref, x_ref, gain_ref, dy_ref, out_ref):
        grad = near_ref[...].astype(f32)
        for j, w_ref in enumerate((wq_ref, wk_ref, wv_ref)):
            grad = grad + dot(d_ref[j], w_ref[...], TT)
        unit, scale = norm_parts(x_ref[...].astype(f32))
        out_ref[...] = (dy_ref[...] + norm_back(unit, scale, gain_ref[...], grad)).astype(bf)

    rows = x.shape[0]
    return call(
        kernel, [d, wq, wk, wv, near, x, gain, dy1], [shape_of(x.shape)], (1,),
        flops=6 * x.size * 768, name="finish",
    )[0]


def output(y2, hidden, w_down):
    def kernel(y_ref, h_ref, w_ref, out_ref):
        out_ref[...] = (y_ref[...] + dot(h_ref[...], w_ref[...])).astype(bf)

    rows, width = y2.shape
    half = pl.BlockSpec((rows, width // 2), lambda i: (0, i))
    return call(
        kernel, [y2, hidden, w_down], [shape_of(y2.shape)], (2,),
        [half, None, pl.BlockSpec((hidden.shape[1], width // 2), lambda i: (0, i))], [half],
        flops=2 * hidden.size * width, name="output",
    )[0]


def key_value_back(d, wk, wv, near):
    keys = d.shape[2]
    half = keys // 2

    def kernel(d_ref, wk_ref, wv_ref, near_ref, out_ref):
        grad = dot(d_ref[0], wk_ref[...], TT) + dot(d_ref[1], wv_ref[...], TT)
        out_ref[...] = (grad + near_ref[...].astype(f32)).astype(bf)

    rows = pl.BlockSpec((half, wk.shape[0]), lambda i: (i, 0))
    part = pl.BlockSpec((2, d.shape[1], half), lambda i: (0, 0, i))
    return call(
        kernel, [d, wk, wv, near], [shape_of((keys, wk.shape[0]))], (2,), [part, None, None, rows], [rows],
        flops=4 * keys * 768 * 768, name="key_value_back",
    )[0]


def ring_factors(groups):
    inner = 1
    while inner * inner * 4 <= groups:
        inner *= 2
    return inner, groups // inner


def places():
    total = lax.axis_size("plots")
    index = lax.axis_index("plots")
    inner, outer = ring_factors(total // 2)
    group = index // 2
    return total, inner, outer, group // inner, group % inner, index % 2


def core_swap(value):
    total = lax.axis_size("plots")
    return lax.ppermute(value, "plots", [(i, i ^ 1) for i in range(total)])


def outer_shift(value, k):
    total, inner, outer, *_ = places()
    stride = 2 * inner
    return lax.ppermute(value, "plots", [(i, ((i // stride + k) % outer) * stride + i % stride) for i in range(total)])


def inner_shift(value, k):
    total, inner, outer, *_ = places()

    def spot(i):
        y = (i // 2) % inner
        return i + ((y + k) % inner - y) * 2

    return lax.ppermute(value, "plots", [(i, spot(i)) for i in range(total)])


def hold(value, *tokens):
    return lax.optimization_barrier((value,) + tokens)[0]


def halves(send_refs, keep_ref, core, start, one, two):
    here = core == 0
    send = jnp.where(here, two, one).astype(bf)
    keep_ref[:, start : start + one.shape[1]] = jnp.where(here, one, two).astype(bf)
    wide = send_refs[0].shape[1]
    for c in range(0, one.shape[1], wide):
        send_refs[(start + c) // wide][...] = send[:, c : c + wide]


def core_scalar():
    return (lax.axis_index("plots") % 2).astype(jnp.int32)[None]


def combine(keep, pieces, spot):
    outer, inner, share, columns = keep.shape

    def kernel(y_ref, keep_ref, *refs):
        *piece_refs, mine_ref, send_ref = refs
        y = y_ref[0]

        @pl.loop(0, outer // steps)
        def _(i):
            start = 0
            for ref in piece_refs:
                at = slice(start, start + ref.shape[3])
                start += ref.shape[3]
                one = keep_ref[i, 0, :, at].astype(f32) + ref[i, 0].astype(f32)
                two = keep_ref[i, 1, :, at].astype(f32) + ref[i, 1].astype(f32)
                mine_ref[i, :, at] = jnp.where(y == 0, one, two).astype(bf)
                send_ref[i, :, at] = jnp.where(y == 0, two, one).astype(bf)

    steps = 2

    def block(a):
        return pl.BlockSpec((outer // steps,) + a.shape[1:], lambda i, s: (i,) + (0,) * (len(a.shape) - 1))

    args = [keep] + [p.reshape(outer, inner, share, p.shape[1]) for p in pieces]
    out = shape_of((outer, share, columns))
    return call(
        kernel, args, [out, out], (steps,), [block(a) for a in args], [block(out)] * 2,
        spot.astype(jnp.int32)[None], name="combine",
    )


class Sum:
    def __init__(self, sends, keep):
        self.token = sends[-1]
        self.mine = keep
        self.got = [core_swap(send) for send in sends]

    def inner_step(self, *tokens):
        total, inner, outer, z, y, core = places()
        split = (outer, inner, self.mine.shape[0] // (outer * inner), self.mine.shape[1])
        mine = self.mine.reshape(split)
        got = lax.optimization_barrier(tuple(self.got) + tokens)[: len(self.got)]
        if inner == 2:
            self.mine, self.token = combine(mine, got, y)
            self.got = lax.ppermute(self.token, "plots", [(i, i ^ 2) for i in range(total)])
        else:
            got = jnp.concatenate(got, 1).reshape(split)
            groups = [[(o * inner + i) * 2 + c for i in range(inner)] for o in range(outer) for c in range(2)]
            self.token = (mine.astype(f32) + got.astype(f32)).astype(bf)
            self.mine = None
            self.got = lax.all_to_all(self.token, "plots", 1, 1, axis_index_groups=groups, tiled=True)

    def outer_step(self, *tokens):
        total, inner, outer, z, y, core = places()
        got = hold(self.got, *tokens)

        def part(at):
            if self.mine is None:
                value = lax.dynamic_index_in_dim(got, at, 0, keepdims=False)
                return jnp.sum(value.astype(f32), axis=0).astype(bf)
            one = lax.dynamic_index_in_dim(self.mine, at, 0, keepdims=False)
            two = lax.dynamic_index_in_dim(got, at, 0, keepdims=False)
            return (one.astype(f32) + two.astype(f32)).astype(bf)

        self.parts = [part((z + k) % outer) for k in range(1, outer)]
        self.got = [outer_shift(value, k + 1) for k, value in enumerate(self.parts)]
        self.token = self.parts[-1]
        self.mine = part(z)

    def seq_step(self, *tokens):
        got = lax.optimization_barrier(tuple(self.got) + tokens)[: len(self.got)]
        self.mine = sum((g.astype(f32) for g in got), self.mine.astype(f32)).astype(bf)
        self.token = self.mine
        self.got = lax.ppermute(self.mine, "seq", SEQ_SWAP)

    def core_step(self, *tokens):
        core = lax.axis_index("plots") % 2
        value = self.mine.astype(f32) + hold(self.got, *tokens).astype(f32)
        value = value.reshape((2, value.shape[0] // 2) + value.shape[1:])
        self.mine = lax.dynamic_index_in_dim(value, core, 0, keepdims=False)
        self.token = lax.dynamic_index_in_dim(value, 1 - core, 0, keepdims=False).astype(bf)
        self.got = core_swap(self.token)

    def done(self):
        core = lax.axis_index("plots") % 2
        other = self.got.astype(f32)
        return jnp.where(core == 0, self.mine, other), jnp.where(core == 0, other, self.mine)


class SeqFirstSum(Sum):
    def seq_first_step(self, *tokens):
        total, inner, outer, *_ = places()
        split = (outer * inner, 2, self.mine.shape[0] // (outer * inner * 2), self.mine.shape[1])
        got = lax.optimization_barrier(tuple(self.got) + tokens)[: len(self.got)]
        self.mine, self.token = combine(self.mine.reshape(split), got, lax.axis_index("seq"))
        self.got = lax.ppermute(self.token, "seq", SEQ_SWAP)

    def inner_step(self, *tokens):
        total, inner, outer, z, y, core = places()
        split = (outer, inner) + self.mine.shape[1:]
        mine, got = self.mine.reshape(split), hold(self.got, *tokens).reshape(split)

        def part(at):
            one = lax.dynamic_index_in_dim(mine, at, 1, keepdims=False)
            two = lax.dynamic_index_in_dim(got, at, 1, keepdims=False)
            return (one.astype(f32) + two.astype(f32)).astype(bf)

        if inner == 2:
            self.token = part(1 - y)
            self.got = lax.ppermute(self.token, "plots", [(i, i ^ 2) for i in range(total)])
            self.mine = part(y)
        else:
            groups = [[(o * inner + i) * 2 + c for i in range(inner)] for o in range(outer) for c in range(2)]
            self.token = (mine.astype(f32) + got.astype(f32)).astype(bf)
            self.mine = None
            self.got = lax.all_to_all(self.token, "plots", 1, 1, axis_index_groups=groups, tiled=True)

    def core_step(self, *tokens):
        core = lax.axis_index("plots") % 2
        got = hold(self.got, *tokens)
        own = lax.axis_index("seq") == core
        self.token = jnp.where(own, got, self.mine)
        self.mine = jnp.where(own, self.mine, got)
        self.got = core_swap(self.token)


def weight_rows(*weights):
    share = weights[0].shape[0] // lax.axis_size("plots")
    at = lax.axis_index("plots") * share
    return jnp.concatenate([lax.dynamic_slice_in_dim(w, at, share, 0) for w in weights], 1)


def finalize(sums, widths, rows, picks, gain):
    share, columns = sums.mine.shape
    pairs = len(widths)
    half = columns - sum(widths)

    def kernel(core_ref, mine_ref, other_ref, rows_ref, gain_ref, *refs):
        here = core_ref[0] == 0
        mine, other = mine_ref[...].astype(f32), other_ref[...].astype(f32)
        one, two = jnp.where(here, mine, other), jnp.where(here, other, mine)
        start = 0
        for j, wide in enumerate(widths):
            refs[2 * j][...] = one[:, start : start + wide]
            refs[2 * j + 1][...] = two[:, start : start + wide]
            start += wide
        refs[2 * pairs][:, :half] = one[:, start:]
        refs[2 * pairs][:, half:] = two[:, start:]
        total, start = 0.0, 0
        for j in picks:
            value = refs[j][...]
            product = value * rows_ref[:, start : start + value.shape[1]].astype(f32)
            high = product.astype(bf)
            ones = jnp.ones((8, value.shape[1]), bf)
            total = total + dot(ones, high, NT) + dot(ones, (product - high.astype(f32)).astype(bf), NT)
            start += value.shape[1]
        refs[-1][...] = total[0:1] / gain_ref[...]

    outs = [shape_of((share, wide), f32) for wide in widths for _ in range(2)]
    outs += [shape_of((share, 2 * half), f32), shape_of((1, share), f32)]
    args = [sums.mine, sums.got, rows, gain[None, :].astype(f32)]
    return call(kernel, args, outs, scalars=core_scalar(), name="finalize")


def combine_rows(keep, got, spot, low):
    outer, inner, rows, lanes = keep.shape

    def kernel(y_ref, keep_ref, got_ref, *refs):
        y = y_ref[0]
        for j, at in enumerate((slice(0, low), slice(low, rows))):
            one = keep_ref[0, 0, at, :].astype(f32) + got_ref[0, 0, at, :].astype(f32)
            two = keep_ref[0, 1, at, :].astype(f32) + got_ref[0, 1, at, :].astype(f32)
            refs[2 * j][0] = jnp.where(y == 0, one, two).astype(bf)
            refs[2 * j + 1][0] = jnp.where(y == 0, two, one).astype(bf)

    outs = [shape_of((outer, low, lanes))] * 2 + [shape_of((outer, rows - low, lanes))] * 2
    block = pl.BlockSpec((1, 2, rows, lanes), lambda i, s: (i, 0, 0, 0))
    out_specs = [pl.BlockSpec((1,) + o.shape[1:], lambda i, s: (i, 0, 0)) for o in outs]
    scalars = spot.astype(jnp.int32)[None]
    return call(kernel, [keep, got], outs, (outer,), [block] * 2, out_specs, scalars, name="combine_rows")


class FeedSum:
    def __init__(self, send, keep):
        self.token = send
        self.mine = keep
        self.got = core_swap(send)

    def first_step(self, *tokens):
        total, inner, outer, z, y, core = places()
        got = hold(self.got, *tokens)
        groups, rows, lanes = got.shape
        self.ring = inner == 2
        if self.ring:
            split = (outer, inner, rows, lanes)
            low = rows * 2 // 5 // 16 * 16
            self.a, self.token, self.b, self.last = combine_rows(self.mine.reshape(split), got.reshape(split), y, low)
            self.got = lax.ppermute(self.token, "plots", [(i, i ^ 2) for i in range(total)])
        else:
            value = (self.mine.astype(f32) + got.astype(f32)).astype(bf)
            pairs = [[2 * g + c for g in range(groups)] for c in range(2)]
            self.token = value
            self.got = lax.psum_scatter(value, "plots", scatter_dimension=0, axis_index_groups=pairs, tiled=True)

    def outer_parts(self, mine, got):
        total, inner, outer, z, y, core = places()

        def part(at):
            one = lax.dynamic_index_in_dim(mine, at, 0, keepdims=False)
            two = lax.dynamic_index_in_dim(got, at, 0, keepdims=False)
            return (one.astype(f32) + two.astype(f32)).astype(bf)

        parts = [part((z + k) % outer) for k in range(1, outer)]
        self.token = parts[-1]
        return [part(z)] + [outer_shift(value, k + 1) for k, value in enumerate(parts)]

    def second_step(self, *tokens):
        if self.ring:
            self.a = self.outer_parts(self.a, hold(self.got, *tokens))
            total = lax.axis_size("plots")
            self.got = lax.ppermute(hold(self.last, self.token), "plots", [(i, i ^ 2) for i in range(total)])

    def third_step(self, *tokens):
        if self.ring:
            parts = lax.optimization_barrier((*self.a, *tokens))[: len(self.a)]
            self.a = sum(p.astype(f32) for p in parts).astype(bf)
            self.b = self.outer_parts(self.b, hold(self.got, self.a))

    def seq_step(self, *tokens):
        if self.ring:
            parts = lax.optimization_barrier((*self.b, *tokens))[: len(self.b)]
            self.mine = jnp.concatenate([self.a, sum(p.astype(f32) for p in parts).astype(bf)], 0)
        else:
            self.mine = hold(self.got, *tokens)[0]
        self.token = self.mine
        self.got = lax.ppermute(self.mine, "seq", SEQ_SWAP)

    def core_step(self, share, blocks, *tokens):
        core = lax.axis_index("plots") % 2
        value = self.mine.astype(f32) + hold(self.got, *tokens).astype(f32)
        lanes = value.shape[1]
        gate = value[: blocks * share].reshape(blocks, 2, share // 2, lanes).transpose(1, 2, 0, 3)
        gate = gate.reshape(2, share // 2, blocks * lanes)
        down = value[blocks * share :].T.reshape(2, lanes // 2, value.shape[0] - blocks * share)

        def trade(a):
            mine = lax.dynamic_index_in_dim(a, core, 0, keepdims=False)
            got = core_swap(lax.dynamic_index_in_dim(a, 1 - core, 0, keepdims=False).astype(bf)).astype(f32)
            return jnp.where(core == 0, mine, got), jnp.where(core == 0, got, mine)

        gate, up = trade(gate)
        return gate, up, jnp.concatenate(trade(down), 1)


def per_device(
    decoder_states,
    encoder_patches,
    token_lengths,
    patch_counts,
    self_gain,
    cross_gain,
    mlp_gain,
    self_query,
    self_key,
    self_value,
    self_output,
    cross_query,
    cross_key,
    cross_value,
    cross_output,
    mlp_gate,
    mlp_up,
    mlp_down,
    output_grad,
):
    plots, rows, width = decoder_states.shape
    assert plots == 1 and width == 64 * HEADS
    patch_rows = encoder_patches.shape[1]
    place = lax.axis_index("seq")
    token = jnp.arange(rows, dtype=jnp.int32)
    slot = jnp.arange(patch_rows, dtype=jnp.int32)

    def length_bias(valid):
        return jnp.broadcast_to(jnp.where(valid, 0.0, MASKED)[None, :], (8, valid.shape[0]))

    self_bias = length_bias(
        jnp.concatenate([(token < token_lengths[0]) & (place == 1), token + place * rows < token_lengths[0]])
    )
    cross_own = length_bias(slot + place * patch_rows < patch_counts[0])
    cross_far = length_bias(slot + (1 - place) * patch_rows < patch_counts[0])
    gain_one, gain_two, gain_three = (g.astype(f32)[None, :] for g in (self_gain, cross_gain, mlp_gain))
    scale = 0.125 * LOG2E

    x = decoder_states[0]
    patches = encoder_patches[0]
    dy = output_grad[0]
    far_x = lax.ppermute(x, "seq", [(0, 1)])
    self_rows = weight_rows(self_query, self_key, self_value)
    cross_rows = weight_rows(cross_query)
    feed_rows = weight_rows(mlp_gate, mlp_up)
    share = width // lax.axis_size("plots")
    spot = lax.axis_index("plots") * share
    self_part, cross_part, feed_part = (
        lax.dynamic_slice_in_dim(g, spot, share, 0) for g in (self_gain, cross_gain, mlp_gain)
    )
    x, self_bias, gain_two = lax.optimization_barrier((x, self_bias, gain_two))
    weights = [self_query, self_key, self_value, cross_key, cross_value]
    first, q1, k1, v1, k2, v2 = start(x, gain_one, patches, weights, scale)
    far_x = hold(far_x, k2)
    far_patches = lax.ppermute(hold(patches, k2), "seq", SEQ_SWAP)
    e1, f1, o1, y1, second, q2, far_first, far_k1, far_v1 = self_forward(
        q1, k1, v1, self_bias, far_x, gain_one, self_key, self_value, x, self_output, gain_two, cross_query, scale
    )
    e2, part2 = attend(q2, [k2], [v2], cross_own)
    far_patches = hold(far_patches, part2)
    part2, self_rows, cross_rows, feed_rows, cross_far, gain_three = lax.optimization_barrier(
        (part2, self_rows, cross_rows, feed_rows, cross_far, gain_three)
    )
    far_e2, f2, far_f2, o2, y2, third, hidden, dgu, far_k2, far_v2, send, keep = cross_forward(
        q2, far_patches, cross_key, cross_value, cross_far, part2, y1, cross_output, gain_three, mlp_gate, mlp_up,
        mlp_down, dy,
    )
    feed = FeedSum(send, keep)
    dgu = hold(dgu, feed.token)
    dy2, b2, do2 = feed_back(dgu, mlp_gate, mlp_up, y2, gain_three, dy, cross_output)
    feed.first_step(do2)
    do2 = hold(do2, feed.token)
    far_dq2, far_d2, far_patch_grad = cross_back_far(far_e2, do2, o2, far_f2, q2, far_k2, far_v2, cross_key, cross_value)
    feed.second_step(far_patch_grad)
    do2 = hold(do2, feed.token)
    near_patch_grad = lax.ppermute(far_patch_grad, "seq", SEQ_SWAP)
    d2, dy1, do1, *sends, keep = cross_back_own(
        e2, hold(do2, far_patch_grad), o2, f2, q2, k2, v2, far_dq2, gain_two, cross_query, y1, dy2, self_output, patches,
        far_patches, far_d2, second, b2, o1,
    )
    near_patch_grad = hold(near_patch_grad, dy1)
    cross = Sum(sends, keep)
    feed.third_step(dy1)
    layer_output = output(y2, hold(hidden, cross.token, feed.token), mlp_down)
    cross.inner_step(layer_output, near_patch_grad)
    do1 = hold(do1, cross.token)
    d1, *sends, keep, far_first_grad = self_back(
        e1, do1, o1, f1, q1, [far_k1, k1], [far_v1, v1], far_first, first, self_key, self_value
    )
    own = SeqFirstSum(sends, keep)
    feed.seq_step(own.token)
    own.seq_first_step(feed.token)
    feed.got = hold(feed.got, own.token)
    cross.outer_step(own.token, feed.got)
    patch_grad = key_value_back(hold(d2, cross.token), cross_key, cross_value, near_patch_grad)
    own.inner_step(patch_grad)
    near_first_grad = lax.ppermute(hold(far_first_grad, own.token), "seq", [(1, 0)])
    cross.seq_step(own.token)
    own.outer_step(cross.token)
    near_first_grad = hold(near_first_grad, own.token)
    input_grad = finish(d1, self_query, self_key, self_value, near_first_grad, x, gain_one, dy1)
    own.seq_step(input_grad)
    cross.core_step(own.token)
    groups = lax.axis_size("plots") // 2
    gate_sum, up_sum, down_sum = feed.core_step(width // groups, groups, cross.token)
    cross_key_grad, cross_value_grad, cross_query_grad, cross_output_grad, self_output_grad, cross_gain_grad = finalize(
        cross, [width, width], cross_rows, [2], cross_part
    )
    own.core_step(cross_gain_grad)
    query_grad, key_grad, value_grad, self_gain_grad = finalize(own, [width], self_rows, [0, 1, 2], self_part)
    feed_gain_grad = jnp.sum(feed_rows.astype(f32) * jnp.concatenate([gate_sum, up_sum], 1), axis=1)
    return (
        layer_output[None],
        input_grad[None],
        patch_grad[None],
        self_gain_grad.reshape(-1),
        cross_gain_grad.reshape(-1),
        feed_gain_grad / feed_part.astype(f32),
        query_grad,
        key_grad,
        value_grad,
        self_output_grad,
        cross_query_grad,
        cross_key_grad,
        cross_value_grad,
        cross_output_grad,
        gate_sum,
        up_sum,
        down_sum,
    )


def solution(mesh):
    rows = P("plots", "seq", None)
    placed = (rows, rows, P("plots"), P("plots")) + (P(),) * 14 + (rows,)
    return jax.shard_map(
        per_device,
        mesh=mesh,
        in_specs=placed,
        out_specs=(rows, rows, rows) + (P("plots"),) * 3 + (P("plots", None),) * 11,
        check_vma=False,
    )
```

```python
import functools

import jax
import jax.numpy as jnp
from jax import lax
from jax.experimental import pallas as pl
from jax.experimental.pallas import tpu as pltpu
from jax.sharding import PartitionSpec as P

HEADS = 12
eps = 1e-06
bf = jnp.bfloat16
f32 = jnp.float32
LOG2E = 1.4426950408889634
LN2 = 0.6931471805599453
MASKED = -1e30
NN = (((1,), (0,)), ((), ()))
NT = (((1,), (1,)), ((), ()))
TN = (((0,), (0,)), ((), ()))
TT = (((0,), (1,)), ((), ()))
SEQ_SWAP = [(0, 1), (1, 0)]


def dot(left, right, dims=NN):
    return lax.dot_general(left, right, dims, preferred_element_type=f32)


def lane_of(shape):
    return lax.broadcasted_iota(jnp.int32, shape, len(shape) - 1)


def head_lanes(lane, half):
    return (lane < 64) if half == 0 else (lane >= 64)


def lane_rows(half):
    lane = lane_of((1, 128))
    inside = jnp.where(head_lanes(lane, half), 1.0, 0.0)
    return inside.astype(bf), jnp.where(lane == 64 - 64 * half, 1.0, 0.0).astype(bf)


ANY = pl.BlockSpec(memory_space=pl.ANY)


def shape_of(shape, dtype=bf):
    return jax.ShapeDtypeStruct(shape, dtype)


def call(kernel, args, outs, grid=(1,), in_specs=None, out_specs=None, scalars=None, scratch=(), flops=0, name=None):
    def whole(a):
        zeros = (0,) * len(a.shape)
        return pl.BlockSpec(a.shape, lambda *_: zeros, pipeline_mode=pl.Buffered(1))

    def specs(given, arrays):
        given = given or [None] * len(arrays)
        return [whole(a) if s is None else s for s, a in zip(given, arrays)]

    grid_spec = pltpu.PrefetchScalarGridSpec(
        num_scalar_prefetch=0 if scalars is None else 1,
        grid=grid,
        in_specs=specs(in_specs, args),
        out_specs=specs(out_specs, outs),
        scratch_shapes=scratch,
    )
    nbytes = sum(a.size * a.dtype.itemsize for a in args) + sum(a.size * a.dtype.itemsize for a in outs)
    if scalars is not None:
        args = [scalars] + list(args)
    return pl.pallas_call(
        kernel,
        grid_spec=grid_spec,
        out_shape=outs,
        compiler_params=pltpu.CompilerParams(vmem_limit_bytes=58 << 20),
        cost_estimate=pl.CostEstimate(flops=flops, bytes_accessed=nbytes, transcendentals=0),
        name=name,
    )(*args)


def attend_kernel(causal, merge, parts, block, q_ref, bias_ref, *refs):
    key_refs, value_refs = refs[:parts], refs[parts : 2 * parts]
    refs = refs[2 * parts :]
    if merge:
        before_ref, e_ref, o_ref, own_ref, new_ref = refs
    elif parts > 1:
        e_ref, o_ref, own_ref = refs
    else:
        e_ref, o_ref = refs
    rows = q_ref.shape[0]
    pairs = q_ref.shape[1] // 128
    lane_b = lane_of((block, 128))
    first = head_lanes(lane_b, 0)
    full = (block, 128)
    items = [(p, b, half) for p in range(pairs) for b in range(rows // block) for half in range(2)]
    kept = {}

    def reaches(b):
        offset, found = 0, []
        for i, k_ref in enumerate(key_refs):
            keys = k_ref.shape[0]
            seen = min(keys, (b + 1) * block) if causal and i == parts - 1 else keys
            found.append((offset, i, seen))
            offset += keys
        return found

    def scores(item):
        p, b, half = item
        lanes = slice(128 * p, 128 * p + 128)
        q = q_ref[b * block : (b + 1) * block, lanes] * lane_rows(half)[0]
        found = []
        for offset, i, seen in reaches(b):
            s = dot(q, key_refs[i][:seen, lanes], NT) + bias_ref[0:1, offset : offset + seen]
            if causal and i == parts - 1:
                row = lax.broadcasted_iota(jnp.int32, s.shape, 0) + b * block
                s = jnp.where(lane_of(s.shape) <= row, s, MASKED)
            found.append(s)
        return found

    def soften(item, found):
        p, b, half = item
        top = functools.reduce(jnp.maximum, [jnp.max(s, axis=1, keepdims=True) for s in found])
        es = []
        for (offset, i, seen), s in zip(reaches(b), found):
            e = jnp.exp2(s - top).astype(bf)
            e_ref[2 * p + half, b * block : (b + 1) * block, offset : offset + seen] = e
            es.append(e)
        return top, es

    def mix(item, top, es):
        p, b, half = item
        lanes = slice(128 * p, 128 * p + 128)
        at = slice(b * block, (b + 1) * block)
        inside, at0 = lane_rows(half)
        spare = 64 - 64 * half
        o = None
        for (offset, i, seen), e in zip(reaches(b), es):
            part = dot(e, value_refs[i][:seen, lanes] * inside + at0)
            o = part if o is None else o + part
        if not merge and parts == 1:
            o_ref[2 * p + half, at, :] = jnp.where(lane_b == spare + 1, top, o)
            return
        l_new = jnp.broadcast_to(o[:, spare : spare + 1], full)
        if merge:
            old = before_ref[2 * p + half, at, :]
            l_old = jnp.broadcast_to(old[:, spare : spare + 1], full)
            m_old = jnp.broadcast_to(old[:, spare + 1 : spare + 2], full)
            top = jnp.broadcast_to(top, full)
            m = jnp.maximum(m_old, top)
            w_old, w_new = jnp.exp2(m_old - m), jnp.exp2(top - m)
            turn = 1.0 / (l_old * w_old + l_new * w_new)
            f_old, f_new = w_old * turn, w_new * turn
            o = old * f_old + o * f_new
        else:
            f_old = f_new = 1.0 / l_new
            o = o * f_new
        if half == 0:
            kept[p, b] = (o, f_old, f_new)
        else:
            o0, old0, new0 = kept.pop((p, b))
            o_ref[at, lanes] = jnp.where(first, o0, o).astype(bf)
            own_ref[at, lanes] = jnp.where(first, old0, f_old)
            if merge:
                new_ref[at, lanes] = jnp.where(first, new0, f_new)

    s = scores(items[0])
    waiting = None
    for i, item in enumerate(items):
        following = scores(items[i + 1]) if i + 1 < len(items) else None
        if waiting is not None:
            mix(*waiting)
        top, es = soften(item, s)
        waiting = (item, top, es)
        s = following
    mix(*waiting)


def attend(q, keys, values, bias, causal=False, before=None, block=256, group=1):
    rows, width = q.shape
    pairs = width // 128
    merge = before is not None
    total = sum(k.shape[0] for k in keys)

    def column(a):
        return pl.BlockSpec((a.shape[0], 128 * group), lambda p: (0, p))

    tall = column(q)
    e_spec = pl.BlockSpec((2 * group, rows, total), lambda p: (p, 0, 0))
    o_spec = pl.BlockSpec((2 * group, rows, 128), lambda p: (p, 0, 0))
    outs, out_specs = [shape_of((2 * pairs, rows, total))], [e_spec]
    args = [q, bias, *keys, *values]
    in_specs = [tall, None] + [column(a) for a in args[2:]]
    if merge:
        args.append(before)
        in_specs.append(o_spec)
    if merge or len(keys) > 1:
        outs += [shape_of((rows, width))] + [shape_of((rows, width), f32)] * (2 if merge else 1)
        out_specs += [tall] * (3 if merge else 2)
    else:
        outs.append(shape_of((2 * pairs, rows, 128), f32))
        out_specs.append(o_spec)
    return call(
        functools.partial(attend_kernel, causal, merge, len(keys), block),
        args,
        outs,
        (pairs // group,),
        in_specs,
        out_specs,
        flops=16 * rows * total * width,
        name="attend",
    )


def attend_back_kernel(causal, last, parts, block, e_ref, do_ref, o_ref, f_ref, q_ref, *refs):
    key_refs, value_refs = refs[:parts], refs[parts : 2 * parts]
    refs = refs[2 * parts :]
    if last:
        before_ref, dq_ref, d_ref = refs
    elif len(refs) == 2:
        dq_ref, d_ref = refs
    else:
        dq_ref, d_ref = None, refs[0]
    base = d_ref.shape[0] - 2
    rows = q_ref.shape[0]
    pairs = q_ref.shape[1] // 128
    lane_b = lane_of((block, 128))
    items = [(p, half, b) for p in range(pairs) for half in range(2) for b in range(rows // block)]
    dq, dk, dv = {}, {}, {}

    def reaches(b):
        offset, found = 0, []
        for i, k_ref in enumerate(key_refs):
            keys = k_ref.shape[0]
            seen = min(keys, (b + 1) * block) if causal and i == parts - 1 else keys
            found.append((offset, i, seen))
            offset += keys
        return found

    def slopes(item):
        p, half, b = item
        lanes = slice(128 * p, 128 * p + 128)
        at = slice(b * block, (b + 1) * block)
        inb = head_lanes(lane_b, half)
        do = do_ref[at, lanes].astype(f32)
        f = f_ref[at, lanes]
        inner = jnp.sum(jnp.where(inb, do * o_ref[at, lanes].astype(f32), 0.0), axis=1, keepdims=True)
        off = inner * f[:, 64 * half : 64 * half + 1]
        dos = jnp.where(inb, do * f, 0.0).astype(bf)
        return dos, off, [dot(dos, value_refs[i][:seen, lanes], NT) for offset, i, seen in reaches(b)]

    def spread(item, dos, off, dps):
        p, half, b = item
        lanes = slice(128 * p, 128 * p + 128)
        at = slice(b * block, (b + 1) * block)
        q = q_ref[at, lanes]
        for (offset, i, seen), dp in zip(reaches(b), dps):
            e = e_ref[2 * p + half, at, offset : offset + seen]
            ds = (e.astype(f32) * (dp - off)).astype(bf)
            part = dot(ds, key_refs[i][:seen, lanes] * lane_rows(half)[0])
            dq[p, b] = part if (p, b) not in dq else dq[p, b] + part
            step = block if causal and i == parts - 1 else seen
            for c in range(0, seen, step):
                key = (p, half, offset + c)
                vt = dot(dos, e[:, c : c + step], TN)
                kt = dot(q, ds[:, c : c + step], TN)
                dv[key] = vt if key not in dv else dv[key] + vt
                dk[key] = kt if key not in dk else dk[key] + kt

    ready = slopes(items[0])
    for i, item in enumerate(items):
        following = slopes(items[i + 1]) if i + 1 < len(items) else None
        spread(item, *ready)
        ready = following
    for p, b in dq:
        lanes = slice(128 * p, 128 * p + 128)
        at = slice(b * block, (b + 1) * block)
        part = dq[p, b]
        if last:
            dq_ref[at, lanes] = ((part + before_ref[at, lanes]) * 0.125).astype(bf)
        elif base == 0:
            dq_ref[at, lanes] = part
        else:
            d_ref[0, lanes, d_ref.shape[2] - rows + b * block : d_ref.shape[2] - rows + (b + 1) * block] = (
                part.T * 0.125
            ).astype(bf)
    for p, half, c in dk:
        wide = dk[p, half, c].shape[1]
        inside = slice(64 * half, 64 * half + 64)
        at = slice(128 * p + 64 * half, 128 * p + 64 * half + 64)
        d_ref[base, at, c : c + wide] = (dk[p, half, c][inside] * LN2).astype(bf)
        d_ref[base + 1, at, c : c + wide] = dv[p, half, c][inside].astype(bf)


def attend_back(e, do, o, f, q, keys, values, causal=False, before=None, whole=False, block=256, group=1):
    rows, width = q.shape
    pairs = width // 128
    total = sum(k.shape[0] for k in keys)

    def column(a):
        return pl.BlockSpec((a.shape[0], 128 * group), lambda p: (0, p))

    tall = column(q)
    args = [e, do, o, f, q, *keys, *values]
    in_specs = [pl.BlockSpec((2 * group, rows, total), lambda p: (p, 0, 0))] + [column(a) for a in args[1:]]
    if before is not None:
        args.append(before)
        in_specs.append(tall)
    return call(
        functools.partial(attend_back_kernel, causal, before is not None, len(keys), block),
        args,
        ([] if whole else [shape_of((rows, width), f32 if before is None else bf)])
        + [shape_of((2 + whole, width, total))],
        (pairs // group,),
        in_specs,
        ([] if whole else [tall]) + [pl.BlockSpec((2 + whole, 128 * group, total), lambda p: (0, p, 0))],
        flops=16 * rows * total * width,
        name="attend_back",
    )


def late(refs, buffers, sems):
    copies = [pltpu.make_async_copy(ref, buffer, sems.at[i]) for i, (ref, buffer) in enumerate(zip(refs, buffers))]

    @pl.when(pl.program_id(0) == 0)
    def _():
        for copy in copies:
            copy.start()

    def fetch(i):
        copies[i].wait()
        return buffers[i]

    return fetch


def self_back(e, do, o, f, q, keys, values, far_first, first, wk, wv):
    rows, width = q.shape
    pairs = width // 128
    total = 2 * rows
    half = width // 2
    pieces = (width + half) // 128
    back = functools.partial(attend_back_kernel, True, False, 2, 256)

    def kernel(core_ref, *refs):
        blocks, (ff_ref, first_ref, wk_ref, wv_ref) = refs[:9], refs[9:13]
        d_ref, *send_refs, keep_ref, out_ref = refs[13 : 16 + pieces]
        all_ref, part_ref, *buffers, sems = refs[16 + pieces :]
        fetch = late([ff_ref, first_ref, wk_ref, wv_ref], buffers, sems)
        i = pl.program_id(0)
        core = core_ref[0]

        @pl.when(i < pairs)
        def _():
            back(*blocks, part_ref)
            d_ref[...] = part_ref[:, :, rows:]
            all_ref[:, pl.ds(pl.multiple_of(i * 128, 128), 128), :] = part_ref[...]

        @pl.when(i == pairs)
        def _():
            far, own = fetch(0)[...], fetch(1)[...]
            query = dot(own, all_ref[0, :, rows:], TT)
            key = dot(far, all_ref[1, :, :rows], TT) + dot(own, all_ref[1, :, rows:], TT)
            halves(send_refs, keep_ref, core, 0, query, key)

        @pl.when(i == pairs + 1)
        def _():
            far, own = buffers[0][...], buffers[1][...]
            value = dot(far, all_ref[2, :, :rows], TT) + dot(own, all_ref[2, :, rows:], TT)
            halves(send_refs, keep_ref, core, width, value[:, :half], value[:, half:])
            grad = dot(all_ref[1, :, :rows], fetch(2)[...], TT) + dot(all_ref[2, :, :rows], fetch(3)[...], TT)
            out_ref[...] = grad.astype(bf)

    def column(a):
        return pl.BlockSpec((a.shape[0], 128), lambda i, s: (0, jnp.minimum(i, pairs - 1)))

    args = [e, do, o, f, q, *keys, *values, far_first, first, wk, wv]
    in_specs = [pl.BlockSpec((2, rows, total), lambda i, s: (jnp.minimum(i, pairs - 1), 0, 0))]
    in_specs += [column(a) for a in args[1:9]] + [pl.BlockSpec(memory_space=pl.ANY)] * 4
    own = pl.BlockSpec((3, 128, rows), lambda i, s: (0, jnp.minimum(i, pairs - 1), 0))
    return call(
        kernel,
        args,
        [shape_of((3, width, rows))]
        + [shape_of((width, 128))] * pieces
        + [shape_of((width, width + half)), shape_of((rows, width))],
        (pairs + 2,),
        in_specs,
        [own] + [None] * (pieces + 2),
        core_scalar(),
        scratch=[pltpu.VMEM((3, width, total), bf), pltpu.VMEM((3, 128, total), bf)]
        + [pltpu.VMEM(a.shape, bf) for a in args[9:]]
        + [pltpu.SemaphoreType.DMA((4,))],
        flops=16 * rows * total * width + 12 * rows * width * width,
        name="self_back",
    )


def cross_back_far(e, do, o, f, q, k, v, wk, wv):
    rows, width = q.shape
    pairs = width // 128
    keys = k.shape[0]
    half = keys // 2

    def kernel(*refs):
        blocks, (wk_ref, wv_ref), (dq_ref, d_ref, out_ref) = refs[:7], refs[7:9], refs[9:12]
        all_ref, *buffers, sems = refs[12:]
        fetch = late([wk_ref, wv_ref], buffers, sems)
        i = pl.program_id(0)

        @pl.when(i < pairs)
        def _():
            attend_back_kernel(False, False, 1, 512, *blocks, dq_ref, d_ref)
            all_ref[:, pl.ds(pl.multiple_of(i * 128, 128), 128), :] = d_ref[...]

        @pl.when(i == pairs)
        def _():
            fetch(0), fetch(1)

        @pl.when(i >= pairs)
        def _():
            at = pl.ds(pl.multiple_of((i - pairs) * half, half), half)
            grad = dot(all_ref[0, :, at], buffers[0][...], TT) + dot(all_ref[1, :, at], buffers[1][...], TT)
            out_ref[...] = grad.astype(bf)

    def spot(i):
        return jnp.minimum(i, pairs - 1)

    def column(a):
        return pl.BlockSpec((a.shape[0], 128), lambda i: (0, spot(i)))

    args = [e, do, o, f, q, k, v, wk, wv]
    return call(
        kernel,
        args,
        [shape_of((rows, width), f32), shape_of((2, width, keys)), shape_of((keys, width))],
        (pairs + 2,),
        [pl.BlockSpec((2, rows, keys), lambda i: (spot(i), 0, 0))] + [column(a) for a in args[1:7]] + [ANY] * 2,
        [column(q), pl.BlockSpec((2, 128, keys), lambda i: (0, spot(i), 0))]
        + [pl.BlockSpec((half, width), lambda i: (jnp.maximum(i - pairs, 0), 0))],
        scratch=[pltpu.VMEM((2, width, keys), bf)] + [pltpu.VMEM(wk.shape, bf)] * 2 + [pltpu.SemaphoreType.DMA((2,))],
        flops=16 * rows * keys * width + 4 * keys * width * width,
        name="cross_back_far",
    )


def cross_back_own(e, do, o, f, q, k, v, before, gain, wq, y1, dy2, wo, patches, far_patches, far_d, second, b2, o1):
    rows, width = q.shape
    pairs = width // 128
    keys = k.shape[0]
    half = width // 2
    chunk = 512
    parts = keys // chunk

    def kernel(core_ref, *refs):
        blocks, gain_ref, late_refs = refs[:8], refs[8], refs[9:20]
        d_ref, *outs = refs[20:29]
        results, refs = refs[29:37], refs[37:]
        dy1_ref, do1_ref, *send_refs, keep_ref = results
        all_ref, dq_ref, acc_ref, b1_ref, *buffers, sems, out_sems = refs
        fetch = late(late_refs, buffers, sems)

        def store(j, at=(slice(None), slice(None)), k=None):
            return pltpu.make_async_copy(results[j].at[at], outs[j].at[at], out_sems.at[j if k is None else k])

        first, rest = (slice(None), slice(0, width)), (slice(None), slice(width, 2 * width + half))
        early = [store(j) for j in (0, 1, 4, 5, 6)] + [store(7, rest)]
        final = [store(2), store(3), store(7, first, 8)]
        i = pl.program_id(0)
        core = core_ref[0]

        @pl.when(i < pairs)
        def _():
            at = pl.ds(pl.multiple_of(i * 128, 128), 128)
            attend_back_kernel(False, True, 1, 256, *blocks, dq_ref.at[:, at], d_ref)
            all_ref[:, at, :] = d_ref[...]

        @pl.when(i == pairs)
        def _():
            for j in range(11):
                fetch(j)
            grad = dot(dq_ref[...], buffers[0][...], NT)
            unit, scale = norm_parts(buffers[1][...])
            dy1 = buffers[2][...] + norm_back(unit, scale, gain_ref[...], grad)
            dy1_ref[...] = dy1
            b1_ref[...] = dy1.astype(bf)
            do1_ref[...] = dot(b1_ref[...], buffers[3][...], NT).astype(bf)
            acc_ref[...] = jnp.zeros_like(acc_ref)
            query, output = dot(buffers[7][...], dq_ref[...], TN), dot(buffers[10][...], buffers[8][...], TN)
            halves(send_refs, keep_ref, core, width, query, output)
            value = dot(buffers[9][...], b1_ref[...], TN)
            halves(send_refs, keep_ref, core, 2 * width, value[:, :half], value[:, half:])
            for copy in early:
                copy.start()

        @pl.when((i > pairs) & (i <= pairs + parts))
        def _():
            at = pl.ds(pl.multiple_of((i - pairs - 1) * chunk, chunk), chunk)

            @pl.loop(0, 2)
            def _(j):
                left, far = buffers[4][at, :], buffers[5][at, :]
                acc_ref[j] += dot(left, all_ref[j, :, at], TT) + dot(far, buffers[6][j, :, at], TT)

        @pl.when(i == pairs + parts + 1)
        def _():
            halves(send_refs, keep_ref, core, 0, acc_ref[0], acc_ref[1])
            for copy in final:
                copy.start()
            for copy in early + final:
                copy.wait()

    def spot(i):
        return jnp.minimum(i, pairs - 1)

    def column(a):
        return pl.BlockSpec((a.shape[0], 128), lambda i, s: (0, spot(i)))

    lates = [wq, y1, dy2, wo, patches, far_patches, far_d, second, b2, o1, o]
    args = [e, do, o, f, q, k, v, before, gain] + lates
    full = shape_of((rows, width), f32)
    outs = [full, shape_of((rows, width))] + [shape_of((width, half))] * 5 + [shape_of((width, 2 * width + half))]
    return call(
        kernel,
        args,
        [shape_of((2, width, keys))] + outs,
        (pairs + parts + 2,),
        [pl.BlockSpec((2, rows, keys), lambda i, s: (spot(i), 0, 0))]
        + [column(a) for a in args[1:8]]
        + [None]
        + [ANY] * 11,
        [pl.BlockSpec((2, 128, keys), lambda i, s: (0, spot(i), 0))] + [ANY] * 8,
        core_scalar(),
        scratch=[pltpu.VMEM(a.shape, a.dtype) for a in outs]
        + [
            pltpu.VMEM((2, width, keys), bf),
            pltpu.VMEM((rows, width), bf),
            pltpu.VMEM((2, width, width), f32),
            pltpu.VMEM((rows, width), bf),
        ]
        + [pltpu.VMEM(a.shape, a.dtype) for a in lates]
        + [pltpu.SemaphoreType.DMA((11,)), pltpu.SemaphoreType.DMA((9,))],
        flops=16 * rows * keys * width + 2 * width * width * (5 * rows + 4 * keys),
        name="cross_back_own",
    )


def rows_loop(out_ref, left_ref, w_ref, finish=lambda v: v):
    @pl.loop(0, left_ref.shape[0] // 256)
    def _(i):
        at = pl.ds(pl.multiple_of(i * 256, 256), 256)
        out_ref[at, :] = finish(dot(left_ref[at, :], w_ref[...])).astype(out_ref.dtype)


def norm_parts(value):
    scale = lax.rsqrt(jnp.mean(value * value, axis=-1, keepdims=True) + eps)
    return value * scale, scale


def norm_back(unit, scale, gain, grad):
    inner = gain * grad
    return scale * (inner - unit * jnp.mean(inner * unit, axis=-1, keepdims=True))


def gelu_parts(u):
    t = jnp.tanh(0.7978845608028654 * (u + 0.044715 * u * u * u))
    value = 0.5 * u * (1.0 + t)
    slope = 0.5 * (1.0 + t) + 0.5 * u * (1.0 - t * t) * (0.7978845608028654 * (1.0 + 3 * 0.044715 * u * u))
    return value, slope


def start(x, gain, patches, weights, scale):
    def kernel(gain_ref, x_ref, w0, w1, w2, p_ref, w3, w4, *refs):
        outs, refs = refs[:6], refs[6:]
        ins, results, in_sems, out_sems = refs[:7], refs[7:13], refs[13], refs[14]
        loads = [
            pltpu.make_async_copy(ref, buffer, in_sems.at[i])
            for i, (ref, buffer) in enumerate(zip((x_ref, w0, w1, w2, p_ref, w3, w4), ins))
        ]
        stores = [
            pltpu.make_async_copy(buffer, ref, out_sems.at[i]) for i, (buffer, ref) in enumerate(zip(results, outs))
        ]
        loads[0].start()
        loads[1].start()
        loads[0].wait()
        for load in loads[2:]:
            load.start()
        first = (norm_parts(ins[0][...].astype(f32))[0] * gain_ref[...]).astype(bf)
        results[0][...] = first
        stores[0].start()
        for j in range(3):
            loads[1 + j].wait()
            rows_loop(results[1 + j], results[0], ins[1 + j], (lambda v: v * scale) if j == 0 else (lambda v: v))
            stores[1 + j].start()
        loads[4].wait()
        for j in range(2):
            loads[5 + j].wait()
            rows_loop(results[4 + j], ins[4], ins[5 + j])
            stores[4 + j].start()
        for store in stores:
            store.wait()

    args = [gain, x, *weights[:3], patches, *weights[3:]]
    outs = [shape_of(x.shape)] * 4 + [shape_of(patches.shape)] * 2
    return call(
        kernel,
        args,
        outs,
        in_specs=[None] + [ANY] * 7,
        out_specs=[ANY] * 6,
        scratch=[pltpu.VMEM(a.shape, bf) for a in args[1:] + outs]
        + [pltpu.SemaphoreType.DMA((7,)), pltpu.SemaphoreType.DMA((6,))],
        flops=2 * 768 * (3 * x.size + 2 * patches.size),
        name="start",
    )


def self_forward(q, k, v, bias, far_x, gain, wk, wv, x, w_out, next_gain, w_query, scale):
    rows, width = q.shape
    pairs = width // 128
    total = 2 * rows

    def kernel(q_ref, k_ref, v_ref, bias_ref, fx_ref, gain_ref, wk_ref, wv_ref, ng_ref, x_ref, wo_ref, wq_ref, *refs):
        e_ref, f_ref, o_ref, y_ref, n_ref, q2_ref, *far_out = refs[:9]
        far_first, far_k, far_v, *buffers, sems, out_sems = refs[9:]
        fetch = late([x_ref, wo_ref, wq_ref], buffers, sems)
        stores = [
            pltpu.make_async_copy(buffer, ref, out_sems.at[j])
            for j, (buffer, ref) in enumerate(zip((far_first, far_k, far_v), far_out))
        ]
        i = pl.program_id(0)

        @pl.when(i == 0)
        def _():
            far_first[...] = (norm_parts(fx_ref[...].astype(f32))[0] * gain_ref[...]).astype(bf)
            rows_loop(far_k, far_first, wk_ref)
            rows_loop(far_v, far_first, wv_ref)
            for store in stores:
                store.start()

        @pl.when((i > 0) & (i <= pairs))
        def _():
            at = pl.ds(pl.multiple_of((i - 1) * 128, 128), 128)
            refs = far_k.at[:, at], k_ref, far_v.at[:, at], v_ref
            attend_kernel(True, False, 2, 256, q_ref, bias_ref, *refs, e_ref, o_ref.at[:, at], f_ref)

        @pl.when(i == pairs + 1)
        def _():
            y = fetch(0)[...].astype(f32) + dot(o_ref[...], fetch(1)[...])
            y_ref[...] = y
            n_ref[...] = (norm_parts(y)[0] * ng_ref[...]).astype(bf)
            q2_ref[...] = (dot(n_ref[...], fetch(2)[...]) * scale).astype(bf)
            for store in stores:
                store.wait()

    def spot(i):
        return jnp.clip(i - 1, 0, pairs - 1)

    column = pl.BlockSpec((rows, 128), lambda i: (0, spot(i)))
    args = [q, k, v, bias, far_x, gain, wk, wv, next_gain, x, w_out, w_query]
    flat = shape_of((rows, width))
    return call(
        kernel,
        args,
        [shape_of((2 * pairs, rows, total)), shape_of((rows, width), f32), flat, shape_of((rows, width), f32)]
        + [flat] * 5,
        (pairs + 2,),
        [column] * 3 + [None] * 6 + [ANY] * 3,
        [pl.BlockSpec((2, rows, total), lambda i: (spot(i), 0, 0)), column] + [None] * 4 + [ANY] * 3,
        scratch=[pltpu.VMEM((rows, width), bf)] * 3
        + [pltpu.VMEM(a.shape, bf) for a in args[9:]]
        + [pltpu.SemaphoreType.DMA((3,)), pltpu.SemaphoreType.DMA((3,))],
        flops=16 * rows * total * width + 8 * rows * width * width,
        name="self_forward",
    )


def cross_forward(q, patches, wk, wv, bias, before, y1, w_out, gain, w_gate, w_up, w_down, dy):
    total, inner, outer, *_ = places()
    groups = inner * outer
    rows, width = q.shape
    keys = patches.shape[0]
    pairs = width // 128
    hidden = w_gate.shape[1]
    share, lanes = width // groups, hidden // groups
    blocks, step = hidden // lanes, 512
    per, chunks = step // lanes, hidden // step
    half = width // 2
    grouped = lanes % 128 == 0 and share % 16 == 0

    def kernel(core_ref, q_ref, bias_ref, before_ref, gain_ref, p_ref, wk_ref, wv_ref, *refs):
        late_refs, refs = refs[:6], refs[6:]
        e_ref, own_ref, new_ref, o_ref, y2_ref, third_ref, h_ref, d_ref, *outs = refs[:12]
        k_ref, v_ref, send_ref, keep_ref, *buffers, sems, out_sems, grad_sems = refs[12:]
        fetch = late(late_refs, buffers, sems)
        stores = [
            pltpu.make_async_copy(buffer, ref, out_sems.at[j])
            for j, (buffer, ref) in enumerate(zip((k_ref, v_ref), outs))
        ]
        i = pl.program_id(0)
        here = core_ref[0] == 0

        def grad_stores(c):
            if grouped:
                rows = pl.ds(pl.multiple_of(c * per * share, per * share), per * share)
                regions = [(slice(None), rows), (pl.ds(c * per, per), slice(blocks * share, blocks * share + half))]
            else:
                regions = [(slice(None), pl.ds(pl.multiple_of(c * step, step), step))]
            return [
                pltpu.make_async_copy(buffer.at[at], ref.at[at], grad_sems.at[c, 2 * j + k])
                for j, (buffer, ref) in enumerate(zip((send_ref, keep_ref), outs[2:]))
                for k, at in enumerate(regions)
            ]

        @pl.when(i == 0)
        def _():
            rows_loop(k_ref, p_ref, wk_ref)
            rows_loop(v_ref, p_ref, wv_ref)
            stores[0].start()
            stores[1].start()

        @pl.when((i > 0) & (i <= pairs))
        def _():
            at = pl.ds(pl.multiple_of((i - 1) * 128, 128), 128)
            refs = k_ref.at[:, at], v_ref.at[:, at], before_ref, e_ref, o_ref.at[:, at], own_ref, new_ref
            attend_kernel(False, True, 1, rows, q_ref, bias_ref, *refs)

        @pl.when(i == pairs + 1)
        def _():
            y2 = fetch(0)[...] + dot(o_ref[...], fetch(1)[...])
            y2_ref[...] = y2
            third_ref[...] = (norm_parts(y2)[0] * gain_ref[...]).astype(bf)
            for j in range(2, 6):
                fetch(j)

        @pl.when(i > pairs)
        def _():
            c = i - pairs - 1
            at = pl.ds(pl.multiple_of(c * step, step), step)
            wg_ref, wu_ref, wd_ref, dy_ref = buffers[2:]
            low = rows // 2

            @pl.loop(0, 2)
            def _(r):
                part = pl.ds(pl.multiple_of(r * low, low), low)
                third = third_ref[part, :]
                gate = dot(third, wg_ref[:, at])
                up = dot(third, wu_ref[:, at])
                dhidden = dot(dy_ref[part, :], wd_ref[at, :], NT)
                act, slope = gelu_parts(gate)
                h_ref[part, :] = (act * up).astype(bf)
                d_ref[0, part, :] = (dhidden * up * slope).astype(bf)
                d_ref[1, part, :] = (dhidden * act).astype(bf)

            third = third_ref[...]
            gate, up = dot(third, d_ref[0], TN), dot(third, d_ref[1], TN)
            send, keep = jnp.where(here, up, gate).astype(bf), jnp.where(here, gate, up).astype(bf)
            for g in range(groups if grouped else 0):
                from_rows = slice(g * share, (g + 1) * share)
                for j in range(per):
                    to = pl.ds(pl.multiple_of((c * per + j) * share, share), share)
                    send_ref[g, to, :] = send[from_rows, j * lanes : (j + 1) * lanes]
                    keep_ref[g, to, :] = keep[from_rows, j * lanes : (j + 1) * lanes]
            if not grouped:
                send_ref[:width, at] = send
                keep_ref[:width, at] = keep
            down = dot(dy_ref[...], h_ref[...], TN)
            send, keep = jnp.where(here, down[half:], down[:half]), jnp.where(here, down[:half], down[half:])
            if not grouped:
                send_ref[width:, at] = send.astype(bf)
                keep_ref[width:, at] = keep.astype(bf)
            to = slice(blocks * share, blocks * share + half)
            for j in range(per if grouped else 0):
                send_ref[c * per + j, to, :] = send[:, j * lanes : (j + 1) * lanes].astype(bf)
                keep_ref[c * per + j, to, :] = keep[:, j * lanes : (j + 1) * lanes].astype(bf)
            for store in grad_stores(c):
                store.start()

        @pl.when(i == pairs + chunks)
        def _():
            for store in stores:
                store.wait()
            for c in range(chunks):
                for store in grad_stores(c):
                    store.wait()

    def spot(i):
        return jnp.clip(i - 1, 0, pairs - 1)

    def chunk(i):
        return jnp.clip(i - 1 - pairs, 0, chunks - 1)

    column = pl.BlockSpec((rows, 128), lambda i, s: (0, spot(i)))
    args = [q, bias, before, gain, patches, wk, wv, y1, w_out, w_gate, w_up, w_down, dy]
    flat, key, full = shape_of((rows, width)), shape_of((keys, width)), shape_of((rows, width), f32)
    grads = shape_of((groups, blocks * share + half, lanes) if grouped else (width + half, hidden))
    *outs, send, keep = call(
        kernel,
        args,
        [shape_of((2 * pairs, rows, keys)), full, full, flat, full, flat]
        + [shape_of((rows, hidden)), shape_of((2, rows, hidden)), key, key, grads, grads],
        (pairs + 1 + chunks,),
        [column, None, pl.BlockSpec((2, rows, 128), lambda i, s: (spot(i), 0, 0))] + [None] * 4 + [ANY] * 6,
        [pl.BlockSpec((2, rows, keys), lambda i, s: (spot(i), 0, 0)), column, column, None, None, None]
        + [pl.BlockSpec((rows, step), lambda i, s: (0, chunk(i)))]
        + [pl.BlockSpec((2, rows, step), lambda i, s: (0, 0, chunk(i)))]
        + [ANY] * 4,
        core_scalar(),
        scratch=[pltpu.VMEM(a.shape, bf) for a in (key, key, grads, grads)]
        + [pltpu.VMEM(a.shape, a.dtype) for a in args[7:]]
        + [pltpu.SemaphoreType.DMA((6,)), pltpu.SemaphoreType.DMA((2,)), pltpu.SemaphoreType.DMA((chunks, 4))],
        flops=16 * rows * keys * width + 4 * keys * width * width + 12 * rows * width * hidden,
        name="cross_forward",
    )

    def group(value):
        if grouped:
            return value
        gate = value[:width].reshape(groups, share, blocks, lanes).swapaxes(1, 2).reshape(groups, -1, lanes)
        return jnp.concatenate([gate, value[width:].reshape(half, groups, lanes).swapaxes(0, 1)], 1)

    return *outs, group(send), group(keep)


def feed_back(d, w_gate, w_up, y2, gain, dy, w_out):
    def kernel(d_ref, wg_ref, wu_ref, gain_ref, y2_ref, dy_ref, wo_ref, dy2_ref, b_ref, do_ref, acc_ref, *refs):
        *buffers, sems = refs
        fetch = late([y2_ref, dy_ref, wo_ref], buffers, sems)
        i = pl.program_id(0)
        part = dot(d_ref[0], wg_ref[...], NT) + dot(d_ref[1], wu_ref[...], NT)

        @pl.when(i == 0)
        def _():
            acc_ref[...] = part

        @pl.when(i > 0)
        def _():
            acc_ref[...] += part

        @pl.when(i == pl.num_programs(0) - 1)
        def _():
            grad = acc_ref[...]
            unit, scale = norm_parts(fetch(0)[...])
            dy2 = fetch(1)[...].astype(f32) + norm_back(unit, scale, gain_ref[...], grad)
            dy2_ref[...] = dy2
            b_ref[...] = dy2.astype(bf)
            do_ref[...] = dot(b_ref[...], fetch(2)[...], NT).astype(bf)

    rows, width = y2.shape
    hidden = w_gate.shape[1]
    column = pl.BlockSpec((width, 512), lambda i: (0, i))
    return call(
        kernel,
        [d, w_gate, w_up, gain, y2, dy, w_out],
        [shape_of(y2.shape, f32), shape_of(y2.shape), shape_of(y2.shape)],
        (hidden // 512,),
        [pl.BlockSpec((2, rows, 512), lambda i: (0, 0, i)), column, column, None, ANY, ANY, ANY],
        scratch=[pltpu.VMEM((rows, width), f32)]
        + [pltpu.VMEM(a.shape, a.dtype) for a in (y2, dy, w_out)]
        + [pltpu.SemaphoreType.DMA((3,))],
        flops=2 * y2.size * (768 + 2 * hidden),
        name="feed_back",
    )


def finish(d, wq, wk, wv, near, x, gain, dy1):
    def kernel(d_ref, wq_ref, wk_ref, wv_ref, near_ref, x_ref, gain_ref, dy_ref, out_ref):
        grad = near_ref[...].astype(f32)
        for j, w_ref in enumerate((wq_ref, wk_ref, wv_ref)):
            grad = grad + dot(d_ref[j], w_ref[...], TT)
        unit, scale = norm_parts(x_ref[...].astype(f32))
        out_ref[...] = (dy_ref[...] + norm_back(unit, scale, gain_ref[...], grad)).astype(bf)

    rows = x.shape[0]
    return call(
        kernel, [d, wq, wk, wv, near, x, gain, dy1], [shape_of(x.shape)], (1,),
        flops=6 * x.size * 768, name="finish",
    )[0]


def output(y2, hidden, w_down):
    def kernel(y_ref, h_ref, w_ref, out_ref):
        out_ref[...] = (y_ref[...] + dot(h_ref[...], w_ref[...])).astype(bf)

    rows, width = y2.shape
    half = pl.BlockSpec((rows, width // 2), lambda i: (0, i))
    return call(
        kernel, [y2, hidden, w_down], [shape_of(y2.shape)], (2,),
        [half, None, pl.BlockSpec((hidden.shape[1], width // 2), lambda i: (0, i))], [half],
        flops=2 * hidden.size * width, name="output",
    )[0]


def key_value_back(d, wk, wv, near):
    keys = d.shape[2]
    half = keys // 2

    def kernel(d_ref, wk_ref, wv_ref, near_ref, out_ref):
        grad = dot(d_ref[0], wk_ref[...], TT) + dot(d_ref[1], wv_ref[...], TT)
        out_ref[...] = (grad + near_ref[...].astype(f32)).astype(bf)

    rows = pl.BlockSpec((half, wk.shape[0]), lambda i: (i, 0))
    part = pl.BlockSpec((2, d.shape[1], half), lambda i: (0, 0, i))
    return call(
        kernel, [d, wk, wv, near], [shape_of((keys, wk.shape[0]))], (2,), [part, None, None, rows], [rows],
        flops=4 * keys * 768 * 768, name="key_value_back",
    )[0]


def ring_factors(groups):
    inner = 1
    while inner * inner * 4 <= groups:
        inner *= 2
    return inner, groups // inner


def places():
    total = lax.axis_size("plots")
    index = lax.axis_index("plots")
    inner, outer = ring_factors(total // 2)
    group = index // 2
    return total, inner, outer, group // inner, group % inner, index % 2


def core_swap(value):
    total = lax.axis_size("plots")
    return lax.ppermute(value, "plots", [(i, i ^ 1) for i in range(total)])


def outer_shift(value, k):
    total, inner, outer, *_ = places()
    stride = 2 * inner
    return lax.ppermute(value, "plots", [(i, ((i // stride + k) % outer) * stride + i % stride) for i in range(total)])


def inner_shift(value, k):
    total, inner, outer, *_ = places()

    def spot(i):
        y = (i // 2) % inner
        return i + ((y + k) % inner - y) * 2

    return lax.ppermute(value, "plots", [(i, spot(i)) for i in range(total)])


def hold(value, *tokens):
    return lax.optimization_barrier((value,) + tokens)[0]


def halves(send_refs, keep_ref, core, start, one, two):
    here = core == 0
    send = jnp.where(here, two, one).astype(bf)
    keep_ref[:, start : start + one.shape[1]] = jnp.where(here, one, two).astype(bf)
    wide = send_refs[0].shape[1]
    for c in range(0, one.shape[1], wide):
        send_refs[(start + c) // wide][...] = send[:, c : c + wide]


def core_scalar():
    return (lax.axis_index("plots") % 2).astype(jnp.int32)[None]


def combine(keep, pieces, spot):
    outer, inner, share, columns = keep.shape

    def kernel(y_ref, keep_ref, *refs):
        *piece_refs, mine_ref, send_ref = refs
        y = y_ref[0]

        @pl.loop(0, outer // steps)
        def _(i):
            start = 0
            for ref in piece_refs:
                at = slice(start, start + ref.shape[3])
                start += ref.shape[3]
                one = keep_ref[i, 0, :, at].astype(f32) + ref[i, 0].astype(f32)
                two = keep_ref[i, 1, :, at].astype(f32) + ref[i, 1].astype(f32)
                mine_ref[i, :, at] = jnp.where(y == 0, one, two).astype(bf)
                send_ref[i, :, at] = jnp.where(y == 0, two, one).astype(bf)

    steps = 2

    def block(a):
        return pl.BlockSpec((outer // steps,) + a.shape[1:], lambda i, s: (i,) + (0,) * (len(a.shape) - 1))

    args = [keep] + [p.reshape(outer, inner, share, p.shape[1]) for p in pieces]
    out = shape_of((outer, share, columns))
    return call(
        kernel, args, [out, out], (steps,), [block(a) for a in args], [block(out)] * 2,
        spot.astype(jnp.int32)[None], name="combine",
    )


class Sum:
    def __init__(self, sends, keep):
        self.token = sends[-1]
        self.mine = keep
        self.got = [core_swap(send) for send in sends]

    def inner_step(self, *tokens):
        total, inner, outer, z, y, core = places()
        split = (outer, inner, self.mine.shape[0] // (outer * inner), self.mine.shape[1])
        mine = self.mine.reshape(split)
        got = lax.optimization_barrier(tuple(self.got) + tokens)[: len(self.got)]
        if inner == 2:
            self.mine, self.token = combine(mine, got, y)
            self.got = lax.ppermute(self.token, "plots", [(i, i ^ 2) for i in range(total)])
        else:
            got = jnp.concatenate(got, 1).reshape(split)
            groups = [[(o * inner + i) * 2 + c for i in range(inner)] for o in range(outer) for c in range(2)]
            self.token = (mine.astype(f32) + got.astype(f32)).astype(bf)
            self.mine = None
            self.got = lax.all_to_all(self.token, "plots", 1, 1, axis_index_groups=groups, tiled=True)

    def outer_step(self, *tokens):
        total, inner, outer, z, y, core = places()
        got = hold(self.got, *tokens)

        def part(at):
            if self.mine is None:
                value = lax.dynamic_index_in_dim(got, at, 0, keepdims=False)
                return jnp.sum(value.astype(f32), axis=0).astype(bf)
            one = lax.dynamic_index_in_dim(self.mine, at, 0, keepdims=False)
            two = lax.dynamic_index_in_dim(got, at, 0, keepdims=False)
            return (one.astype(f32) + two.astype(f32)).astype(bf)

        self.parts = [part((z + k) % outer) for k in range(1, outer)]
        self.got = [outer_shift(value, k + 1) for k, value in enumerate(self.parts)]
        self.token = self.parts[-1]
        self.mine = part(z)

    def seq_step(self, *tokens):
        got = lax.optimization_barrier(tuple(self.got) + tokens)[: len(self.got)]
        self.mine = sum((g.astype(f32) for g in got), self.mine.astype(f32)).astype(bf)
        self.token = self.mine
        self.got = lax.ppermute(self.mine, "seq", SEQ_SWAP)

    def core_step(self, *tokens):
        core = lax.axis_index("plots") % 2
        value = self.mine.astype(f32) + hold(self.got, *tokens).astype(f32)
        value = value.reshape((2, value.shape[0] // 2) + value.shape[1:])
        self.mine = lax.dynamic_index_in_dim(value, core, 0, keepdims=False)
        self.token = lax.dynamic_index_in_dim(value, 1 - core, 0, keepdims=False).astype(bf)
        self.got = core_swap(self.token)

    def done(self):
        core = lax.axis_index("plots") % 2
        other = self.got.astype(f32)
        return jnp.where(core == 0, self.mine, other), jnp.where(core == 0, other, self.mine)


class SeqFirstSum(Sum):
    def seq_first_step(self, *tokens):
        total, inner, outer, *_ = places()
        split = (outer * inner, 2, self.mine.shape[0] // (outer * inner * 2), self.mine.shape[1])
        got = lax.optimization_barrier(tuple(self.got) + tokens)[: len(self.got)]
        self.mine, self.token = combine(self.mine.reshape(split), got, lax.axis_index("seq"))
        self.got = lax.ppermute(self.token, "seq", SEQ_SWAP)

    def inner_step(self, *tokens):
        total, inner, outer, z, y, core = places()
        split = (outer, inner) + self.mine.shape[1:]
        mine, got = self.mine.reshape(split), hold(self.got, *tokens).reshape(split)

        def part(at):
            one = lax.dynamic_index_in_dim(mine, at, 1, keepdims=False)
            two = lax.dynamic_index_in_dim(got, at, 1, keepdims=False)
            return (one.astype(f32) + two.astype(f32)).astype(bf)

        if inner == 2:
            self.token = part(1 - y)
            self.got = lax.ppermute(self.token, "plots", [(i, i ^ 2) for i in range(total)])
            self.mine = part(y)
        else:
            groups = [[(o * inner + i) * 2 + c for i in range(inner)] for o in range(outer) for c in range(2)]
            self.token = (mine.astype(f32) + got.astype(f32)).astype(bf)
            self.mine = None
            self.got = lax.all_to_all(self.token, "plots", 1, 1, axis_index_groups=groups, tiled=True)

    def core_step(self, *tokens):
        core = lax.axis_index("plots") % 2
        got = hold(self.got, *tokens)
        own = lax.axis_index("seq") == core
        self.token = jnp.where(own, got, self.mine)
        self.mine = jnp.where(own, self.mine, got)
        self.got = core_swap(self.token)


def weight_rows(*weights):
    share = weights[0].shape[0] // lax.axis_size("plots")
    at = lax.axis_index("plots") * share
    return jnp.concatenate([lax.dynamic_slice_in_dim(w, at, share, 0) for w in weights], 1)


def finalize(sums, widths, rows, picks, gain):
    share, columns = sums.mine.shape
    pairs = len(widths)
    half = columns - sum(widths)

    def kernel(core_ref, mine_ref, other_ref, rows_ref, gain_ref, *refs):
        here = core_ref[0] == 0
        mine, other = mine_ref[...].astype(f32), other_ref[...].astype(f32)
        one, two = jnp.where(here, mine, other), jnp.where(here, other, mine)
        start = 0
        for j, wide in enumerate(widths):
            refs[2 * j][...] = one[:, start : start + wide]
            refs[2 * j + 1][...] = two[:, start : start + wide]
            start += wide
        refs[2 * pairs][:, :half] = one[:, start:]
        refs[2 * pairs][:, half:] = two[:, start:]
        total, start = 0.0, 0
        for j in picks:
            value = refs[j][...]
            product = value * rows_ref[:, start : start + value.shape[1]].astype(f32)
            high = product.astype(bf)
            ones = jnp.ones((8, value.shape[1]), bf)
            total = total + dot(ones, high, NT) + dot(ones, (product - high.astype(f32)).astype(bf), NT)
            start += value.shape[1]
        refs[-1][...] = total[0:1] / gain_ref[...]

    outs = [shape_of((share, wide), f32) for wide in widths for _ in range(2)]
    outs += [shape_of((share, 2 * half), f32), shape_of((1, share), f32)]
    args = [sums.mine, sums.got, rows, gain[None, :].astype(f32)]
    return call(kernel, args, outs, scalars=core_scalar(), name="finalize")


def combine_rows(keep, got, spot, low):
    outer, inner, rows, lanes = keep.shape

    def kernel(y_ref, keep_ref, got_ref, *refs):
        y = y_ref[0]
        for j, at in enumerate((slice(0, low), slice(low, rows))):
            one = keep_ref[0, 0, at, :].astype(f32) + got_ref[0, 0, at, :].astype(f32)
            two = keep_ref[0, 1, at, :].astype(f32) + got_ref[0, 1, at, :].astype(f32)
            refs[2 * j][0] = jnp.where(y == 0, one, two).astype(bf)
            refs[2 * j + 1][0] = jnp.where(y == 0, two, one).astype(bf)

    outs = [shape_of((outer, low, lanes))] * 2 + [shape_of((outer, rows - low, lanes))] * 2
    block = pl.BlockSpec((1, 2, rows, lanes), lambda i, s: (i, 0, 0, 0))
    out_specs = [pl.BlockSpec((1,) + o.shape[1:], lambda i, s: (i, 0, 0)) for o in outs]
    scalars = spot.astype(jnp.int32)[None]
    return call(kernel, [keep, got], outs, (outer,), [block] * 2, out_specs, scalars, name="combine_rows")


class FeedSum:
    def __init__(self, send, keep):
        self.token = send
        self.mine = keep
        self.got = core_swap(send)

    def first_step(self, *tokens):
        total, inner, outer, z, y, core = places()
        got = hold(self.got, *tokens)
        groups, rows, lanes = got.shape
        self.ring = inner == 2
        if self.ring:
            split = (outer, inner, rows, lanes)
            low = rows * 2 // 5 // 16 * 16
            self.a, self.token, self.b, self.last = combine_rows(self.mine.reshape(split), got.reshape(split), y, low)
            self.got = lax.ppermute(self.token, "plots", [(i, i ^ 2) for i in range(total)])
        else:
            value = (self.mine.astype(f32) + got.astype(f32)).astype(bf)
            pairs = [[2 * g + c for g in range(groups)] for c in range(2)]
            self.token = value
            self.got = lax.psum_scatter(value, "plots", scatter_dimension=0, axis_index_groups=pairs, tiled=True)

    def outer_parts(self, mine, got):
        total, inner, outer, z, y, core = places()

        def part(at):
            one = lax.dynamic_index_in_dim(mine, at, 0, keepdims=False)
            two = lax.dynamic_index_in_dim(got, at, 0, keepdims=False)
            return (one.astype(f32) + two.astype(f32)).astype(bf)

        parts = [part((z + k) % outer) for k in range(1, outer)]
        self.token = parts[-1]
        return [part(z)] + [outer_shift(value, k + 1) for k, value in enumerate(parts)]

    def second_step(self, *tokens):
        if self.ring:
            self.a = self.outer_parts(self.a, hold(self.got, *tokens))
            total = lax.axis_size("plots")
            self.got = lax.ppermute(hold(self.last, self.token), "plots", [(i, i ^ 2) for i in range(total)])

    def third_step(self, *tokens):
        if self.ring:
            parts = lax.optimization_barrier((*self.a, *tokens))[: len(self.a)]
            self.a = sum(p.astype(f32) for p in parts).astype(bf)
            self.b = self.outer_parts(self.b, hold(self.got, self.a))

    def seq_step(self, *tokens):
        if self.ring:
            parts = lax.optimization_barrier((*self.b, *tokens))[: len(self.b)]
            self.mine = jnp.concatenate([self.a, sum(p.astype(f32) for p in parts).astype(bf)], 0)
        else:
            self.mine = hold(self.got, *tokens)[0]
        self.token = self.mine
        self.got = lax.ppermute(self.mine, "seq", SEQ_SWAP)

    def core_step(self, share, blocks, *tokens):
        core = lax.axis_index("plots") % 2
        value = self.mine.astype(f32) + hold(self.got, *tokens).astype(f32)
        lanes = value.shape[1]
        gate = value[: blocks * share].reshape(blocks, 2, share // 2, lanes).transpose(1, 2, 0, 3)
        gate = gate.reshape(2, share // 2, blocks * lanes)
        down = value[blocks * share :].T.reshape(2, lanes // 2, value.shape[0] - blocks * share)

        def trade(a):
            mine = lax.dynamic_index_in_dim(a, core, 0, keepdims=False)
            got = core_swap(lax.dynamic_index_in_dim(a, 1 - core, 0, keepdims=False).astype(bf)).astype(f32)
            return jnp.where(core == 0, mine, got), jnp.where(core == 0, got, mine)

        gate, up = trade(gate)
        return gate, up, jnp.concatenate(trade(down), 1)


def per_device(
    decoder_states,
    encoder_patches,
    token_lengths,
    patch_counts,
    self_gain,
    cross_gain,
    mlp_gain,
    self_query,
    self_key,
    self_value,
    self_output,
    cross_query,
    cross_key,
    cross_value,
    cross_output,
    mlp_gate,
    mlp_up,
    mlp_down,
    output_grad,
):
    plots, rows, width = decoder_states.shape
    assert plots == 1 and width == 64 * HEADS
    patch_rows = encoder_patches.shape[1]
    place = lax.axis_index("seq")
    token = jnp.arange(rows, dtype=jnp.int32)
    slot = jnp.arange(patch_rows, dtype=jnp.int32)

    def length_bias(valid):
        return jnp.broadcast_to(jnp.where(valid, 0.0, MASKED)[None, :], (8, valid.shape[0]))

    self_bias = length_bias(
        jnp.concatenate([(token < token_lengths[0]) & (place == 1), token + place * rows < token_lengths[0]])
    )
    cross_own = length_bias(slot + place * patch_rows < patch_counts[0])
    cross_far = length_bias(slot + (1 - place) * patch_rows < patch_counts[0])
    gain_one, gain_two, gain_three = (g.astype(f32)[None, :] for g in (self_gain, cross_gain, mlp_gain))
    scale = 0.125 * LOG2E

    x = decoder_states[0]
    patches = encoder_patches[0]
    dy = output_grad[0]
    far_x = lax.ppermute(x, "seq", [(0, 1)])
    self_rows = weight_rows(self_query, self_key, self_value)
    cross_rows = weight_rows(cross_query)
    feed_rows = weight_rows(mlp_gate, mlp_up)
    share = width // lax.axis_size("plots")
    spot = lax.axis_index("plots") * share
    self_part, cross_part, feed_part = (
        lax.dynamic_slice_in_dim(g, spot, share, 0) for g in (self_gain, cross_gain, mlp_gain)
    )
    x, self_bias, gain_two = lax.optimization_barrier((x, self_bias, gain_two))
    weights = [self_query, self_key, self_value, cross_key, cross_value]
    first, q1, k1, v1, k2, v2 = start(x, gain_one, patches, weights, scale)
    far_x = hold(far_x, k2)
    far_patches = lax.ppermute(hold(patches, k2), "seq", SEQ_SWAP)
    e1, f1, o1, y1, second, q2, far_first, far_k1, far_v1 = self_forward(
        q1, k1, v1, self_bias, far_x, gain_one, self_key, self_value, x, self_output, gain_two, cross_query, scale
    )
    e2, part2 = attend(q2, [k2], [v2], cross_own)
    far_patches = hold(far_patches, part2)
    part2, self_rows, cross_rows, feed_rows, cross_far, gain_three = lax.optimization_barrier(
        (part2, self_rows, cross_rows, feed_rows, cross_far, gain_three)
    )
    far_e2, f2, far_f2, o2, y2, third, hidden, dgu, far_k2, far_v2, send, keep = cross_forward(
        q2, far_patches, cross_key, cross_value, cross_far, part2, y1, cross_output, gain_three, mlp_gate, mlp_up,
        mlp_down, dy,
    )
    feed = FeedSum(send, keep)
    dgu = hold(dgu, feed.token)
    dy2, b2, do2 = feed_back(dgu, mlp_gate, mlp_up, y2, gain_three, dy, cross_output)
    feed.first_step(do2)
    do2 = hold(do2, feed.token)
    far_dq2, far_d2, far_patch_grad = cross_back_far(far_e2, do2, o2, far_f2, q2, far_k2, far_v2, cross_key, cross_value)
    feed.second_step(far_patch_grad)
    do2 = hold(do2, feed.token)
    near_patch_grad = lax.ppermute(far_patch_grad, "seq", SEQ_SWAP)
    d2, dy1, do1, *sends, keep = cross_back_own(
        e2, hold(do2, far_patch_grad), o2, f2, q2, k2, v2, far_dq2, gain_two, cross_query, y1, dy2, self_output, patches,
        far_patches, far_d2, second, b2, o1,
    )
    near_patch_grad = hold(near_patch_grad, dy1)
    cross = Sum(sends, keep)
    feed.third_step(dy1)
    layer_output = output(y2, hold(hidden, cross.token, feed.token), mlp_down)
    cross.inner_step(layer_output, near_patch_grad)
    do1 = hold(do1, cross.token)
    d1, *sends, keep, far_first_grad = self_back(
        e1, do1, o1, f1, q1, [far_k1, k1], [far_v1, v1], far_first, first, self_key, self_value
    )
    own = SeqFirstSum(sends, keep)
    feed.seq_step(own.token)
    own.seq_first_step(feed.token)
    feed.got = hold(feed.got, own.token)
    cross.outer_step(own.token, feed.got)
    patch_grad = key_value_back(hold(d2, cross.token), cross_key, cross_value, near_patch_grad)
    own.inner_step(patch_grad)
    near_first_grad = lax.ppermute(hold(far_first_grad, own.token), "seq", [(1, 0)])
    cross.seq_step(own.token)
    own.outer_step(cross.token)
    near_first_grad = hold(near_first_grad, own.token)
    input_grad = finish(d1, self_query, self_key, self_value, near_first_grad, x, gain_one, dy1)
    own.seq_step(input_grad)
    cross.core_step(own.token)
    groups = lax.axis_size("plots") // 2
    gate_sum, up_sum, down_sum = feed.core_step(width // groups, groups, cross.token)
    cross_key_grad, cross_value_grad, cross_query_grad, cross_output_grad, self_output_grad, cross_gain_grad = finalize(
        cross, [width, width], cross_rows, [2], cross_part
    )
    own.core_step(cross_gain_grad)
    query_grad, key_grad, value_grad, self_gain_grad = finalize(own, [width], self_rows, [0, 1, 2], self_part)
    feed_gain_grad = jnp.sum(feed_rows.astype(f32) * jnp.concatenate([gate_sum, up_sum], 1), axis=1)
    return (
        layer_output[None],
        input_grad[None],
        patch_grad[None],
        self_gain_grad.reshape(-1),
        cross_gain_grad.reshape(-1),
        feed_gain_grad / feed_part.astype(f32),
        query_grad,
        key_grad,
        value_grad,
        self_output_grad,
        cross_query_grad,
        cross_key_grad,
        cross_value_grad,
        cross_output_grad,
        gate_sum,
        up_sum,
        down_sum,
    )


def solution(mesh):
    rows = P("plots", "seq", None)
    placed = (rows, rows, P("plots"), P("plots")) + (P(),) * 14 + (rows,)
    return jax.shard_map(
        per_device,
        mesh=mesh,
        in_specs=placed,
        out_specs=(rows, rows, rows) + (P("plots"),) * 3 + (P("plots", None),) * 11,
        check_vma=False,
    )
```
